32 devices in a mesh: groups: 2 (over y), blk: 4 (over z), uly: 2 (over x), cfg: 2 (over core).
Axes of the slice: x: 2, y: 2, z: 4, core: 2. Of those that a mesh axis runs over, the one named last changes fastest.
Arguments:
- query_rows: bfloat16 [2, 1024, 1536], P('cfg', ('groups', 'blk', 'uly')), parts along dimension 1, may hold values from -6 to 6
- key_rows: bfloat16 [2, 1024, 1536], P('cfg', ('groups', 'blk', 'uly')), parts along dimension 1, may hold values from -6 to 6
- value_rows: bfloat16 [2, 1024, 1536], P('cfg', ('groups', 'blk', 'uly')), parts along dimension 1, may hold values from -6 to 6
Outputs:
- attended: bfloat16 [2, 1024, 1536], P('cfg', ('groups', 'blk', 'uly')), parts along dimension 1
The draws below stay inside these ranges and needn't reach their ends.
There are 2 independent parts, one for each index of `groups`. The reference program is written for one: setup_inputs(seed, part) draws one part's arguments, and reference() takes and returns one part's arrays. A program takes and returns all parts, laid end to end along the dimension named above; each array names one. Nothing has to cross between parts.
All inputs are finite; a program needn't handle non-finite values.
Results may differ from the reference program's by a relative error of at most 0.0045.
Values may be sent and summed in bfloat16 or wider, within the bound.
No kernel may reach another device: no remote copies, remote signals or barrier semaphores. Data moves between devices by JAX's collectives and lax.ppermute only.
A program may use at most 128 MiB of HBM per device.

```python
import math
import jax
import jax.numpy as jnp
from jax import lax

HEADS = 12
HD = 128
BRANCHES = 2
WIDTH = 1536
SEQ = 512


def joint_draw(key, which_one):
    shape = (BRANCHES, SEQ, WIDTH)
    own_key = jax.random.fold_in(key, 11 + which_one)
    base = jnp.clip(1.58 * jax.random.normal(own_key, shape, jnp.float32), -6.0, 6.0)
    return base.astype(jnp.bfloat16)


def draw_query_rows(key, part):
    return joint_draw(key, 0)


def draw_key_rows(key, part):
    return joint_draw(key, 1)


def shard_levels(rng, shape, split, low, top_value):
    loudness, own = 1.0, jax.random.fold_in(rng, 6)
    for axis_at, shards_of in split:
        heights = jnp.exp(jax.random.uniform(jax.random.fold_in(own, axis_at), (shards_of,), jnp.float32, low / len(split), top_value / len(split)))
        loudness = loudness * jnp.repeat(heights, shape[axis_at] // shards_of).reshape([-1 if axis == axis_at else 1 for axis in range(len(shape))])
    return loudness


def scatter_about(rng, shape, spread, most, shards=(), kind=jnp.bfloat16):
    loudness = shard_levels(rng, shape, shards, -0.22, 0.18) if shards else 1.0
    values = jax.random.normal(rng, shape, jnp.float32) * spread * loudness
    return jnp.minimum(jnp.maximum(values, -most), most).astype(kind)


def setup_inputs(seed: int = 0, part: int = 0) -> dict:
    arg_keys = jax.random.split(jax.random.key(seed), 4)
    part_splits = jax.random.split(jax.random.fold_in(arg_keys[3], part), 4)
    return {
        "query_rows": draw_query_rows(jax.random.fold_in(jax.random.fold_in(arg_keys[3], part), 71), part),
        "key_rows": draw_key_rows(jax.random.fold_in(jax.random.fold_in(arg_keys[3], part), 71), part),
        "value_rows": scatter_about(part_splits[2], (BRANCHES, SEQ, WIDTH), 1.0, 6.0, ((0, 2), (1, 8))),
    }


def one_head(triple):
    query_head, key_head, value_head = triple
    score_scale = 1.0 / math.sqrt(HD)
    scores = jnp.dot(query_head, key_head.T, preferred_element_type=jnp.float32) * score_scale
    row_max = lax.optimization_barrier(jnp.max(scores, axis=1, keepdims=True))
    weights = jnp.exp(scores - row_max)
    totals = lax.optimization_barrier(jnp.sum(weights, axis=1, keepdims=True))
    probabilities = weights.astype(jnp.bfloat16)
    mixed = jnp.dot(probabilities, value_head, preferred_element_type=jnp.float32)
    return (mixed / totals).astype(jnp.bfloat16)

def heads_first(array):
    return array.reshape(BRANCHES, SEQ, HEADS, HD).transpose(0, 2, 1, 3).reshape(BRANCHES * HEADS, SEQ, HD)

def reference(query_rows, key_rows, value_rows):
    result = lax.map(one_head, (heads_first(query_rows), heads_first(key_rows), heads_first(value_rows)))
    return result.reshape(BRANCHES, HEADS, SEQ, HD).transpose(0, 2, 1, 3).reshape(BRANCHES, SEQ, WIDTH)
```

```python
import functools
import math

import jax
import jax.numpy as jnp
from jax import lax
from jax.experimental import pallas as pl
from jax.experimental.pallas import tpu as pltpu
from jax.sharding import PartitionSpec as P

HD = 128
ANY = pl.BlockSpec(memory_space=pl.ANY)
VMEM = pl.BlockSpec(memory_space=pltpu.VMEM)


def attend(queries, key_part, value_part):
    query_mat = queries[0, :, 0]
    row_count, head_count, head_size = query_mat.shape
    score_scale = 1.0 / math.sqrt(head_size)
    start_state = (
        jnp.full((head_count, row_count), -1e30, jnp.float32),
        jnp.zeros((head_count, row_count), jnp.float32),
        jnp.zeros((row_count, head_count, head_size), jnp.float32),
    )

    def absorb(state, pieces):
        key_piece = pieces[0][0, :, 0]
        value_piece = pieces[1][0, :, 0]
        scores = (
            jnp.einsum("qhd,khd->hqk", query_mat, key_piece, preferred_element_type=jnp.float32)
            * score_scale
        )
        running, totals, accumulated = state
        new_max = jnp.maximum(running, jnp.max(scores, axis=2))
        weights = jnp.exp(scores - new_max[:, :, None])
        factor = jnp.exp(running - new_max)
        totals = totals * factor + jnp.sum(weights, axis=2)
        probabilities = weights.astype(jnp.bfloat16)
        contrib = jnp.einsum(
            "hqk,khd->qhd", probabilities, value_piece, preferred_element_type=jnp.float32
        )
        accumulated = accumulated * factor.T[:, :, None] + contrib
        return (new_max, totals, accumulated)

    whole_keys, whole_values = (
        lax.all_gather(key_part, "blk", axis=1, tiled=True),
        lax.all_gather(value_part, "blk", axis=1, tiled=True),
    )
    key_count = whole_keys.shape[1]
    block_rows = math.gcd(key_count, 1024)

    def one_block(state, counter):
        offset = counter * block_rows
        key_block = lax.dynamic_slice_in_dim(whole_keys, offset, block_rows, 1)
        value_block = lax.dynamic_slice_in_dim(whole_values, offset, block_rows, 1)
        return (absorb(state, (key_block, value_block)), None)

    result, unused = lax.scan(
        one_block, start_state, jnp.arange(key_count // block_rows, dtype=jnp.int32)
    )
    output = (result[2] / result[1].T[:, :, None]).astype(jnp.bfloat16)
    return output.reshape(1, row_count, 1, head_count, head_size)


def local_generic(query_rows, key_rows, value_rows):
    ulysses = lax.axis_size("uly")
    tokens = query_rows.shape[1]
    width = query_rows.shape[2]
    heads_local = width // HD // ulysses

    def split_heads(array):
        array = array.reshape(1, tokens, ulysses, heads_local, HD)
        return lax.all_to_all(array, "uly", split_axis=2, concat_axis=1, tiled=True)

    mixed = attend(split_heads(query_rows), split_heads(key_rows), split_heads(value_rows))
    merged = lax.all_to_all(mixed, "uly", split_axis=1, concat_axis=2, tiled=True)
    return merged.reshape(1, tokens, width)


def pack_kernel(blocks, part, q_ref, k_ref, v_ref, *refs):
    outs, sems = refs[:-1], refs[-1]
    me = lax.axis_index("blk")
    copies = []
    for s in range(blocks):
        columns = pl.ds(pl.multiple_of((me ^ s) * part, 128), part)
        kv_out, q_out = outs[2 * s], outs[2 * s + 1]
        copies.append((k_ref.at[0, :, columns], kv_out.at[0]))
        copies.append((v_ref.at[0, :, columns], kv_out.at[1]))
        copies.append((q_ref.at[0, :, columns], q_out))
    started = [
        pltpu.make_async_copy(src, dst, sems.at[at]) for at, (src, dst) in enumerate(copies)
    ]
    for copy in started:
        copy.start()
    for copy in started:
        copy.wait()


def attend_kernel(blocks, columns_of, *refs):
    q_refs = refs[:blocks]
    kv_refs = refs[blocks : blocks + blocks * columns_of]
    out_refs = refs[blocks + blocks * columns_of :]
    tokens, part = q_refs[0].shape
    scale = 1.0 / math.sqrt(HD)
    for head in range(part // HD):
        lanes = slice(head * HD, (head + 1) * HD)
        queries = jnp.concatenate([ref[:, lanes] for ref in q_refs], axis=0)
        keys = jnp.concatenate([ref[0, :, lanes] for ref in kv_refs], axis=0)
        values = jnp.concatenate([ref[1, :, lanes] for ref in kv_refs], axis=0)
        scores = (
            lax.dot_general(
                queries, keys, (((1,), (1,)), ((), ())), preferred_element_type=jnp.float32
            )
            * scale
        )
        weights = jnp.exp(scores - jnp.max(scores, axis=1, keepdims=True))
        totals = jnp.sum(weights, axis=1, keepdims=True)
        mixed = jnp.dot(
            weights.astype(jnp.bfloat16), values, preferred_element_type=jnp.float32
        )
        result = (mixed / totals).astype(jnp.bfloat16)
        for at, ref in enumerate(out_refs):
            ref[:, lanes] = result[at * tokens : (at + 1) * tokens]


def unpack_kernel(blocks, part, *refs):
    ins, out_ref, sems = refs[:blocks], refs[blocks], refs[-1]
    me = lax.axis_index("blk")
    started = []
    for s in range(blocks):
        columns = pl.ds(pl.multiple_of((me ^ s) * part, 128), part)
        started.append(pltpu.make_async_copy(ins[s], out_ref.at[0, :, columns], sems.at[s]))
    for copy in started:
        copy.start()
    for copy in started:
        copy.wait()


def local_blocks(query_rows, key_rows, value_rows):
    blocks, columns_of = lax.axis_size("blk"), lax.axis_size("uly")
    tokens, width = query_rows.shape[1:]
    part = width // blocks
    heads = part // HD
    kind = query_rows.dtype
    kv_shape = jax.ShapeDtypeStruct((2, tokens, part), kind)
    q_shape = jax.ShapeDtypeStruct((tokens, part), kind)

    packed = pl.pallas_call(
        functools.partial(pack_kernel, blocks, part),
        out_shape=[kv_shape, q_shape] * blocks,
        in_specs=[ANY] * 3,
        out_specs=[ANY] * (2 * blocks),
        scratch_shapes=[pltpu.SemaphoreType.DMA((3 * blocks,))],
        cost_estimate=pl.CostEstimate(flops=0, bytes_accessed=6 * tokens * width * 2, transcendentals=0),
        name="pack",
    )(query_rows, key_rows, value_rows)
    own_kv, own_q = packed[0::2], packed[1::2]

    def to_block(array, s):
        return lax.ppermute(array, "blk", [(i, i ^ s) for i in range(blocks)]) if s else array

    def to_column(array, t):
        return lax.ppermute(array, "uly", [(i, (i + t) % columns_of) for i in range(columns_of)])

    order = list(range(blocks))[::-1]
    kv = {s: to_block(own_kv[s], s) for s in order}
    queries = {s: to_block(own_q[s], s) for s in order}
    all_kv = [kv[s] for s in range(blocks)]
    for t in range(1, columns_of):
        all_kv += [to_column(kv[s], t) for s in range(blocks)]

    all_tokens = tokens * blocks * columns_of
    pairs = heads * tokens * blocks * all_tokens
    mixed = pl.pallas_call(
        functools.partial(attend_kernel, blocks, columns_of),
        out_shape=[q_shape] * blocks,
        in_specs=[VMEM] * (blocks + blocks * columns_of),
        out_specs=[VMEM] * blocks,
        compiler_params=pltpu.CompilerParams(vmem_limit_bytes=32 * 1024 * 1024),
        cost_estimate=pl.CostEstimate(
            flops=4 * HD * pairs,
            bytes_accessed=2 * part * (2 * all_tokens + 2 * tokens * blocks),
            transcendentals=pairs,
        ),
        name="attend",
    )(*[queries[s] for s in range(blocks)], *all_kv)

    back = [to_block(mixed[s], s) for s in range(blocks)]
    return pl.pallas_call(
        functools.partial(unpack_kernel, blocks, part),
        out_shape=jax.ShapeDtypeStruct((1, tokens, width), kind),
        in_specs=[ANY] * blocks,
        out_specs=ANY,
        scratch_shapes=[pltpu.SemaphoreType.DMA((blocks,))],
        cost_estimate=pl.CostEstimate(flops=0, bytes_accessed=2 * tokens * width * 2, transcendentals=0),
        name="unpack",
    )(*back)


def local(query_rows, key_rows, value_rows):
    blocks = lax.axis_size("blk")
    heads = query_rows.shape[2] // HD
    few = heads % blocks == 0 and blocks & (blocks - 1) == 0
    plan = local_blocks if few else local_generic
    return plan(query_rows, key_rows, value_rows)


def solution(mesh):
    in_specs = (
        P("cfg", ("groups", "blk", "uly"), None),
        P("cfg", ("groups", "blk", "uly"), None),
        P("cfg", ("groups", "blk", "uly"), None),
    )
    out_specs = P("cfg", ("groups", "blk", "uly"), None)
    return jax.shard_map(local, mesh=mesh, in_specs=in_specs, out_specs=out_specs, check_vma=False)
```

```python
import functools
import math

import jax
import jax.numpy as jnp
from jax import lax
from jax.experimental import pallas as pl
from jax.experimental.pallas import tpu as pltpu
from jax.sharding import PartitionSpec as P

HD = 128
ANY = pl.BlockSpec(memory_space=pl.ANY)
VMEM = pl.BlockSpec(memory_space=pltpu.VMEM)


def attend(queries, key_part, value_part):
    query_mat = queries[0, :, 0]
    row_count, head_count, head_size = query_mat.shape
    score_scale = 1.0 / math.sqrt(head_size)
    start_state = (
        jnp.full((head_count, row_count), -1e30, jnp.float32),
        jnp.zeros((head_count, row_count), jnp.float32),
        jnp.zeros((row_count, head_count, head_size), jnp.float32),
    )

    def absorb(state, pieces):
        key_piece = pieces[0][0, :, 0]
        value_piece = pieces[1][0, :, 0]
        scores = (
            jnp.einsum("qhd,khd->hqk", query_mat, key_piece, preferred_element_type=jnp.float32)
            * score_scale
        )
        running, totals, accumulated = state
        new_max = jnp.maximum(running, jnp.max(scores, axis=2))
        weights = jnp.exp(scores - new_max[:, :, None])
        factor = jnp.exp(running - new_max)
        totals = totals * factor + jnp.sum(weights, axis=2)
        probabilities = weights.astype(jnp.bfloat16)
        contrib = jnp.einsum(
            "hqk,khd->qhd", probabilities, value_piece, preferred_element_type=jnp.float32
        )
        accumulated = accumulated * factor.T[:, :, None] + contrib
        return (new_max, totals, accumulated)

    whole_keys, whole_values = (
        lax.all_gather(key_part, "blk", axis=1, tiled=True),
        lax.all_gather(value_part, "blk", axis=1, tiled=True),
    )
    key_count = whole_keys.shape[1]
    block_rows = math.gcd(key_count, 1024)

    def one_block(state, counter):
        offset = counter * block_rows
        key_block = lax.dynamic_slice_in_dim(whole_keys, offset, block_rows, 1)
        value_block = lax.dynamic_slice_in_dim(whole_values, offset, block_rows, 1)
        return (absorb(state, (key_block, value_block)), None)

    result, unused = lax.scan(
        one_block, start_state, jnp.arange(key_count // block_rows, dtype=jnp.int32)
    )
    output = (result[2] / result[1].T[:, :, None]).astype(jnp.bfloat16)
    return output.reshape(1, row_count, 1, head_count, head_size)


def local_generic(query_rows, key_rows, value_rows):
    ulysses = lax.axis_size("uly")
    tokens = query_rows.shape[1]
    width = query_rows.shape[2]
    heads_local = width // HD // ulysses

    def split_heads(array):
        array = array.reshape(1, tokens, ulysses, heads_local, HD)
        return lax.all_to_all(array, "uly", split_axis=2, concat_axis=1, tiled=True)

    mixed = attend(split_heads(query_rows), split_heads(key_rows), split_heads(value_rows))
    merged = lax.all_to_all(mixed, "uly", split_axis=1, concat_axis=2, tiled=True)
    return merged.reshape(1, tokens, width)


def run_copies(pairs, sems):
    started = [pltpu.make_async_copy(src, dst, sems.at[at]) for at, (src, dst) in enumerate(pairs)]
    for copy in started:
        copy.start()
    for copy in started:
        copy.wait()


def pack_kernel(partners, part, with_query, q_ref, k_ref, v_ref, *refs):
    outs, sems = refs[:-1], refs[-1]
    me = lax.axis_index("blk")
    pairs = []
    for s, query, out in zip(partners, with_query, outs):
        columns = pl.ds(pl.multiple_of((me ^ s) * part, 128), part)
        sources = {"kv": (k_ref, v_ref), "kvq": (k_ref, v_ref, q_ref), "q": (q_ref,)}[query]
        for at, ref in enumerate(sources):
            pairs.append((ref.at[0, :, columns], out.at[at]))
    run_copies(pairs, sems)


def attend_kernel(query_places, key_places, *refs):
    query_count, key_count = len(query_places), len(key_places)
    q_refs = refs[:query_count]
    kv_refs = refs[query_count : query_count + key_count]
    out_refs = refs[query_count + key_count :]
    tokens, part = out_refs[0].shape
    scale = 1.0 / math.sqrt(HD)
    for head in range(part // HD):
        lanes = slice(head * HD, (head + 1) * HD)
        queries = jnp.concatenate(
            [ref[at, :, lanes] for ref, at in zip(q_refs, query_places)], axis=0
        )
        keys = jnp.concatenate([ref[0, :, lanes] for ref in kv_refs], axis=0)
        values = jnp.concatenate([ref[1, :, lanes] for ref in kv_refs], axis=0)
        scores = (
            lax.dot_general(
                queries, keys, (((1,), (1,)), ((), ())), preferred_element_type=jnp.float32
            )
            * scale
        )
        weights = jnp.exp(scores - jnp.max(scores, axis=1, keepdims=True))
        totals = jnp.sum(weights, axis=1, keepdims=True)
        mixed = jnp.dot(
            weights.astype(jnp.bfloat16), values, preferred_element_type=jnp.float32
        )
        result = (mixed / totals).astype(jnp.bfloat16)
        for at, ref in enumerate(out_refs):
            ref[:, lanes] = result[at * tokens : (at + 1) * tokens]


def unpack_kernel(blocks, part, *refs):
    ins, out_ref, sems = refs[:blocks], refs[blocks], refs[-1]
    me = lax.axis_index("blk")
    pairs = []
    for s in range(blocks):
        columns = pl.ds(pl.multiple_of((me ^ s) * part, 128), part)
        pairs.append((ins[s], out_ref.at[0, :, columns]))
    run_copies(pairs, sems)


def local_blocks(query_rows, key_rows, value_rows):
    blocks, columns_of = lax.axis_size("blk"), lax.axis_size("uly")
    tokens, width = query_rows.shape[1:]
    part = width // blocks
    heads = part // HD
    kind = query_rows.dtype
    far = list(range(2, blocks))

    partners = far + [1, 0] + far + [0]
    contents = ["kv"] * len(far) + ["kvq", "kv"] + ["q"] * len(far) + ["q"]
    deep = {"kv": 2, "kvq": 3, "q": 1}
    packed = pl.pallas_call(
        functools.partial(pack_kernel, partners, part, contents),
        out_shape=[jax.ShapeDtypeStruct((deep[c], tokens, part), kind) for c in contents],
        in_specs=[ANY] * 3,
        out_specs=[VMEM] * len(partners),
        scratch_shapes=[pltpu.SemaphoreType.DMA((3 * blocks,))],
        cost_estimate=pl.CostEstimate(flops=0, bytes_accessed=6 * tokens * width * 2, transcendentals=0),
        name="pack",
    )(query_rows, key_rows, value_rows)

    def to_block(array, s):
        return lax.ppermute(array, "blk", [(i, i ^ s) for i in range(blocks)])

    def to_column(array, t):
        return lax.ppermute(array, "uly", [(i, (i + t) % columns_of) for i in range(columns_of)])

    own = packed[len(far) + 1]
    kv = {s: to_block(packed[at], s) for at, s in enumerate(far)}
    kv[1] = to_block(packed[len(far)], 1)
    kv[0] = own
    far_q = {s: to_block(packed[len(far) + 2 + at], s) for at, s in enumerate(far)}
    all_kv = [kv[s] for s in range(blocks)]
    for t in range(1, columns_of):
        for s in range(blocks):
            all_kv.append(to_column(kv[s][:2] if s == 1 else kv[s], t))

    all_tokens = tokens * blocks * columns_of

    def attend_blocks(query_arrays, places):
        pairs = heads * tokens * len(places) * all_tokens
        return pl.pallas_call(
            functools.partial(attend_kernel, places, [0] * len(all_kv)),
            out_shape=[jax.ShapeDtypeStruct((tokens, part), kind)] * len(places),
            in_specs=[VMEM] * (len(places) + len(all_kv)),
            out_specs=[VMEM] * len(places),
            compiler_params=pltpu.CompilerParams(vmem_limit_bytes=32 * 1024 * 1024),
            cost_estimate=pl.CostEstimate(
                flops=4 * HD * pairs,
                bytes_accessed=2 * part * (2 * all_tokens + 2 * tokens * len(places)),
                transcendentals=pairs,
            ),
            name="attend",
        )(*query_arrays, *all_kv)

    mixed = dict(zip((0, 1), attend_blocks([packed[-1], kv[1]], [0, 2])))
    for s in far:
        mixed[s] = attend_blocks([far_q[s]], [0])[0]
    back = [mixed[0]] + [to_block(mixed[s], s) for s in range(1, blocks)]
    return pl.pallas_call(
        functools.partial(unpack_kernel, blocks, part),
        out_shape=jax.ShapeDtypeStruct((1, tokens, width), kind),
        in_specs=[VMEM] * blocks,
        out_specs=ANY,
        scratch_shapes=[pltpu.SemaphoreType.DMA((blocks,))],
        cost_estimate=pl.CostEstimate(flops=0, bytes_accessed=2 * tokens * width * 2, transcendentals=0),
        name="unpack",
    )(*back)


def local(query_rows, key_rows, value_rows):
    blocks = lax.axis_size("blk")
    heads = query_rows.shape[2] // HD
    few = blocks >= 2 and heads % blocks == 0 and blocks & (blocks - 1) == 0
    plan = local_blocks if few else local_generic
    return plan(query_rows, key_rows, value_rows)


def solution(mesh):
    in_specs = (
        P("cfg", ("groups", "blk", "uly"), None),
        P("cfg", ("groups", "blk", "uly"), None),
        P("cfg", ("groups", "blk", "uly"), None),
    )
    out_specs = P("cfg", ("groups", "blk", "uly"), None)
    return jax.shard_map(local, mesh=mesh, in_specs=in_specs, out_specs=out_specs, check_vma=False)
```

```python
import functools
import math

import jax
import jax.numpy as jnp
from jax import lax
from jax.experimental import pallas as pl
from jax.experimental.pallas import tpu as pltpu
from jax.sharding import PartitionSpec as P

HD = 128
HBM = pl.BlockSpec(memory_space=pltpu.HBM)
VMEM = pl.BlockSpec(memory_space=pltpu.VMEM)
SMALL = pltpu.CompilerParams(vmem_limit_bytes=4 * 1024 * 1024)


def attend(queries, key_part, value_part):
    query_mat = queries[0, :, 0]
    row_count, head_count, head_size = query_mat.shape
    score_scale = 1.0 / math.sqrt(head_size)
    start_state = (
        jnp.full((head_count, row_count), -1e30, jnp.float32),
        jnp.zeros((head_count, row_count), jnp.float32),
        jnp.zeros((row_count, head_count, head_size), jnp.float32),
    )

    def absorb(state, pieces):
        key_piece = pieces[0][0, :, 0]
        value_piece = pieces[1][0, :, 0]
        scores = (
            jnp.einsum("qhd,khd->hqk", query_mat, key_piece, preferred_element_type=jnp.float32)
            * score_scale
        )
        running, totals, accumulated = state
        new_max = jnp.maximum(running, jnp.max(scores, axis=2))
        weights = jnp.exp(scores - new_max[:, :, None])
        factor = jnp.exp(running - new_max)
        totals = totals * factor + jnp.sum(weights, axis=2)
        probabilities = weights.astype(jnp.bfloat16)
        contrib = jnp.einsum(
            "hqk,khd->qhd", probabilities, value_piece, preferred_element_type=jnp.float32
        )
        accumulated = accumulated * factor.T[:, :, None] + contrib
        return (new_max, totals, accumulated)

    whole_keys, whole_values = (
        lax.all_gather(key_part, "blk", axis=1, tiled=True),
        lax.all_gather(value_part, "blk", axis=1, tiled=True),
    )
    key_count = whole_keys.shape[1]
    block_rows = math.gcd(key_count, 1024)

    def one_block(state, counter):
        offset = counter * block_rows
        key_block = lax.dynamic_slice_in_dim(whole_keys, offset, block_rows, 1)
        value_block = lax.dynamic_slice_in_dim(whole_values, offset, block_rows, 1)
        return (absorb(state, (key_block, value_block)), None)

    result, unused = lax.scan(
        one_block, start_state, jnp.arange(key_count // block_rows, dtype=jnp.int32)
    )
    output = (result[2] / result[1].T[:, :, None]).astype(jnp.bfloat16)
    return output.reshape(1, row_count, 1, head_count, head_size)


def local_generic(query_rows, key_rows, value_rows):
    ulysses = lax.axis_size("uly")
    tokens = query_rows.shape[1]
    width = query_rows.shape[2]
    heads_local = width // HD // ulysses

    def split_heads(array):
        array = array.reshape(1, tokens, ulysses, heads_local, HD)
        return lax.all_to_all(array, "uly", split_axis=2, concat_axis=1, tiled=True)

    mixed = attend(split_heads(query_rows), split_heads(key_rows), split_heads(value_rows))
    merged = lax.all_to_all(mixed, "uly", split_axis=1, concat_axis=2, tiled=True)
    return merged.reshape(1, tokens, width)


def run_copies(pairs, sems):
    started = [pltpu.make_async_copy(src, dst, sems.at[at]) for at, (src, dst) in enumerate(pairs)]
    for copy in started:
        copy.start()
    for copy in started:
        copy.wait()


def pack_kernel(messages, part, q_ref, k_ref, v_ref, *refs):
    outs, sems = refs[:-1], refs[-1]
    sources = {"q": q_ref, "k": k_ref, "v": v_ref}
    me = lax.axis_index("blk")
    pairs = []
    for (s, names), out in zip(messages, outs):
        columns = pl.ds(pl.multiple_of((me ^ s) * part, 128), part)
        for at, name in enumerate(names):
            pairs.append((sources[name].at[0, :, columns], out.at[at]))
    run_copies(pairs, sems)


def join_kernel(places, *refs):
    for at, (source, place) in enumerate(places):
        refs[-1][at] = refs[source][place]


def join(arrays, places):
    shape = (len(places),) + arrays[0].shape[1:]
    size = math.prod(shape) * 2
    return pl.pallas_call(
        functools.partial(join_kernel, places),
        out_shape=jax.ShapeDtypeStruct(shape, arrays[0].dtype),
        in_specs=[VMEM] * len(arrays),
        out_specs=VMEM,
        compiler_params=SMALL,
        cost_estimate=pl.CostEstimate(flops=0, bytes_accessed=2 * size, transcendentals=0),
        name="join",
    )(*arrays)


def attend_kernel(query_places, key_places, value_places, *refs):
    blocks = len(query_places)
    ins, out_refs = refs[:-blocks], refs[-blocks:]
    tokens, part = out_refs[0].shape
    scale = 1.0 / math.sqrt(HD)
    for head in range(part // HD):
        lanes = slice(head * HD, (head + 1) * HD)
        queries, keys, values = (
            jnp.concatenate([ins[source][at, :, lanes] for source, at in places], axis=0)
            for places in (query_places, key_places, value_places)
        )
        scores = (
            lax.dot_general(
                queries, keys, (((1,), (1,)), ((), ())), preferred_element_type=jnp.float32
            )
            * scale
        )
        weights = jnp.exp(scores - jnp.max(scores, axis=1, keepdims=True))
        totals = jnp.sum(weights, axis=1, keepdims=True)
        mixed = jnp.dot(
            weights.astype(jnp.bfloat16), values, preferred_element_type=jnp.float32
        )
        result = (mixed / totals).astype(jnp.bfloat16)
        for at, ref in enumerate(out_refs):
            ref[:, lanes] = result[at * tokens : (at + 1) * tokens]


def unpack_kernel(blocks, part, *refs):
    ins, out_ref, sems = refs[:blocks], refs[blocks], refs[-1]
    me = lax.axis_index("blk")
    pairs = []
    for s in range(blocks):
        columns = pl.ds(pl.multiple_of((me ^ s) * part, 128), part)
        pairs.append((ins[s], out_ref.at[0, :, columns]))
    run_copies(pairs, sems)


def local_blocks(query_rows, key_rows, value_rows):
    blocks, columns_of = lax.axis_size("blk"), lax.axis_size("uly")
    tokens, width = query_rows.shape[1:]
    part = width // blocks
    heads = part // HD
    kind = query_rows.dtype
    far = list(range(2, blocks))

    messages = [(s, "k") for s in far] + [(1, "kvq")] + [(s, "vq") for s in far]
    messages += [(0, "kv"), (0, "q")]
    packed = pl.pallas_call(
        functools.partial(pack_kernel, messages, part),
        out_shape=[jax.ShapeDtypeStruct((len(m), tokens, part), kind) for s, m in messages],
        in_specs=[HBM] * 3,
        out_specs=[VMEM] * len(messages),
        scratch_shapes=[pltpu.SemaphoreType.DMA((3 * blocks,))],
        compiler_params=SMALL,
        cost_estimate=pl.CostEstimate(
            flops=0, bytes_accessed=6 * tokens * width * 2, transcendentals=0
        ),
        name="pack",
    )(query_rows, key_rows, value_rows)

    def to_block(array, s):
        return lax.ppermute(array, "blk", [(i, i ^ s) for i in range(blocks)])

    def to_column(array, t):
        return lax.ppermute(array, "uly", [(i, (i + t) % columns_of) for i in range(columns_of)])

    sent = {message: array for message, array in zip(messages, packed)}
    held = [sent[0, "kv"], sent[0, "q"]]
    held += [to_block(sent[m], m[0]) for m in messages[:-2]]
    at_near = 2 + len(far)
    at_keys = {s: 2 + at for at, s in enumerate(far)}
    at_values = {s: 3 + len(far) + at for at, s in enumerate(far)}
    query_places = [(1, 0), (at_near, 2)] + [(at_values[s], 1) for s in far]
    key_places = [(0, 0), (at_near, 0)] + [(at_keys[s], 0) for s in far]
    value_places = [(0, 1), (at_near, 1)] + [(at_values[s], 0) for s in far]
    near = join([held[0], held[at_near]], [(0, 0), (0, 1), (1, 0), (1, 1)])
    far_places = [(at, 0) for at in range(len(far))]
    far_keys = join([held[at_keys[s]] for s in far], far_places)
    far_values = join([held[at_values[s]] for s in far], far_places)
    for t in range(1, columns_of):
        base = len(held)
        held += [to_column(array, t) for array in (near, far_keys, far_values)]
        key_places += [(base, 0), (base, 2)] + [(base + 1, at) for at in range(len(far))]
        value_places += [(base, 1), (base, 3)] + [(base + 2, at) for at in range(len(far))]

    all_tokens = tokens * blocks * columns_of
    pairs = heads * tokens * blocks * all_tokens
    mixed = pl.pallas_call(
        functools.partial(attend_kernel, query_places, key_places, value_places),
        out_shape=[jax.ShapeDtypeStruct((tokens, part), kind)] * blocks,
        in_specs=[VMEM] * len(held),
        out_specs=[VMEM] * blocks,
        compiler_params=pltpu.CompilerParams(vmem_limit_bytes=24 * 1024 * 1024),
        cost_estimate=pl.CostEstimate(
            flops=4 * HD * pairs,
            bytes_accessed=2 * part * (2 * all_tokens + 2 * tokens * blocks),
            transcendentals=pairs,
        ),
        name="attend",
    )(*held)

    back = {s: to_block(mixed[s], s) for s in range(blocks - 1, 0, -1)}
    return pl.pallas_call(
        functools.partial(unpack_kernel, blocks, part),
        out_shape=jax.ShapeDtypeStruct((1, tokens, width), kind),
        in_specs=[VMEM] * blocks,
        out_specs=HBM,
        scratch_shapes=[pltpu.SemaphoreType.DMA((blocks,))],
        compiler_params=SMALL,
        cost_estimate=pl.CostEstimate(
            flops=0, bytes_accessed=2 * tokens * width * 2, transcendentals=0
        ),
        name="unpack",
    )(mixed[0], *[back[s] for s in range(1, blocks)])


def local(query_rows, key_rows, value_rows):
    blocks = lax.axis_size("blk")
    heads = query_rows.shape[2] // HD
    few = blocks >= 4 and heads % blocks == 0 and blocks & (blocks - 1) == 0
    plan = local_blocks if few else local_generic
    return plan(query_rows, key_rows, value_rows)


def solution(mesh):
    in_specs = (
        P("cfg", ("groups", "blk", "uly"), None),
        P("cfg", ("groups", "blk", "uly"), None),
        P("cfg", ("groups", "blk", "uly"), None),
    )
    out_specs = P("cfg", ("groups", "blk", "uly"), None)
    return jax.shard_map(local, mesh=mesh, in_specs=in_specs, out_specs=out_specs, check_vma=False)
```

```python
import functools
import math

import jax
import jax.numpy as jnp
from jax import lax
from jax.experimental import pallas as pl
from jax.experimental.pallas import tpu as pltpu
from jax.sharding import PartitionSpec as P

HD = 128
ANY = pl.BlockSpec(memory_space=pl.ANY)
HBM = pl.BlockSpec(memory_space=pltpu.HBM)
VMEM = pl.BlockSpec(memory_space=pltpu.VMEM)
SMALL = pltpu.CompilerParams(vmem_limit_bytes=4 * 1024 * 1024)


def attend(queries, key_part, value_part):
    query_mat = queries[0, :, 0]
    row_count, head_count, head_size = query_mat.shape
    score_scale = 1.0 / math.sqrt(head_size)
    start_state = (
        jnp.full((head_count, row_count), -1e30, jnp.float32),
        jnp.zeros((head_count, row_count), jnp.float32),
        jnp.zeros((row_count, head_count, head_size), jnp.float32),
    )

    def absorb(state, pieces):
        key_piece = pieces[0][0, :, 0]
        value_piece = pieces[1][0, :, 0]
        scores = (
            jnp.einsum("qhd,khd->hqk", query_mat, key_piece, preferred_element_type=jnp.float32)
            * score_scale
        )
        running, totals, accumulated = state
        new_max = jnp.maximum(running, jnp.max(scores, axis=2))
        weights = jnp.exp(scores - new_max[:, :, None])
        factor = jnp.exp(running - new_max)
        totals = totals * factor + jnp.sum(weights, axis=2)
        probabilities = weights.astype(jnp.bfloat16)
        contrib = jnp.einsum(
            "hqk,khd->qhd", probabilities, value_piece, preferred_element_type=jnp.float32
        )
        accumulated = accumulated * factor.T[:, :, None] + contrib
        return (new_max, totals, accumulated)

    whole_keys, whole_values = (
        lax.all_gather(key_part, "blk", axis=1, tiled=True),
        lax.all_gather(value_part, "blk", axis=1, tiled=True),
    )
    key_count = whole_keys.shape[1]
    block_rows = math.gcd(key_count, 1024)

    def one_block(state, counter):
        offset = counter * block_rows
        key_block = lax.dynamic_slice_in_dim(whole_keys, offset, block_rows, 1)
        value_block = lax.dynamic_slice_in_dim(whole_values, offset, block_rows, 1)
        return (absorb(state, (key_block, value_block)), None)

    result, unused = lax.scan(
        one_block, start_state, jnp.arange(key_count // block_rows, dtype=jnp.int32)
    )
    output = (result[2] / result[1].T[:, :, None]).astype(jnp.bfloat16)
    return output.reshape(1, row_count, 1, head_count, head_size)


def local_generic(query_rows, key_rows, value_rows):
    ulysses = lax.axis_size("uly")
    tokens = query_rows.shape[1]
    width = query_rows.shape[2]
    heads_local = width // HD // ulysses

    def split_heads(array):
        array = array.reshape(1, tokens, ulysses, heads_local, HD)
        return lax.all_to_all(array, "uly", split_axis=2, concat_axis=1, tiled=True)

    mixed = attend(split_heads(query_rows), split_heads(key_rows), split_heads(value_rows))
    merged = lax.all_to_all(mixed, "uly", split_axis=1, concat_axis=2, tiled=True)
    return merged.reshape(1, tokens, width)


def run_copies(pairs, sems):
    started = [pltpu.make_async_copy(src, dst, sems.at[at]) for at, (src, dst) in enumerate(pairs)]
    for copy in started:
        copy.start()
    for copy in started:
        copy.wait()


def pack_kernel(messages, part, q_ref, k_ref, v_ref, *refs):
    outs, sems = refs[:-1], refs[-1]
    sources = {"q": q_ref, "k": k_ref, "v": v_ref}
    me = lax.axis_index("blk")
    pairs = []
    for (s, names), out in zip(messages, outs):
        columns = pl.ds(pl.multiple_of((me ^ s) * part, 128), part)
        for at, name in enumerate(names):
            pairs.append((sources[name].at[0, :, columns], out.at[at]))
    run_copies(pairs, sems)


def join_kernel(places, *refs):
    for at, (source, place) in enumerate(places):
        refs[-1][at] = refs[source][place]


def join(arrays, places):
    shape = (len(places),) + arrays[0].shape[1:]
    size = math.prod(shape) * 2
    return pl.pallas_call(
        functools.partial(join_kernel, places),
        out_shape=jax.ShapeDtypeStruct(shape, arrays[0].dtype),
        in_specs=[VMEM] * len(arrays),
        out_specs=VMEM,
        compiler_params=SMALL,
        cost_estimate=pl.CostEstimate(flops=0, bytes_accessed=2 * size, transcendentals=0),
        name="join",
    )(*arrays)


def hold_kernel(array_ref, until_ref, out_ref):
    pass


def hold(array, until):
    return pl.pallas_call(
        hold_kernel,
        out_shape=jax.ShapeDtypeStruct(array.shape, array.dtype),
        in_specs=[ANY, ANY],
        out_specs=ANY,
        input_output_aliases={0: 0},
        compiler_params=SMALL,
        name="hold",
    )(array, until)


def attend_kernel(query_places, key_places, value_places, *refs):
    blocks = len(query_places)
    ins, out_refs = refs[:-blocks], refs[-blocks:]
    tokens, part = out_refs[0].shape
    scale = 1.0 / math.sqrt(HD)
    for head in range(part // HD):
        lanes = slice(head * HD, (head + 1) * HD)
        queries, keys, values = (
            jnp.concatenate([ins[source][at, :, lanes] for source, at in places], axis=0)
            for places in (query_places, key_places, value_places)
        )
        scores = (
            lax.dot_general(
                queries, keys, (((1,), (1,)), ((), ())), preferred_element_type=jnp.float32
            )
            * scale
        )
        weights = jnp.exp(scores - jnp.max(scores, axis=1, keepdims=True))
        totals = jnp.sum(weights, axis=1, keepdims=True)
        mixed = jnp.dot(
            weights.astype(jnp.bfloat16), values, preferred_element_type=jnp.float32
        )
        result = (mixed / totals).astype(jnp.bfloat16)
        for at, ref in enumerate(out_refs):
            ref[:, lanes] = result[at * tokens : (at + 1) * tokens]


def unpack_kernel(order, part, *refs):
    ins, out_ref, sems = refs[:-2], refs[-2], refs[-1]
    me = lax.axis_index("blk")
    pairs = []
    for s, ref in zip(order, ins):
        columns = pl.ds(pl.multiple_of((me ^ s) * part, 128), part)
        pairs.append((ref, out_ref.at[0, :, columns]))
    run_copies(pairs, sems)


def local_blocks(query_rows, key_rows, value_rows):
    blocks, columns_of = lax.axis_size("blk"), lax.axis_size("uly")
    tokens, width = query_rows.shape[1:]
    part = width // blocks
    heads = part // HD
    kind = query_rows.dtype
    messages = [(s, "kvq") for s in range(blocks - 1, 0, -1)] + [(0, "kv"), (0, "q")]
    packed = pl.pallas_call(
        functools.partial(pack_kernel, messages, part),
        out_shape=[jax.ShapeDtypeStruct((len(m), tokens, part), kind) for s, m in messages],
        in_specs=[HBM] * 3,
        out_specs=[VMEM] * len(messages),
        scratch_shapes=[pltpu.SemaphoreType.DMA((3 * blocks,))],
        compiler_params=SMALL,
        cost_estimate=pl.CostEstimate(
            flops=0, bytes_accessed=6 * tokens * width * 2, transcendentals=0
        ),
        name="pack",
    )(*[pltpu.with_memory_space_constraint(x, pltpu.HBM) for x in (query_rows, key_rows, value_rows)])

    def to_block(array, s):
        return lax.ppermute(array, "blk", [(i, i ^ s) for i in range(blocks)])

    def to_column(array, t):
        return lax.ppermute(array, "uly", [(i, (i + t) % columns_of) for i in range(columns_of)])

    sent = {message[0]: array for message, array in zip(messages, packed)}
    own_kv, own_q = packed[-2:]
    got = {s: to_block(sent[s], s) for s in (1, 3)}
    got[2] = to_block(hold(sent[2], got[1]), 2)
    held = [own_kv, own_q] + [got[s] for s in range(1, blocks)]
    query_places = [(1, 0)] + [(1 + s, 2) for s in range(1, blocks)]
    key_places = [(0, 0)] + [(1 + s, 0) for s in range(1, blocks)]
    value_places = [(0, 1)] + [(1 + s, 1) for s in range(1, blocks)]
    groups = [join([own_kv, got[1]], [(0, 0), (0, 1), (1, 0), (1, 1)])]
    groups += [join([got[s]], [(0, 0), (0, 1)]) for s in range(blocks - 1, 1, -1)]
    for t in range(1, columns_of):
        for group in groups:
            for at in range(0, group.shape[0], 2):
                key_places.append((len(held), at))
                value_places.append((len(held), at + 1))
            held.append(to_column(group, t))

    all_tokens = tokens * blocks * columns_of
    pairs = heads * tokens * blocks * all_tokens
    mixed = pl.pallas_call(
        functools.partial(attend_kernel, query_places, key_places, value_places),
        out_shape=[jax.ShapeDtypeStruct((tokens, part), kind)] * blocks,
        in_specs=[VMEM] * len(held),
        out_specs=[VMEM] * blocks,
        compiler_params=pltpu.CompilerParams(vmem_limit_bytes=24 * 1024 * 1024),
        cost_estimate=pl.CostEstimate(
            flops=4 * HD * pairs,
            bytes_accessed=2 * part * (2 * all_tokens + 2 * tokens * blocks),
            transcendentals=pairs,
        ),
        name="attend",
    )(*held)

    order = [0] + list(range(blocks - 1, 0, -1))
    back = [to_block(mixed[s], s) if s else mixed[0] for s in order]
    return pl.pallas_call(
        functools.partial(unpack_kernel, order, part),
        out_shape=jax.ShapeDtypeStruct((1, tokens, width), kind),
        in_specs=[VMEM] * blocks,
        out_specs=HBM,
        scratch_shapes=[pltpu.SemaphoreType.DMA((blocks,))],
        compiler_params=SMALL,
        cost_estimate=pl.CostEstimate(
            flops=0, bytes_accessed=2 * tokens * width * 2, transcendentals=0
        ),
        name="unpack",
    )(*back)


def local(query_rows, key_rows, value_rows):
    blocks = lax.axis_size("blk")
    heads = query_rows.shape[2] // HD
    few = blocks == 4 and heads % blocks == 0
    plan = local_blocks if few else local_generic
    return plan(query_rows, key_rows, value_rows)


def solution(mesh):
    in_specs = (
        P("cfg", ("groups", "blk", "uly"), None),
        P("cfg", ("groups", "blk", "uly"), None),
        P("cfg", ("groups", "blk", "uly"), None),
    )
    out_specs = P("cfg", ("groups", "blk", "uly"), None)
    return jax.shard_map(local, mesh=mesh, in_specs=in_specs, out_specs=out_specs, check_vma=False)
```

```python
import functools
import math

import jax
import jax.numpy as jnp
from jax import lax
from jax.experimental import pallas as pl
from jax.experimental.pallas import tpu as pltpu
from jax.sharding import PartitionSpec as P

HD = 128
EFFORT = 15 * 10**8
ANY = pl.BlockSpec(memory_space=pl.ANY)
HBM = pl.BlockSpec(memory_space=pltpu.HBM)
VMEM = pl.BlockSpec(memory_space=pltpu.VMEM)
SMALL = pltpu.CompilerParams(vmem_limit_bytes=4 * 1024 * 1024)


def attend(queries, key_part, value_part):
    query_mat = queries[0, :, 0]
    row_count, head_count, head_size = query_mat.shape
    score_scale = 1.0 / math.sqrt(head_size)
    start_state = (
        jnp.full((head_count, row_count), -1e30, jnp.float32),
        jnp.zeros((head_count, row_count), jnp.float32),
        jnp.zeros((row_count, head_count, head_size), jnp.float32),
    )

    def absorb(state, pieces):
        key_piece = pieces[0][0, :, 0]
        value_piece = pieces[1][0, :, 0]
        scores = (
            jnp.einsum("qhd,khd->hqk", query_mat, key_piece, preferred_element_type=jnp.float32)
            * score_scale
        )
        running, totals, accumulated = state
        new_max = jnp.maximum(running, jnp.max(scores, axis=2))
        weights = jnp.exp(scores - new_max[:, :, None])
        factor = jnp.exp(running - new_max)
        totals = totals * factor + jnp.sum(weights, axis=2)
        probabilities = weights.astype(jnp.bfloat16)
        contrib = jnp.einsum(
            "hqk,khd->qhd", probabilities, value_piece, preferred_element_type=jnp.float32
        )
        accumulated = accumulated * factor.T[:, :, None] + contrib
        return (new_max, totals, accumulated)

    whole_keys, whole_values = (
        lax.all_gather(key_part, "blk", axis=1, tiled=True),
        lax.all_gather(value_part, "blk", axis=1, tiled=True),
    )
    key_count = whole_keys.shape[1]
    block_rows = math.gcd(key_count, 1024)

    def one_block(state, counter):
        offset = counter * block_rows
        key_block = lax.dynamic_slice_in_dim(whole_keys, offset, block_rows, 1)
        value_block = lax.dynamic_slice_in_dim(whole_values, offset, block_rows, 1)
        return (absorb(state, (key_block, value_block)), None)

    result, unused = lax.scan(
        one_block, start_state, jnp.arange(key_count // block_rows, dtype=jnp.int32)
    )
    output = (result[2] / result[1].T[:, :, None]).astype(jnp.bfloat16)
    return output.reshape(1, row_count, 1, head_count, head_size)


def local_generic(query_rows, key_rows, value_rows):
    ulysses = lax.axis_size("uly")
    tokens = query_rows.shape[1]
    width = query_rows.shape[2]
    heads_local = width // HD // ulysses

    def split_heads(array):
        array = array.reshape(1, tokens, ulysses, heads_local, HD)
        return lax.all_to_all(array, "uly", split_axis=2, concat_axis=1, tiled=True)

    mixed = attend(split_heads(query_rows), split_heads(key_rows), split_heads(value_rows))
    merged = lax.all_to_all(mixed, "uly", split_axis=1, concat_axis=2, tiled=True)
    return merged.reshape(1, tokens, width)


def run_copies(pairs, sems):
    started = [pltpu.make_async_copy(src, dst, sems.at[at]) for at, (src, dst) in enumerate(pairs)]
    for copy in started:
        copy.start()
    for copy in started:
        copy.wait()


def pack_kernel(messages, part, q_ref, k_ref, v_ref, *refs):
    outs, sems = refs[:-1], refs[-1]
    sources = {"q": q_ref, "k": k_ref, "v": v_ref}
    me = lax.axis_index("blk")
    pairs = []
    for (s, pieces), out in zip(messages, outs):
        start = 0
        for name, first, lanes in pieces:
            columns = pl.ds(pl.multiple_of((me ^ s) * part + first, 128), lanes)
            pairs.append((sources[name].at[0, :, columns], out.at[:, pl.ds(start, lanes)]))
            start += lanes
    run_copies(pairs, sems)


def join_kernel(pieces, *refs):
    lanes = refs[-1].shape[2]
    for at, (source, start) in enumerate(pieces):
        refs[-1][at] = refs[source][:, start : start + lanes]


def join(arrays, starts, lanes, effort=0, after=()):
    shape = (len(arrays), arrays[0].shape[0], lanes)
    return pl.pallas_call(
        functools.partial(join_kernel, list(enumerate(starts))),
        out_shape=jax.ShapeDtypeStruct(shape, arrays[0].dtype),
        in_specs=[VMEM] * (len(arrays) + len(after)),
        out_specs=VMEM,
        compiler_params=SMALL,
        cost_estimate=pl.CostEstimate(
            flops=effort, bytes_accessed=4 * math.prod(shape), transcendentals=0
        ),
        name="join",
    )(*arrays, *after)


def hold_kernel(array_ref, until_ref, out_ref):
    pass


def hold(array, until):
    return pl.pallas_call(
        hold_kernel,
        out_shape=jax.ShapeDtypeStruct(array.shape, array.dtype),
        in_specs=[ANY, ANY],
        out_specs=ANY,
        input_output_aliases={0: 0},
        compiler_params=SMALL,
        name="hold",
    )(array, until)


def attend_kernel(plan, *refs):
    blocks = len(plan[0][0])
    ins, out_refs = refs[:-blocks], refs[-blocks:]
    tokens = out_refs[0].shape[0]
    scale = 1.0 / math.sqrt(HD)

    def load(place):
        source, row, first = place
        lanes = slice(first, first + HD)
        return ins[source][:, lanes] if row is None else ins[source][row, :, lanes]

    for head, all_places in enumerate(plan):
        queries, keys, values = (
            jnp.concatenate([load(place) for place in places], axis=0) for places in all_places
        )
        scores = (
            lax.dot_general(
                queries, keys, (((1,), (1,)), ((), ())), preferred_element_type=jnp.float32
            )
            * scale
        )
        weights = jnp.exp(scores - jnp.max(scores, axis=1, keepdims=True))
        totals = jnp.sum(weights, axis=1, keepdims=True)
        mixed = jnp.dot(
            weights.astype(jnp.bfloat16), values, preferred_element_type=jnp.float32
        )
        result = (mixed / totals).astype(jnp.bfloat16)
        for block, ref in enumerate(out_refs):
            ref[:, head * HD : (head + 1) * HD] = result[block * tokens : (block + 1) * tokens]


def unpack_kernel(order, part, *refs):
    ins, out_ref, sems = refs[:-2], refs[-2], refs[-1]
    me = lax.axis_index("blk")
    pairs = []
    for s, ref in zip(order, ins):
        columns = pl.ds(pl.multiple_of((me ^ s) * part, 128), part)
        pairs.append((ref, out_ref.at[0, :, columns]))
    run_copies(pairs, sems)


def local_blocks(query_rows, key_rows, value_rows):
    blocks, columns_of = lax.axis_size("blk"), lax.axis_size("uly")
    tokens, width = query_rows.shape[1:]
    part = width // blocks
    heads = part // HD
    kind = query_rows.dtype
    far = list(range(blocks - 1, 1, -1))

    kv, q = (("k", 0, part), ("v", 0, part)), (("q", 0, part),)
    messages = [(s, kv) for s in far] + [(1, kv + q)] + [(s, q) for s in far] + [(0, kv), (0, q)]
    packed = pl.pallas_call(
        functools.partial(pack_kernel, messages, part),
        out_shape=[
            jax.ShapeDtypeStruct((tokens, sum(piece[2] for piece in pieces)), kind)
            for s, pieces in messages
        ],
        in_specs=[HBM] * 3,
        out_specs=[VMEM] * len(messages),
        scratch_shapes=[pltpu.SemaphoreType.DMA((sum(len(m[1]) for m in messages),))],
        compiler_params=SMALL,
        cost_estimate=pl.CostEstimate(
            flops=0, bytes_accessed=6 * tokens * width * 2, transcendentals=0
        ),
        name="pack",
    )(*[pltpu.with_memory_space_constraint(x, pltpu.HBM) for x in (query_rows, key_rows, value_rows)])

    def to_block(array, s):
        return lax.ppermute(array, "blk", [(i, i ^ s) for i in range(blocks)])

    def to_column(array, t):
        return lax.ppermute(array, "uly", [(i, (i + t) % columns_of) for i in range(columns_of)])

    sent = {message: array for message, array in zip(messages, packed)}
    own_kv, own_q = packed[-2:]
    far_kv = [to_block(sent[s, kv], s) for s in far]
    near_kvq = to_block(sent[1, kv + q], 1)
    near_kv = join([own_kv, near_kvq], [0, 0], 2 * part)
    far_q = [to_block(hold(sent[s, q], near_kv), s) for s in far]
    groups = [near_kv, join(far_kv, [0] * len(far), 2 * part)]
    crossed = [to_column(group, t) for group in groups for t in range(1, columns_of)]
    far_q = join(far_q, [0] * len(far), part, EFFORT)
    near_q = join([own_q, near_kvq], [0, 2 * part], part, EFFORT, crossed[: columns_of - 1])
    arrays = [near_q, far_q, near_kvq, own_kv] + far_kv
    key_places = [(at, None, 0) for at in range(2, len(arrays))]
    for array in crossed:
        key_places += [(len(arrays), at, 0) for at in range(array.shape[0])]
        arrays.append(array)
    query_places = [(0, 0, 0), (0, 1, 0)]
    query_places += [(1, far.index(s), 0) for s in range(2, blocks)]

    def moved(places, lanes):
        return [(source, row, first + lanes) for source, row, first in places]

    plan = [
        (moved(query_places, lane), moved(key_places, lane), moved(key_places, part + lane))
        for lane in range(0, part, HD)
    ]
    all_tokens = tokens * blocks * columns_of

    pairs = heads * tokens * blocks * all_tokens
    mixed = pl.pallas_call(
        functools.partial(attend_kernel, plan),
        out_shape=[jax.ShapeDtypeStruct((tokens, part), kind)] * blocks,
        in_specs=[VMEM] * len(arrays),
        out_specs=[VMEM] * blocks,
        compiler_params=pltpu.CompilerParams(vmem_limit_bytes=24 * 1024 * 1024),
        cost_estimate=pl.CostEstimate(
            flops=4 * HD * pairs,
            bytes_accessed=4 * part * (all_tokens + tokens * blocks),
            transcendentals=pairs,
        ),
        name="attend",
    )(*arrays)

    order = [0] + far + [1]
    back = [to_block(mixed[s], s) if s else mixed[0] for s in order]
    return pl.pallas_call(
        functools.partial(unpack_kernel, order, part),
        out_shape=jax.ShapeDtypeStruct((1, tokens, width), kind),
        in_specs=[VMEM] * blocks,
        out_specs=HBM,
        scratch_shapes=[pltpu.SemaphoreType.DMA((blocks,))],
        compiler_params=SMALL,
        cost_estimate=pl.CostEstimate(
            flops=0, bytes_accessed=2 * tokens * width * 2, transcendentals=0
        ),
        name="unpack",
    )(*back)


def local(query_rows, key_rows, value_rows):
    blocks = lax.axis_size("blk")
    heads = query_rows.shape[2] // HD
    few = blocks == 4 and heads % blocks == 0
    plan = local_blocks if few else local_generic
    return plan(query_rows, key_rows, value_rows)


def solution(mesh):
    in_specs = (
        P("cfg", ("groups", "blk", "uly"), None),
        P("cfg", ("groups", "blk", "uly"), None),
        P("cfg", ("groups", "blk", "uly"), None),
    )
    out_specs = P("cfg", ("groups", "blk", "uly"), None)
    return jax.shard_map(local, mesh=mesh, in_specs=in_specs, out_specs=out_specs, check_vma=False)
```

```python
import functools
import math

import jax
import jax.numpy as jnp
from jax import lax
from jax.experimental import pallas as pl
from jax.experimental.pallas import tpu as pltpu
from jax.sharding import PartitionSpec as P

HD = 128
HBM = pl.BlockSpec(memory_space=pltpu.HBM)
VMEM = pl.BlockSpec(memory_space=pltpu.VMEM)
SMALL = pltpu.CompilerParams(vmem_limit_bytes=4 * 1024 * 1024)


def attend(queries, key_part, value_part):
    query_mat = queries[0, :, 0]
    row_count, head_count, head_size = query_mat.shape
    score_scale = 1.0 / math.sqrt(head_size)
    start_state = (
        jnp.full((head_count, row_count), -1e30, jnp.float32),
        jnp.zeros((head_count, row_count), jnp.float32),
        jnp.zeros((row_count, head_count, head_size), jnp.float32),
    )

    def absorb(state, pieces):
        key_piece = pieces[0][0, :, 0]
        value_piece = pieces[1][0, :, 0]
        scores = (
            jnp.einsum("qhd,khd->hqk", query_mat, key_piece, preferred_element_type=jnp.float32)
            * score_scale
        )
        running, totals, accumulated = state
        new_max = jnp.maximum(running, jnp.max(scores, axis=2))
        weights = jnp.exp(scores - new_max[:, :, None])
        factor = jnp.exp(running - new_max)
        totals = totals * factor + jnp.sum(weights, axis=2)
        probabilities = weights.astype(jnp.bfloat16)
        contrib = jnp.einsum(
            "hqk,khd->qhd", probabilities, value_piece, preferred_element_type=jnp.float32
        )
        accumulated = accumulated * factor.T[:, :, None] + contrib
        return (new_max, totals, accumulated)

    whole_keys, whole_values = (
        lax.all_gather(key_part, "blk", axis=1, tiled=True),
        lax.all_gather(value_part, "blk", axis=1, tiled=True),
    )
    key_count = whole_keys.shape[1]
    block_rows = math.gcd(key_count, 1024)

    def one_block(state, counter):
        offset = counter * block_rows
        key_block = lax.dynamic_slice_in_dim(whole_keys, offset, block_rows, 1)
        value_block = lax.dynamic_slice_in_dim(whole_values, offset, block_rows, 1)
        return (absorb(state, (key_block, value_block)), None)

    result, unused = lax.scan(
        one_block, start_state, jnp.arange(key_count // block_rows, dtype=jnp.int32)
    )
    output = (result[2] / result[1].T[:, :, None]).astype(jnp.bfloat16)
    return output.reshape(1, row_count, 1, head_count, head_size)


def local_generic(query_rows, key_rows, value_rows):
    ulysses = lax.axis_size("uly")
    tokens = query_rows.shape[1]
    width = query_rows.shape[2]
    heads_local = width // HD // ulysses

    def split_heads(array):
        array = array.reshape(1, tokens, ulysses, heads_local, HD)
        return lax.all_to_all(array, "uly", split_axis=2, concat_axis=1, tiled=True)

    mixed = attend(split_heads(query_rows), split_heads(key_rows), split_heads(value_rows))
    merged = lax.all_to_all(mixed, "uly", split_axis=1, concat_axis=2, tiled=True)
    return merged.reshape(1, tokens, width)


AXES = ("blk", "uly")


def place_of(mask, members):
    here = lax.axis_index("blk") * lax.axis_size("uly") + lax.axis_index("uly")
    return lax.rem(here ^ mask, members)


def run_copies(pairs, sems):
    started = [pltpu.make_async_copy(src, dst, sems.at[at]) for at, (src, dst) in enumerate(pairs)]
    for copy in started:
        copy.start()
    for copy in started:
        copy.wait()


def pack_kernel(messages, members, part, q_ref, k_ref, v_ref, *refs):
    outs, sems = refs[:-1], refs[-1]
    sources = {"q": q_ref, "k": k_ref, "v": v_ref}
    pairs = []
    for (mask, names), out in zip(messages, outs):
        columns = pl.ds(pl.multiple_of(place_of(mask, members) * part, 128), part)
        for at, name in enumerate(names):
            pairs.append((sources[name].at[0, :, columns], out.at[:, pl.ds(at * part, part)]))
    run_copies(pairs, sems)


def attend_kernel(members, *refs):
    ins, out_refs = refs[:-members], refs[-members:]
    tokens, part = out_refs[0].shape
    scale = 1.0 / math.sqrt(HD)

    def rows(sources, first):
        return jnp.concatenate([ref[:, first : first + HD] for ref in sources], axis=0)

    for lane in range(0, part, HD):
        queries = rows(ins[:members], 2 * part + lane)
        keys = rows(ins, lane)
        values = rows(ins, part + lane)
        scores = (
            lax.dot_general(
                queries, keys, (((1,), (1,)), ((), ())), preferred_element_type=jnp.float32
            )
            * scale
        )
        weights = jnp.exp(scores - jnp.max(scores, axis=1, keepdims=True))
        totals = jnp.sum(weights, axis=1, keepdims=True)
        mixed = jnp.dot(
            weights.astype(jnp.bfloat16), values, preferred_element_type=jnp.float32
        )
        result = (mixed / totals).astype(jnp.bfloat16)
        for at, ref in enumerate(out_refs):
            ref[:, lane : lane + HD] = result[at * tokens : (at + 1) * tokens]


def unpack_kernel(members, part, *refs):
    ins, out_ref, sems = refs[:-2], refs[-2], refs[-1]
    pairs = []
    for mask, ref in enumerate(ins):
        columns = pl.ds(pl.multiple_of(place_of(mask, members) * part, 128), part)
        pairs.append((ref, out_ref.at[0, :, columns]))
    run_copies(pairs, sems)


def local_halves(query_rows, key_rows, value_rows):
    devices = lax.axis_size("blk") * lax.axis_size("uly")
    members = devices // 2
    tokens, width = query_rows.shape[1:]
    part = width // members
    heads = part // HD
    kind = query_rows.dtype

    messages = [(mask, "kv") for mask in range(members, devices)]
    messages += [(mask, "kvq") for mask in range(members)]
    packed = pl.pallas_call(
        functools.partial(pack_kernel, messages, members, part),
        out_shape=[jax.ShapeDtypeStruct((tokens, len(m[1]) * part), kind) for m in messages],
        in_specs=[HBM] * 3,
        out_specs=[VMEM] * len(messages),
        scratch_shapes=[pltpu.SemaphoreType.DMA((sum(len(m[1]) for m in messages),))],
        compiler_params=SMALL,
        cost_estimate=pl.CostEstimate(
            flops=0, bytes_accessed=6 * tokens * width * 2, transcendentals=0
        ),
        name="pack",
    )(*[pltpu.with_memory_space_constraint(x, pltpu.HBM) for x in (query_rows, key_rows, value_rows)])

    def swap(array, mask):
        return lax.ppermute(array, AXES, [(i, i ^ mask) for i in range(devices)]) if mask else array

    got = [swap(array, mask) for (mask, names), array in zip(messages, packed)]
    arrays = got[members:] + got[:members]

    pairs = heads * tokens * members * tokens * devices
    mixed = pl.pallas_call(
        functools.partial(attend_kernel, members),
        out_shape=[jax.ShapeDtypeStruct((tokens, part), kind)] * members,
        in_specs=[VMEM] * devices,
        out_specs=[VMEM] * members,
        compiler_params=pltpu.CompilerParams(vmem_limit_bytes=24 * 1024 * 1024),
        cost_estimate=pl.CostEstimate(
            flops=4 * HD * pairs,
            bytes_accessed=4 * part * tokens * (devices + members),
            transcendentals=pairs,
        ),
        name="attend",
    )(*arrays)

    back = [swap(array, mask) for mask, array in enumerate(mixed)]
    return pl.pallas_call(
        functools.partial(unpack_kernel, members, part),
        out_shape=jax.ShapeDtypeStruct((1, tokens, width), kind),
        in_specs=[VMEM] * members,
        out_specs=HBM,
        scratch_shapes=[pltpu.SemaphoreType.DMA((members,))],
        compiler_params=SMALL,
        cost_estimate=pl.CostEstimate(
            flops=0, bytes_accessed=2 * tokens * width * 2, transcendentals=0
        ),
        name="unpack",
    )(*back)


def local(query_rows, key_rows, value_rows):
    blocks, columns = lax.axis_size("blk"), lax.axis_size("uly")
    heads = query_rows.shape[2] // HD
    devices = blocks * columns
    powers = devices & (devices - 1) == 0 and blocks > 1
    few = powers and devices <= 8 and heads % (devices // 2) == 0
    plan = local_halves if few else local_generic
    return plan(query_rows, key_rows, value_rows)


def solution(mesh):
    in_specs = (
        P("cfg", ("groups", "blk", "uly"), None),
        P("cfg", ("groups", "blk", "uly"), None),
        P("cfg", ("groups", "blk", "uly"), None),
    )
    out_specs = P("cfg", ("groups", "blk", "uly"), None)
    return jax.shard_map(local, mesh=mesh, in_specs=in_specs, out_specs=out_specs, check_vma=False)
```

```python
import functools
import math

import jax
import jax.numpy as jnp
from jax import lax
from jax.experimental import pallas as pl
from jax.experimental.pallas import tpu as pltpu
from jax.sharding import PartitionSpec as P

HD = 128
EFFORT = 10**8
ANY = pl.BlockSpec(memory_space=pl.ANY)
HBM = pl.BlockSpec(memory_space=pltpu.HBM)
VMEM = pl.BlockSpec(memory_space=pltpu.VMEM)
SMALL = pltpu.CompilerParams(vmem_limit_bytes=4 * 1024 * 1024)


def attend(queries, key_part, value_part):
    query_mat = queries[0, :, 0]
    row_count, head_count, head_size = query_mat.shape
    score_scale = 1.0 / math.sqrt(head_size)
    start_state = (
        jnp.full((head_count, row_count), -1e30, jnp.float32),
        jnp.zeros((head_count, row_count), jnp.float32),
        jnp.zeros((row_count, head_count, head_size), jnp.float32),
    )

    def absorb(state, pieces):
        key_piece = pieces[0][0, :, 0]
        value_piece = pieces[1][0, :, 0]
        scores = (
            jnp.einsum("qhd,khd->hqk", query_mat, key_piece, preferred_element_type=jnp.float32)
            * score_scale
        )
        running, totals, accumulated = state
        new_max = jnp.maximum(running, jnp.max(scores, axis=2))
        weights = jnp.exp(scores - new_max[:, :, None])
        factor = jnp.exp(running - new_max)
        totals = totals * factor + jnp.sum(weights, axis=2)
        probabilities = weights.astype(jnp.bfloat16)
        contrib = jnp.einsum(
            "hqk,khd->qhd", probabilities, value_piece, preferred_element_type=jnp.float32
        )
        accumulated = accumulated * factor.T[:, :, None] + contrib
        return (new_max, totals, accumulated)

    whole_keys, whole_values = (
        lax.all_gather(key_part, "blk", axis=1, tiled=True),
        lax.all_gather(value_part, "blk", axis=1, tiled=True),
    )
    key_count = whole_keys.shape[1]
    block_rows = math.gcd(key_count, 1024)

    def one_block(state, counter):
        offset = counter * block_rows
        key_block = lax.dynamic_slice_in_dim(whole_keys, offset, block_rows, 1)
        value_block = lax.dynamic_slice_in_dim(whole_values, offset, block_rows, 1)
        return (absorb(state, (key_block, value_block)), None)

    result, unused = lax.scan(
        one_block, start_state, jnp.arange(key_count // block_rows, dtype=jnp.int32)
    )
    output = (result[2] / result[1].T[:, :, None]).astype(jnp.bfloat16)
    return output.reshape(1, row_count, 1, head_count, head_size)


def local_generic(query_rows, key_rows, value_rows):
    ulysses = lax.axis_size("uly")
    tokens = query_rows.shape[1]
    width = query_rows.shape[2]
    heads_local = width // HD // ulysses

    def split_heads(array):
        array = array.reshape(1, tokens, ulysses, heads_local, HD)
        return lax.all_to_all(array, "uly", split_axis=2, concat_axis=1, tiled=True)

    mixed = attend(split_heads(query_rows), split_heads(key_rows), split_heads(value_rows))
    merged = lax.all_to_all(mixed, "uly", split_axis=1, concat_axis=2, tiled=True)
    return merged.reshape(1, tokens, width)


def run_copies(pairs, sems):
    started = [pltpu.make_async_copy(src, dst, sems.at[at]) for at, (src, dst) in enumerate(pairs)]
    for copy in started:
        copy.start()
    for copy in started:
        copy.wait()


def pack_kernel(messages, part, q_ref, k_ref, v_ref, *refs):
    outs, sems = refs[:-1], refs[-1]
    sources = {"q": q_ref, "k": k_ref, "v": v_ref}
    me = lax.axis_index("blk")
    pairs = []
    for (s, pieces), out in zip(messages, outs):
        start = 0
        for name, first, lanes in pieces:
            columns = pl.ds(pl.multiple_of((me ^ s) * part + first, 128), lanes)
            pairs.append((sources[name].at[0, :, columns], out.at[:, pl.ds(start, lanes)]))
            start += lanes
    run_copies(pairs, sems)


def join_kernel(pieces, *refs):
    lanes = refs[-1].shape[2]
    for at, (source, start) in enumerate(pieces):
        refs[-1][at] = refs[source][:, start : start + lanes]


def join(arrays, starts, lanes, effort=0, after=()):
    shape = (len(arrays), arrays[0].shape[0], lanes)
    return pl.pallas_call(
        functools.partial(join_kernel, list(enumerate(starts))),
        out_shape=jax.ShapeDtypeStruct(shape, arrays[0].dtype),
        in_specs=[VMEM] * (len(arrays) + len(after)),
        out_specs=VMEM,
        compiler_params=SMALL,
        cost_estimate=pl.CostEstimate(
            flops=effort, bytes_accessed=4 * math.prod(shape), transcendentals=0
        ),
        name="join",
    )(*arrays, *after)


def hold_kernel(array_ref, until_ref, out_ref):
    pass


def hold(array, until):
    return pl.pallas_call(
        hold_kernel,
        out_shape=jax.ShapeDtypeStruct(array.shape, array.dtype),
        in_specs=[ANY, ANY],
        out_specs=ANY,
        input_output_aliases={0: 0},
        compiler_params=SMALL,
        name="hold",
    )(array, until)


def attend_kernel(plan, *refs):
    blocks = len(plan[0][0])
    ins, out_refs = refs[:-blocks], refs[-blocks:]
    tokens = out_refs[0].shape[0]
    scale = 1.0 / math.sqrt(HD)

    def load(place):
        source, row, first = place
        lanes = slice(first, first + HD)
        return ins[source][:, lanes] if row is None else ins[source][row, :, lanes]

    for head, all_places in enumerate(plan):
        queries, keys, values = (
            jnp.concatenate([load(place) for place in places], axis=0) for places in all_places
        )
        scores = (
            lax.dot_general(
                queries, keys, (((1,), (1,)), ((), ())), preferred_element_type=jnp.float32
            )
            * scale
        )
        weights = jnp.exp(scores - jnp.max(scores, axis=1, keepdims=True))
        totals = jnp.sum(weights, axis=1, keepdims=True)
        mixed = jnp.dot(
            weights.astype(jnp.bfloat16), values, preferred_element_type=jnp.float32
        )
        result = (mixed / totals).astype(jnp.bfloat16)
        for block, ref in enumerate(out_refs):
            ref[:, head * HD : (head + 1) * HD] = result[block * tokens : (block + 1) * tokens]


def unpack_kernel(order, part, *refs):
    ins, out_ref, sems = refs[:-2], refs[-2], refs[-1]
    me = lax.axis_index("blk")
    pairs = []
    for s, ref in zip(order, ins):
        columns = pl.ds(pl.multiple_of((me ^ s) * part, 128), part)
        pairs.append((ref, out_ref.at[0, :, columns]))
    run_copies(pairs, sems)


def local_blocks(query_rows, key_rows, value_rows):
    blocks, columns_of = lax.axis_size("blk"), lax.axis_size("uly")
    tokens, width = query_rows.shape[1:]
    part = width // blocks
    heads = part // HD
    kind = query_rows.dtype
    far = list(range(blocks - 1, 1, -1))

    kv, q = (("k", 0, part), ("v", 0, part)), (("q", 0, part),)
    messages = [(s, kv) for s in far] + [(1, kv + q)] + [(s, q) for s in far] + [(0, kv), (0, q)]
    packed = pl.pallas_call(
        functools.partial(pack_kernel, messages, part),
        out_shape=[
            jax.ShapeDtypeStruct((tokens, sum(piece[2] for piece in pieces)), kind)
            for s, pieces in messages
        ],
        in_specs=[HBM] * 3,
        out_specs=[VMEM] * len(messages),
        scratch_shapes=[pltpu.SemaphoreType.DMA((sum(len(m[1]) for m in messages),))],
        compiler_params=SMALL,
        cost_estimate=pl.CostEstimate(
            flops=0, bytes_accessed=6 * tokens * width * 2, transcendentals=0
        ),
        name="pack",
    )(*[pltpu.with_memory_space_constraint(x, pltpu.HBM) for x in (query_rows, key_rows, value_rows)])

    def to_block(array, s):
        return lax.ppermute(array, "blk", [(i, i ^ s) for i in range(blocks)])

    def to_column(array, t):
        return lax.ppermute(array, "uly", [(i, (i + t) % columns_of) for i in range(columns_of)])

    sent = {message: array for message, array in zip(messages, packed)}
    own_kv, own_q = packed[-2:]
    far_kv = [to_block(sent[s, kv], s) for s in far]
    near_kvq = to_block(sent[1, kv + q], 1)
    near_kv = join([own_kv, near_kvq], [0, 0], 2 * part)
    far_q = [to_block(hold(sent[s, q], near_kv), s) for s in far]
    groups = [near_kv, join(far_kv, [0] * len(far), 2 * part)]
    crossed = [to_column(group, t) for group in groups for t in range(1, columns_of)]
    far_q = join(far_q, [0] * len(far), part)
    near_q = join([own_q, near_kvq], [0, 2 * part], part, EFFORT, crossed[: columns_of - 1])
    arrays = [near_q, far_q, near_kvq, own_kv] + far_kv
    key_places = [(at, None, 0) for at in range(2, len(arrays))]
    for array in crossed:
        key_places += [(len(arrays), at, 0) for at in range(array.shape[0])]
        arrays.append(array)
    query_places = [(0, 0, 0), (0, 1, 0)]
    query_places += [(1, far.index(s), 0) for s in range(2, blocks)]

    def moved(places, lanes):
        return [(source, row, first + lanes) for source, row, first in places]

    plan = [
        (moved(query_places, lane), moved(key_places, lane), moved(key_places, part + lane))
        for lane in range(0, part, HD)
    ]
    all_tokens = tokens * blocks * columns_of

    pairs = heads * tokens * blocks * all_tokens
    mixed = pl.pallas_call(
        functools.partial(attend_kernel, plan),
        out_shape=[jax.ShapeDtypeStruct((tokens, part), kind)] * blocks,
        in_specs=[VMEM] * len(arrays),
        out_specs=[VMEM] * blocks,
        compiler_params=pltpu.CompilerParams(vmem_limit_bytes=24 * 1024 * 1024),
        cost_estimate=pl.CostEstimate(
            flops=4 * HD * pairs,
            bytes_accessed=4 * part * (all_tokens + tokens * blocks),
            transcendentals=pairs,
        ),
        name="attend",
    )(*arrays)

    order = [0] + far + [1]
    back = [to_block(mixed[s], s) if s else mixed[0] for s in order]
    return pl.pallas_call(
        functools.partial(unpack_kernel, order, part),
        out_shape=jax.ShapeDtypeStruct((1, tokens, width), kind),
        in_specs=[VMEM] * blocks,
        out_specs=HBM,
        scratch_shapes=[pltpu.SemaphoreType.DMA((blocks,))],
        compiler_params=SMALL,
        cost_estimate=pl.CostEstimate(
            flops=0, bytes_accessed=2 * tokens * width * 2, transcendentals=0
        ),
        name="unpack",
    )(*back)


def local(query_rows, key_rows, value_rows):
    blocks = lax.axis_size("blk")
    heads = query_rows.shape[2] // HD
    few = blocks == 4 and heads % blocks == 0
    plan = local_blocks if few else local_generic
    return plan(query_rows, key_rows, value_rows)


def solution(mesh):
    in_specs = (
        P("cfg", ("groups", "blk", "uly"), None),
        P("cfg", ("groups", "blk", "uly"), None),
        P("cfg", ("groups", "blk", "uly"), None),
    )
    out_specs = P("cfg", ("groups", "blk", "uly"), None)
    return jax.shard_map(local, mesh=mesh, in_specs=in_specs, out_specs=out_specs, check_vma=False)
```

```python
import functools
import math

import jax
import jax.numpy as jnp
from jax import lax
from jax.experimental import pallas as pl
from jax.experimental.pallas import tpu as pltpu
from jax.sharding import PartitionSpec as P

HD = 128
EFFORT = 4 * 10**9
ANY = pl.BlockSpec(memory_space=pl.ANY)
HBM = pl.BlockSpec(memory_space=pltpu.HBM)
VMEM = pl.BlockSpec(memory_space=pltpu.VMEM)
SMALL = pltpu.CompilerParams(vmem_limit_bytes=4 * 1024 * 1024)


def attend(queries, key_part, value_part):
    query_mat = queries[0, :, 0]
    row_count, head_count, head_size = query_mat.shape
    score_scale = 1.0 / math.sqrt(head_size)
    start_state = (
        jnp.full((head_count, row_count), -1e30, jnp.float32),
        jnp.zeros((head_count, row_count), jnp.float32),
        jnp.zeros((row_count, head_count, head_size), jnp.float32),
    )

    def absorb(state, pieces):
        key_piece = pieces[0][0, :, 0]
        value_piece = pieces[1][0, :, 0]
        scores = (
            jnp.einsum("qhd,khd->hqk", query_mat, key_piece, preferred_element_type=jnp.float32)
            * score_scale
        )
        running, totals, accumulated = state
        new_max = jnp.maximum(running, jnp.max(scores, axis=2))
        weights = jnp.exp(scores - new_max[:, :, None])
        factor = jnp.exp(running - new_max)
        totals = totals * factor + jnp.sum(weights, axis=2)
        probabilities = weights.astype(jnp.bfloat16)
        contrib = jnp.einsum(
            "hqk,khd->qhd", probabilities, value_piece, preferred_element_type=jnp.float32
        )
        accumulated = accumulated * factor.T[:, :, None] + contrib
        return (new_max, totals, accumulated)

    whole_keys, whole_values = (
        lax.all_gather(key_part, "blk", axis=1, tiled=True),
        lax.all_gather(value_part, "blk", axis=1, tiled=True),
    )
    key_count = whole_keys.shape[1]
    block_rows = math.gcd(key_count, 1024)

    def one_block(state, counter):
        offset = counter * block_rows
        key_block = lax.dynamic_slice_in_dim(whole_keys, offset, block_rows, 1)
        value_block = lax.dynamic_slice_in_dim(whole_values, offset, block_rows, 1)
        return (absorb(state, (key_block, value_block)), None)

    result, unused = lax.scan(
        one_block, start_state, jnp.arange(key_count // block_rows, dtype=jnp.int32)
    )
    output = (result[2] / result[1].T[:, :, None]).astype(jnp.bfloat16)
    return output.reshape(1, row_count, 1, head_count, head_size)


def local_generic(query_rows, key_rows, value_rows):
    ulysses = lax.axis_size("uly")
    tokens = query_rows.shape[1]
    width = query_rows.shape[2]
    heads_local = width // HD // ulysses

    def split_heads(array):
        array = array.reshape(1, tokens, ulysses, heads_local, HD)
        return lax.all_to_all(array, "uly", split_axis=2, concat_axis=1, tiled=True)

    mixed = attend(split_heads(query_rows), split_heads(key_rows), split_heads(value_rows))
    merged = lax.all_to_all(mixed, "uly", split_axis=1, concat_axis=2, tiled=True)
    return merged.reshape(1, tokens, width)


AXES = ("blk", "uly")


def place_of(mask, members):
    here = lax.axis_index("blk") * lax.axis_size("uly") + lax.axis_index("uly")
    return lax.rem(here ^ mask, members)


def run_copies(pairs, sems):
    started = [pltpu.make_async_copy(src, dst, sems.at[at]) for at, (src, dst) in enumerate(pairs)]
    for copy in started:
        copy.start()
    for copy in started:
        copy.wait()


def pack_kernel(messages, members, part, q_ref, k_ref, v_ref, *refs):
    outs, sems = refs[:-1], refs[-1]
    sources = {"q": q_ref, "k": k_ref, "v": v_ref}
    pairs = []
    for (mask, names), out in zip(messages, outs):
        columns = pl.ds(pl.multiple_of(place_of(mask, members) * part, 128), part)
        for at, name in enumerate(names):
            pairs.append((sources[name].at[0, :, columns], out.at[:, pl.ds(at * part, part)]))
    run_copies(pairs, sems)


def hold_kernel(*refs):
    pass


def hold(arrays, until=(), effort=0):
    return pl.pallas_call(
        hold_kernel,
        out_shape=[jax.ShapeDtypeStruct(array.shape, array.dtype) for array in arrays],
        in_specs=[ANY] * (len(arrays) + len(until)),
        out_specs=[ANY] * len(arrays),
        input_output_aliases={at: at for at in range(len(arrays))},
        compiler_params=SMALL,
        cost_estimate=pl.CostEstimate(flops=effort, bytes_accessed=0, transcendentals=0),
        name="hold",
    )(*arrays, *until)


def rows(sources, first):
    return jnp.concatenate([ref[:, first : first + HD] for ref in sources], axis=0)


def scores_of(query_refs, key_refs, lane, part):
    scores = lax.dot_general(
        rows(query_refs, 2 * part + lane),
        rows(key_refs, lane),
        (((1,), (1,)), ((), ())),
        preferred_element_type=jnp.float32,
    )
    return scores * (1.0 / math.sqrt(HD))


def mix(weights, key_refs, lane, part):
    values = rows(key_refs, part + lane)
    return jnp.dot(weights.astype(jnp.bfloat16), values, preferred_element_type=jnp.float32)


def first_kernel(members, *refs):
    ins, (largest_ref, totals_ref, mixed_ref) = refs[:-3], refs[-3:]
    part = mixed_ref.shape[0] * HD
    for head in range(part // HD):
        scores = scores_of(ins[:members], ins, head * HD, part)
        largest = jnp.max(scores, axis=1, keepdims=True)
        weights = jnp.exp(scores - largest)
        totals = jnp.sum(weights, axis=1, keepdims=True)
        largest_ref[head] = jnp.broadcast_to(largest, largest_ref.shape[1:])
        totals_ref[head] = jnp.broadcast_to(totals, totals_ref.shape[1:])
        mixed_ref[head] = mix(weights, ins, head * HD, part)


def last_kernel(members, *refs):
    query_refs, key_refs = refs[:members], refs[members:-3 - members]
    largest_ref, totals_ref, mixed_ref = refs[-3 - members : -members]
    out_refs = refs[-members:]
    tokens, part = out_refs[0].shape
    for head in range(part // HD):
        lane = head * HD
        scores = scores_of(query_refs, key_refs, lane, part)
        before = largest_ref[head][:, :1]
        largest = jnp.maximum(before, jnp.max(scores, axis=1, keepdims=True))
        weights = jnp.exp(scores - largest)
        factor = jnp.exp(before - largest)
        totals = totals_ref[head][:, :1] * factor + jnp.sum(weights, axis=1, keepdims=True)
        mixed = mixed_ref[head] * factor + mix(weights, key_refs, lane, part)
        result = (mixed / totals).astype(jnp.bfloat16)
        for at, ref in enumerate(out_refs):
            ref[:, lane : lane + HD] = result[at * tokens : (at + 1) * tokens]


def unpack_kernel(members, order, part, *refs):
    ins, out_ref, sems = refs[:-2], refs[-2], refs[-1]
    pairs = []
    for mask, ref in zip(order, ins):
        columns = pl.ds(pl.multiple_of(place_of(mask, members) * part, 128), part)
        pairs.append((ref, out_ref.at[0, :, columns]))
    run_copies(pairs, sems)


def local_halves(query_rows, key_rows, value_rows):
    devices = lax.axis_size("blk") * lax.axis_size("uly")
    members = devices // 2
    tokens, width = query_rows.shape[1:]
    part = width // members
    heads = part // HD
    kind = query_rows.dtype

    messages = [(mask, "kv") for mask in range(devices - 1, members - 1, -1)]
    messages += [(mask, "kvq") for mask in range(members)]
    packed = pl.pallas_call(
        functools.partial(pack_kernel, messages, members, part),
        out_shape=[jax.ShapeDtypeStruct((tokens, len(m[1]) * part), kind) for m in messages],
        in_specs=[HBM] * 3,
        out_specs=[VMEM] * len(messages),
        scratch_shapes=[pltpu.SemaphoreType.DMA((sum(len(m[1]) for m in messages),))],
        compiler_params=SMALL,
        cost_estimate=pl.CostEstimate(
            flops=0, bytes_accessed=6 * tokens * width * 2, transcendentals=0
        ),
        name="pack",
    )(*[pltpu.with_memory_space_constraint(x, pltpu.HBM) for x in (query_rows, key_rows, value_rows)])

    def swap(array, mask):
        return lax.ppermute(array, AXES, [(i, i ^ mask) for i in range(devices)]) if mask else array

    far = [swap(array, mask) for (mask, names), array in zip(messages[:members], packed)]
    near = [packed[members]]
    for mask in range(1, members):
        ready = hold([packed[members + mask]], near[1:2])[0] if mask > 1 else packed[members + 1]
        near.append(swap(ready, mask))
    soon, late = near + list(hold(far[: members // 2], effort=EFFORT)), far[members // 2 :]

    def cost_of(keys):
        pairs = heads * tokens * members * tokens * len(keys)
        return pl.CostEstimate(
            flops=4 * HD * pairs,
            bytes_accessed=4 * part * tokens * (members + len(keys)),
            transcendentals=pairs,
        )

    roomy = pltpu.CompilerParams(vmem_limit_bytes=24 * 1024 * 1024)
    state = pl.pallas_call(
        functools.partial(first_kernel, members),
        out_shape=[jax.ShapeDtypeStruct((heads, tokens * members, HD), jnp.float32)] * 3,
        in_specs=[VMEM] * len(soon),
        out_specs=[VMEM] * 3,
        compiler_params=roomy,
        cost_estimate=cost_of(soon),
        name="first",
    )(*soon)
    mixed = pl.pallas_call(
        functools.partial(last_kernel, members),
        out_shape=[jax.ShapeDtypeStruct((tokens, part), kind)] * members,
        in_specs=[VMEM] * (members + len(late) + 3),
        out_specs=[VMEM] * members,
        compiler_params=roomy,
        cost_estimate=cost_of(late),
        name="last",
    )(*near, *late, *state)

    order = list(range(members))[::-1]
    back = [swap(mixed[mask], mask) for mask in order]
    return pl.pallas_call(
        functools.partial(unpack_kernel, members, order, part),
        out_shape=jax.ShapeDtypeStruct((1, tokens, width), kind),
        in_specs=[VMEM] * members,
        out_specs=HBM,
        scratch_shapes=[pltpu.SemaphoreType.DMA((members,))],
        compiler_params=SMALL,
        cost_estimate=pl.CostEstimate(
            flops=0, bytes_accessed=2 * tokens * width * 2, transcendentals=0
        ),
        name="unpack",
    )(*back)


def local(query_rows, key_rows, value_rows):
    blocks, columns = lax.axis_size("blk"), lax.axis_size("uly")
    heads = query_rows.shape[2] // HD
    devices = blocks * columns
    powers = devices & (devices - 1) == 0 and blocks > 1
    few = powers and devices <= 8 and heads % (devices // 2) == 0
    plan = local_halves if few else local_generic
    return plan(query_rows, key_rows, value_rows)


def solution(mesh):
    in_specs = (
        P("cfg", ("groups", "blk", "uly"), None),
        P("cfg", ("groups", "blk", "uly"), None),
        P("cfg", ("groups", "blk", "uly"), None),
    )
    out_specs = P("cfg", ("groups", "blk", "uly"), None)
    return jax.shard_map(local, mesh=mesh, in_specs=in_specs, out_specs=out_specs, check_vma=False)
```

```python
import functools
import math

import jax
import jax.numpy as jnp
from jax import lax
from jax.experimental import pallas as pl
from jax.experimental.pallas import tpu as pltpu
from jax.sharding import PartitionSpec as P

HD = 128
EFFORT = 10**9
ANY = pl.BlockSpec(memory_space=pl.ANY)
HBM = pl.BlockSpec(memory_space=pltpu.HBM)
VMEM = pl.BlockSpec(memory_space=pltpu.VMEM)
SMALL = pltpu.CompilerParams(vmem_limit_bytes=4 * 1024 * 1024)


def attend(queries, key_part, value_part):
    query_mat = queries[0, :, 0]
    row_count, head_count, head_size = query_mat.shape
    score_scale = 1.0 / math.sqrt(head_size)
    start_state = (
        jnp.full((head_count, row_count), -1e30, jnp.float32),
        jnp.zeros((head_count, row_count), jnp.float32),
        jnp.zeros((row_count, head_count, head_size), jnp.float32),
    )

    def absorb(state, pieces):
        key_piece = pieces[0][0, :, 0]
        value_piece = pieces[1][0, :, 0]
        scores = (
            jnp.einsum("qhd,khd->hqk", query_mat, key_piece, preferred_element_type=jnp.float32)
            * score_scale
        )
        running, totals, accumulated = state
        new_max = jnp.maximum(running, jnp.max(scores, axis=2))
        weights = jnp.exp(scores - new_max[:, :, None])
        factor = jnp.exp(running - new_max)
        totals = totals * factor + jnp.sum(weights, axis=2)
        probabilities = weights.astype(jnp.bfloat16)
        contrib = jnp.einsum(
            "hqk,khd->qhd", probabilities, value_piece, preferred_element_type=jnp.float32
        )
        accumulated = accumulated * factor.T[:, :, None] + contrib
        return (new_max, totals, accumulated)

    whole_keys, whole_values = (
        lax.all_gather(key_part, "blk", axis=1, tiled=True),
        lax.all_gather(value_part, "blk", axis=1, tiled=True),
    )
    key_count = whole_keys.shape[1]
    block_rows = math.gcd(key_count, 1024)

    def one_block(state, counter):
        offset = counter * block_rows
        key_block = lax.dynamic_slice_in_dim(whole_keys, offset, block_rows, 1)
        value_block = lax.dynamic_slice_in_dim(whole_values, offset, block_rows, 1)
        return (absorb(state, (key_block, value_block)), None)

    result, unused = lax.scan(
        one_block, start_state, jnp.arange(key_count // block_rows, dtype=jnp.int32)
    )
    output = (result[2] / result[1].T[:, :, None]).astype(jnp.bfloat16)
    return output.reshape(1, row_count, 1, head_count, head_size)


def local_generic(query_rows, key_rows, value_rows):
    ulysses = lax.axis_size("uly")
    tokens = query_rows.shape[1]
    width = query_rows.shape[2]
    heads_local = width // HD // ulysses

    def split_heads(array):
        array = array.reshape(1, tokens, ulysses, heads_local, HD)
        return lax.all_to_all(array, "uly", split_axis=2, concat_axis=1, tiled=True)

    mixed = attend(split_heads(query_rows), split_heads(key_rows), split_heads(value_rows))
    merged = lax.all_to_all(mixed, "uly", split_axis=1, concat_axis=2, tiled=True)
    return merged.reshape(1, tokens, width)


def run_copies(pairs, sems):
    started = [pltpu.make_async_copy(src, dst, sems.at[at]) for at, (src, dst) in enumerate(pairs)]
    for copy in started:
        copy.start()
    for copy in started:
        copy.wait()


def pack_kernel(messages, part, q_ref, k_ref, v_ref, *refs):
    outs, sems = refs[:-1], refs[-1]
    sources = {"q": q_ref, "k": k_ref, "v": v_ref}
    me = lax.axis_index("blk")
    pairs = []
    for (s, pieces), out in zip(messages, outs):
        start = 0
        for name, first, lanes in pieces:
            columns = pl.ds(pl.multiple_of((me ^ s) * part + first, 128), lanes)
            pairs.append((sources[name].at[0, :, columns], out.at[:, pl.ds(start, lanes)]))
            start += lanes
    run_copies(pairs, sems)


def join_kernel(pieces, *refs):
    lanes = refs[-1].shape[2]
    for at, (source, start) in enumerate(pieces):
        refs[-1][at] = refs[source][:, start : start + lanes]


def join(arrays, starts, lanes, effort=0, after=()):
    shape = (len(arrays), arrays[0].shape[0], lanes)
    return pl.pallas_call(
        functools.partial(join_kernel, list(enumerate(starts))),
        out_shape=jax.ShapeDtypeStruct(shape, arrays[0].dtype),
        in_specs=[VMEM] * (len(arrays) + len(after)),
        out_specs=VMEM,
        compiler_params=SMALL,
        cost_estimate=pl.CostEstimate(
            flops=effort, bytes_accessed=4 * math.prod(shape), transcendentals=0
        ),
        name="join",
    )(*arrays, *after)


def hold_kernel(array_ref, until_ref, out_ref):
    pass


def hold(array, until):
    return pl.pallas_call(
        hold_kernel,
        out_shape=jax.ShapeDtypeStruct(array.shape, array.dtype),
        in_specs=[ANY, ANY],
        out_specs=ANY,
        input_output_aliases={0: 0},
        compiler_params=SMALL,
        name="hold",
    )(array, until)


def attend_kernel(plan, *refs):
    blocks = len(plan[0][0])
    ins, out_refs = refs[:-blocks], refs[-blocks:]
    tokens = out_refs[0].shape[0]
    scale = 1.0 / math.sqrt(HD)

    def load(place):
        source, row, first = place
        lanes = slice(first, first + HD)
        return ins[source][:, lanes] if row is None else ins[source][row, :, lanes]

    def rows(places):
        return jnp.concatenate([load(place) for place in places], axis=0)

    scores = [
        lax.dot_general(
            rows(queries), rows(keys), (((1,), (1,)), ((), ())), preferred_element_type=jnp.float32
        )
        * scale
        for queries, keys, values in plan
    ]
    weights = [jnp.exp(s - jnp.max(s, axis=1, keepdims=True)) for s in scores]
    mixed = [
        jnp.dot(w.astype(jnp.bfloat16), rows(values), preferred_element_type=jnp.float32)
        for w, (queries, keys, values) in zip(weights, plan)
    ]
    for head, (w, m) in enumerate(zip(weights, mixed)):
        result = (m / jnp.sum(w, axis=1, keepdims=True)).astype(jnp.bfloat16)
        for block, ref in enumerate(out_refs):
            ref[:, head * HD : (head + 1) * HD] = result[block * tokens : (block + 1) * tokens]


def unpack_kernel(order, part, *refs):
    ins, out_ref, sems = refs[:-2], refs[-2], refs[-1]
    me = lax.axis_index("blk")
    pairs = []
    for s, ref in zip(order, ins):
        columns = pl.ds(pl.multiple_of((me ^ s) * part, 128), part)
        pairs.append((ref, out_ref.at[0, :, columns]))
    run_copies(pairs, sems)


def local_blocks(query_rows, key_rows, value_rows):
    blocks, columns_of = lax.axis_size("blk"), lax.axis_size("uly")
    tokens, width = query_rows.shape[1:]
    part = width // blocks
    heads = part // HD
    kind = query_rows.dtype
    far = list(range(blocks - 1, 1, -1))

    kv, q = (("k", 0, part), ("v", 0, part)), (("q", 0, part),)
    messages = [(s, kv) for s in far] + [(1, kv + q)] + [(s, q) for s in far] + [(0, kv), (0, q)]
    packed = pl.pallas_call(
        functools.partial(pack_kernel, messages, part),
        out_shape=[
            jax.ShapeDtypeStruct((tokens, sum(piece[2] for piece in pieces)), kind)
            for s, pieces in messages
        ],
        in_specs=[HBM] * 3,
        out_specs=[VMEM] * len(messages),
        scratch_shapes=[pltpu.SemaphoreType.DMA((sum(len(m[1]) for m in messages),))],
        compiler_params=SMALL,
        cost_estimate=pl.CostEstimate(
            flops=0, bytes_accessed=6 * tokens * width * 2, transcendentals=0
        ),
        name="pack",
    )(*[pltpu.with_memory_space_constraint(x, pltpu.HBM) for x in (query_rows, key_rows, value_rows)])

    def to_block(array, s):
        return lax.ppermute(array, "blk", [(i, i ^ s) for i in range(blocks)])

    def to_column(array, t):
        return lax.ppermute(array, "uly", [(i, (i + t) % columns_of) for i in range(columns_of)])

    sent = {message: array for message, array in zip(messages, packed)}
    own_kv, own_q = packed[-2:]
    far_kv = [to_block(sent[s, kv], s) for s in far]
    near_kvq = to_block(sent[1, kv + q], 1)
    near_kv = join([own_kv, near_kvq], [0, 0], 2 * part)
    groups = [near_kv, join(far_kv, [0] * len(far), 2 * part)]
    far_q = [to_block(hold(sent[s, q], far_kv[0] if s == far[0] else groups[1]), s) for s in far]
    crossed = [to_column(group, t) for group in groups for t in range(1, columns_of)]
    far_q[0] = join(far_q[:1], [0], part, EFFORT)
    near_q = join([own_q, near_kvq], [0, 2 * part], part, EFFORT, crossed[: columns_of - 1])
    arrays = [near_q] + far_q
    query_places = [(0, 0, 0), (0, 1, 0)]
    query_places += [(1 + far.index(s), 0 if s == far[0] else None, 0) for s in range(2, blocks)]
    key_places = [(len(arrays) + at, None, 0) for at in range(blocks)]
    arrays += [near_kvq, own_kv] + far_kv
    for array in crossed:
        key_places += [(len(arrays), at, 0) for at in range(array.shape[0])]
        arrays.append(array)

    def moved(places, lanes):
        return [(source, row, first + lanes) for source, row, first in places]

    plan = [
        (moved(query_places, lane), moved(key_places, lane), moved(key_places, part + lane))
        for lane in range(0, part, HD)
    ]
    all_tokens = tokens * blocks * columns_of

    pairs = heads * tokens * blocks * all_tokens
    mixed = pl.pallas_call(
        functools.partial(attend_kernel, plan),
        out_shape=[jax.ShapeDtypeStruct((tokens, part), kind)] * blocks,
        in_specs=[VMEM] * len(arrays),
        out_specs=[VMEM] * blocks,
        compiler_params=pltpu.CompilerParams(vmem_limit_bytes=24 * 1024 * 1024),
        cost_estimate=pl.CostEstimate(
            flops=4 * HD * pairs,
            bytes_accessed=4 * part * (all_tokens + tokens * blocks),
            transcendentals=pairs,
        ),
        name="attend",
    )(*arrays)

    order = [0] + far + [1]
    back = [to_block(mixed[s], s) if s else mixed[0] for s in order]
    return pl.pallas_call(
        functools.partial(unpack_kernel, order, part),
        out_shape=jax.ShapeDtypeStruct((1, tokens, width), kind),
        in_specs=[VMEM] * blocks,
        out_specs=HBM,
        scratch_shapes=[pltpu.SemaphoreType.DMA((blocks,))],
        compiler_params=SMALL,
        cost_estimate=pl.CostEstimate(
            flops=0, bytes_accessed=2 * tokens * width * 2, transcendentals=0
        ),
        name="unpack",
    )(*back)


def local(query_rows, key_rows, value_rows):
    blocks = lax.axis_size("blk")
    heads = query_rows.shape[2] // HD
    few = blocks == 4 and heads % blocks == 0
    plan = local_blocks if few else local_generic
    return plan(query_rows, key_rows, value_rows)


def solution(mesh):
    in_specs = (
        P("cfg", ("groups", "blk", "uly"), None),
        P("cfg", ("groups", "blk", "uly"), None),
        P("cfg", ("groups", "blk", "uly"), None),
    )
    out_specs = P("cfg", ("groups", "blk", "uly"), None)
    return jax.shard_map(local, mesh=mesh, in_specs=in_specs, out_specs=out_specs, check_vma=False)
```

```python
import functools
import math

import jax
import jax.numpy as jnp
from jax import lax
from jax.experimental import pallas as pl
from jax.experimental.pallas import tpu as pltpu
from jax.sharding import PartitionSpec as P

HD = 128
EFFORT = 10**9
ANY = pl.BlockSpec(memory_space=pl.ANY)
HBM = pl.BlockSpec(memory_space=pltpu.HBM)
VMEM = pl.BlockSpec(memory_space=pltpu.VMEM)
SMALL = pltpu.CompilerParams(vmem_limit_bytes=4 * 1024 * 1024)


def attend(queries, key_part, value_part):
    query_mat = queries[0, :, 0]
    row_count, head_count, head_size = query_mat.shape
    score_scale = 1.0 / math.sqrt(head_size)
    start_state = (
        jnp.full((head_count, row_count), -1e30, jnp.float32),
        jnp.zeros((head_count, row_count), jnp.float32),
        jnp.zeros((row_count, head_count, head_size), jnp.float32),
    )

    def absorb(state, pieces):
        key_piece = pieces[0][0, :, 0]
        value_piece = pieces[1][0, :, 0]
        scores = (
            jnp.einsum("qhd,khd->hqk", query_mat, key_piece, preferred_element_type=jnp.float32)
            * score_scale
        )
        running, totals, accumulated = state
        new_max = jnp.maximum(running, jnp.max(scores, axis=2))
        weights = jnp.exp(scores - new_max[:, :, None])
        factor = jnp.exp(running - new_max)
        totals = totals * factor + jnp.sum(weights, axis=2)
        probabilities = weights.astype(jnp.bfloat16)
        contrib = jnp.einsum(
            "hqk,khd->qhd", probabilities, value_piece, preferred_element_type=jnp.float32
        )
        accumulated = accumulated * factor.T[:, :, None] + contrib
        return (new_max, totals, accumulated)

    whole_keys, whole_values = (
        lax.all_gather(key_part, "blk", axis=1, tiled=True),
        lax.all_gather(value_part, "blk", axis=1, tiled=True),
    )
    key_count = whole_keys.shape[1]
    block_rows = math.gcd(key_count, 1024)

    def one_block(state, counter):
        offset = counter * block_rows
        key_block = lax.dynamic_slice_in_dim(whole_keys, offset, block_rows, 1)
        value_block = lax.dynamic_slice_in_dim(whole_values, offset, block_rows, 1)
        return (absorb(state, (key_block, value_block)), None)

    result, unused = lax.scan(
        one_block, start_state, jnp.arange(key_count // block_rows, dtype=jnp.int32)
    )
    output = (result[2] / result[1].T[:, :, None]).astype(jnp.bfloat16)
    return output.reshape(1, row_count, 1, head_count, head_size)


def local_generic(query_rows, key_rows, value_rows):
    ulysses = lax.axis_size("uly")
    tokens = query_rows.shape[1]
    width = query_rows.shape[2]
    heads_local = width // HD // ulysses

    def split_heads(array):
        array = array.reshape(1, tokens, ulysses, heads_local, HD)
        return lax.all_to_all(array, "uly", split_axis=2, concat_axis=1, tiled=True)

    mixed = attend(split_heads(query_rows), split_heads(key_rows), split_heads(value_rows))
    merged = lax.all_to_all(mixed, "uly", split_axis=1, concat_axis=2, tiled=True)
    return merged.reshape(1, tokens, width)


def run_copies(pairs, sems):
    started = [pltpu.make_async_copy(src, dst, sems.at[at]) for at, (src, dst) in enumerate(pairs)]
    for copy in started:
        copy.start()
    for copy in started:
        copy.wait()


def pack_kernel(messages, part, q_ref, k_ref, v_ref, *refs):
    outs, sems = refs[:-1], refs[-1]
    sources = {"q": q_ref, "k": k_ref, "v": v_ref}
    me = lax.axis_index("blk")
    pairs = []
    for (s, pieces), out in zip(messages, outs):
        start = 0
        for name, first, lanes in pieces:
            columns = pl.ds(pl.multiple_of((me ^ s) * part + first, 128), lanes)
            pairs.append((sources[name].at[0, :, columns], out.at[:, pl.ds(start, lanes)]))
            start += lanes
    run_copies(pairs, sems)


def join_kernel(pieces, *refs):
    lanes = refs[-1].shape[2]
    for at, (source, start) in enumerate(pieces):
        refs[-1][at] = refs[source][:, start : start + lanes]


def join(arrays, starts, lanes, effort=0, after=()):
    shape = (len(arrays), arrays[0].shape[0], lanes)
    return pl.pallas_call(
        functools.partial(join_kernel, list(enumerate(starts))),
        out_shape=jax.ShapeDtypeStruct(shape, arrays[0].dtype),
        in_specs=[VMEM] * (len(arrays) + len(after)),
        out_specs=VMEM,
        compiler_params=SMALL,
        cost_estimate=pl.CostEstimate(
            flops=effort, bytes_accessed=4 * math.prod(shape), transcendentals=0
        ),
        name="join",
    )(*arrays, *after)


def hold_kernel(*refs):
    pass


def hold(arrays, until=(), effort=0):
    return pl.pallas_call(
        hold_kernel,
        out_shape=[jax.ShapeDtypeStruct(array.shape, array.dtype) for array in arrays],
        in_specs=[ANY] * (len(arrays) + len(until)),
        out_specs=[ANY] * len(arrays),
        input_output_aliases={at: at for at in range(len(arrays))},
        compiler_params=SMALL,
        cost_estimate=pl.CostEstimate(flops=effort, bytes_accessed=0, transcendentals=0),
        name="hold",
    )(*arrays, *until)


def attend_kernel(held, keys, queries, *refs):
    key_refs, query_refs, out_refs = refs[:held], refs[held : -len(queries)], refs[-len(queries) :]
    tokens, part = out_refs[0].shape
    scale = 1.0 / math.sqrt(HD)

    def rows(sources, places, first):
        lanes = slice(first, first + HD)
        pieces = [
            sources[at][:, lanes] if row is None else sources[at][row, :, lanes]
            for at, row in places
        ]
        return jnp.concatenate(pieces, axis=0)

    lanes = range(0, part, HD)
    scores = [
        lax.dot_general(
            rows(query_refs, queries, lane),
            rows(key_refs, keys, lane),
            (((1,), (1,)), ((), ())),
            preferred_element_type=jnp.float32,
        )
        * scale
        for lane in lanes
    ]
    weights = [jnp.exp(s - jnp.max(s, axis=1, keepdims=True)) for s in scores]
    mixed = [
        jnp.dot(
            w.astype(jnp.bfloat16),
            rows(key_refs, keys, part + lane),
            preferred_element_type=jnp.float32,
        )
        for w, lane in zip(weights, lanes)
    ]
    for w, m, lane in zip(weights, mixed, lanes):
        result = (m / jnp.sum(w, axis=1, keepdims=True)).astype(jnp.bfloat16)
        for block, ref in enumerate(out_refs):
            ref[:, lane : lane + HD] = result[block * tokens : (block + 1) * tokens]


def unpack_kernel(order, part, *refs):
    ins, out_ref, sems = refs[:-2], refs[-2], refs[-1]
    me = lax.axis_index("blk")
    pairs = []
    for s, ref in zip(order, ins):
        columns = pl.ds(pl.multiple_of((me ^ s) * part, 128), part)
        pairs.append((ref, out_ref.at[0, :, columns]))
    run_copies(pairs, sems)


def local_blocks(query_rows, key_rows, value_rows):
    blocks, columns_of = lax.axis_size("blk"), lax.axis_size("uly")
    tokens, width = query_rows.shape[1:]
    part = width // blocks
    heads = part // HD
    kind = query_rows.dtype
    far = list(range(blocks - 1, 1, -1))

    kv, q = (("k", 0, part), ("v", 0, part)), (("q", 0, part),)
    messages = [(s, kv) for s in far] + [(1, kv + q)] + [(s, q) for s in far] + [(0, kv), (0, q)]
    packed = pl.pallas_call(
        functools.partial(pack_kernel, messages, part),
        out_shape=[
            jax.ShapeDtypeStruct((tokens, sum(piece[2] for piece in pieces)), kind)
            for s, pieces in messages
        ],
        in_specs=[HBM] * 3,
        out_specs=[VMEM] * len(messages),
        scratch_shapes=[pltpu.SemaphoreType.DMA((sum(len(m[1]) for m in messages),))],
        compiler_params=SMALL,
        cost_estimate=pl.CostEstimate(
            flops=0, bytes_accessed=6 * tokens * width * 2, transcendentals=0
        ),
        name="pack",
    )(*[pltpu.with_memory_space_constraint(x, pltpu.HBM) for x in (query_rows, key_rows, value_rows)])

    def to_block(array, s):
        return lax.ppermute(array, "blk", [(i, i ^ s) for i in range(blocks)])

    def to_column(array, t):
        return lax.ppermute(array, "uly", [(i, (i + t) % columns_of) for i in range(columns_of)])

    sent = {message: array for message, array in zip(messages, packed)}
    own_kv, own_q = packed[-2:]
    far_kv = [to_block(sent[s, kv], s) for s in far]
    near_kvq = to_block(sent[1, kv + q], 1)
    near_kv = join([own_kv, near_kvq], [0, 0], 2 * part)
    groups = [near_kv, join(far_kv, [0] * len(far), 2 * part)]
    far_q = [to_block(hold([sent[s, q]], [far_kv[0] if s == far[0] else groups[1]])[0], s) for s in far]
    crossed = [to_column(group, t) for group in groups for t in range(1, columns_of)]
    far_q[0] = join(far_q[:1], [0], part, EFFORT)
    near_q = join([own_q, near_kvq], [0, 2 * part], part, EFFORT, crossed[: columns_of - 1])

    holders = [near_kvq, own_kv] + far_kv
    keys = [(at, None) for at in range(len(holders))]
    for array in crossed:
        keys += [(len(holders), at) for at in range(array.shape[0])]
        holders.append(array)

    def attend(query_arrays, query_places):
        rows = tokens * len(query_places)
        pairs = heads * rows * tokens * len(keys)
        return pl.pallas_call(
            functools.partial(attend_kernel, len(holders), keys, query_places),
            out_shape=[jax.ShapeDtypeStruct((tokens, part), kind)] * len(query_places),
            in_specs=[VMEM] * (len(holders) + len(query_arrays)),
            out_specs=[VMEM] * len(query_places),
            compiler_params=pltpu.CompilerParams(vmem_limit_bytes=24 * 1024 * 1024),
            cost_estimate=pl.CostEstimate(
                flops=4 * HD * pairs,
                bytes_accessed=4 * part * (rows + tokens * len(keys)),
                transcendentals=pairs,
            ),
            name="attend",
        )(*holders, *query_arrays)

    mixed = dict(zip([0, 1] + far[:-1], attend([near_q] + far_q[:-1], [(0, 0), (0, 1), (1, 0)])))
    last_q = hold([far_q[-1]], [mixed[0]])
    mixed[far[-1]] = attend(last_q, [(0, None)])[0]
    back = {s: to_block(mixed[s], s) for s in far + [1]}
    early = [1] + far[:-1]
    back.update(zip(early, hold([back[s] for s in early], effort=EFFORT)))
    back[0] = mixed[0]
    order = [0] + far + [1]
    back = [back[s] for s in order]
    return pl.pallas_call(
        functools.partial(unpack_kernel, order, part),
        out_shape=jax.ShapeDtypeStruct((1, tokens, width), kind),
        in_specs=[VMEM] * blocks,
        out_specs=HBM,
        scratch_shapes=[pltpu.SemaphoreType.DMA((blocks,))],
        compiler_params=SMALL,
        cost_estimate=pl.CostEstimate(
            flops=0, bytes_accessed=2 * tokens * width * 2, transcendentals=0
        ),
        name="unpack",
    )(*back)


def local(query_rows, key_rows, value_rows):
    blocks = lax.axis_size("blk")
    heads = query_rows.shape[2] // HD
    few = blocks == 4 and heads % blocks == 0
    plan = local_blocks if few else local_generic
    return plan(query_rows, key_rows, value_rows)


def solution(mesh):
    in_specs = (
        P("cfg", ("groups", "blk", "uly"), None),
        P("cfg", ("groups", "blk", "uly"), None),
        P("cfg", ("groups", "blk", "uly"), None),
    )
    out_specs = P("cfg", ("groups", "blk", "uly"), None)
    return jax.shard_map(local, mesh=mesh, in_specs=in_specs, out_specs=out_specs, check_vma=False)
```

```python
import functools
import math

import jax
import jax.numpy as jnp
from jax import lax
from jax.experimental import pallas as pl
from jax.experimental.pallas import tpu as pltpu
from jax.sharding import PartitionSpec as P

HD = 128
EFFORT = 15 * 10**8
ANY = pl.BlockSpec(memory_space=pl.ANY)
HBM = pl.BlockSpec(memory_space=pltpu.HBM)
VMEM = pl.BlockSpec(memory_space=pltpu.VMEM)
SMALL = pltpu.CompilerParams(vmem_limit_bytes=4 * 1024 * 1024)


def attend(queries, key_part, value_part):
    query_mat = queries[0, :, 0]
    row_count, head_count, head_size = query_mat.shape
    score_scale = 1.0 / math.sqrt(head_size)
    start_state = (
        jnp.full((head_count, row_count), -1e30, jnp.float32),
        jnp.zeros((head_count, row_count), jnp.float32),
        jnp.zeros((row_count, head_count, head_size), jnp.float32),
    )

    def absorb(state, pieces):
        key_piece = pieces[0][0, :, 0]
        value_piece = pieces[1][0, :, 0]
        scores = (
            jnp.einsum("qhd,khd->hqk", query_mat, key_piece, preferred_element_type=jnp.float32)
            * score_scale
        )
        running, totals, accumulated = state
        new_max = jnp.maximum(running, jnp.max(scores, axis=2))
        weights = jnp.exp(scores - new_max[:, :, None])
        factor = jnp.exp(running - new_max)
        totals = totals * factor + jnp.sum(weights, axis=2)
        probabilities = weights.astype(jnp.bfloat16)
        contrib = jnp.einsum(
            "hqk,khd->qhd", probabilities, value_piece, preferred_element_type=jnp.float32
        )
        accumulated = accumulated * factor.T[:, :, None] + contrib
        return (new_max, totals, accumulated)

    whole_keys, whole_values = (
        lax.all_gather(key_part, "blk", axis=1, tiled=True),
        lax.all_gather(value_part, "blk", axis=1, tiled=True),
    )
    key_count = whole_keys.shape[1]
    block_rows = math.gcd(key_count, 1024)

    def one_block(state, counter):
        offset = counter * block_rows
        key_block = lax.dynamic_slice_in_dim(whole_keys, offset, block_rows, 1)
        value_block = lax.dynamic_slice_in_dim(whole_values, offset, block_rows, 1)
        return (absorb(state, (key_block, value_block)), None)

    result, unused = lax.scan(
        one_block, start_state, jnp.arange(key_count // block_rows, dtype=jnp.int32)
    )
    output = (result[2] / result[1].T[:, :, None]).astype(jnp.bfloat16)
    return output.reshape(1, row_count, 1, head_count, head_size)


def local_generic(query_rows, key_rows, value_rows):
    ulysses = lax.axis_size("uly")
    tokens = query_rows.shape[1]
    width = query_rows.shape[2]
    heads_local = width // HD // ulysses

    def split_heads(array):
        array = array.reshape(1, tokens, ulysses, heads_local, HD)
        return lax.all_to_all(array, "uly", split_axis=2, concat_axis=1, tiled=True)

    mixed = attend(split_heads(query_rows), split_heads(key_rows), split_heads(value_rows))
    merged = lax.all_to_all(mixed, "uly", split_axis=1, concat_axis=2, tiled=True)
    return merged.reshape(1, tokens, width)


def run_copies(pairs, sems):
    started = [pltpu.make_async_copy(src, dst, sems.at[at]) for at, (src, dst) in enumerate(pairs)]
    for copy in started:
        copy.start()
    for copy in started:
        copy.wait()


def pack_kernel(messages, part, q_ref, k_ref, v_ref, *refs):
    outs, sems = refs[:-1], refs[-1]
    sources = {"q": q_ref, "k": k_ref, "v": v_ref}
    me = lax.axis_index("blk")
    pairs = []
    for (s, pieces), out in zip(messages, outs):
        start = 0
        for name, first, lanes in pieces:
            columns = pl.ds(pl.multiple_of((me ^ s) * part + first, 128), lanes)
            pairs.append((sources[name].at[0, :, columns], out.at[:, pl.ds(start, lanes)]))
            start += lanes
    run_copies(pairs, sems)


def join_kernel(pieces, *refs):
    lanes = refs[-1].shape[2]
    for at, (source, start) in enumerate(pieces):
        refs[-1][at] = refs[source][:, start : start + lanes]


def join(arrays, starts, lanes, effort=0, after=()):
    shape = (len(arrays), arrays[0].shape[0], lanes)
    return pl.pallas_call(
        functools.partial(join_kernel, list(enumerate(starts))),
        out_shape=jax.ShapeDtypeStruct(shape, arrays[0].dtype),
        in_specs=[VMEM] * (len(arrays) + len(after)),
        out_specs=VMEM,
        compiler_params=SMALL,
        cost_estimate=pl.CostEstimate(
            flops=effort, bytes_accessed=4 * math.prod(shape), transcendentals=0
        ),
        name="join",
    )(*arrays, *after)


def hold_kernel(*refs):
    pass


def hold(arrays, until=(), effort=0):
    return pl.pallas_call(
        hold_kernel,
        out_shape=[jax.ShapeDtypeStruct(array.shape, array.dtype) for array in arrays],
        in_specs=[ANY] * (len(arrays) + len(until)),
        out_specs=[ANY] * len(arrays),
        input_output_aliases={at: at for at in range(len(arrays))},
        compiler_params=SMALL,
        cost_estimate=pl.CostEstimate(flops=effort, bytes_accessed=0, transcendentals=0),
        name="hold",
    )(*arrays, *until)


def attend_kernel(held, keys, queries, *refs):
    key_refs, query_refs, out_refs = refs[:held], refs[held : -len(queries)], refs[-len(queries) :]
    tokens, part = out_refs[0].shape
    scale = 1.0 / math.sqrt(HD)

    def rows(sources, places, first):
        lanes = slice(first, first + HD)
        pieces = [
            sources[at][:, lanes] if row is None else sources[at][row, :, lanes]
            for at, row in places
        ]
        return jnp.concatenate(pieces, axis=0)

    lanes = range(0, part, HD)
    scores = [
        lax.dot_general(
            rows(query_refs, queries, lane),
            rows(key_refs, keys, lane),
            (((1,), (1,)), ((), ())),
            preferred_element_type=jnp.float32,
        )
        * scale
        for lane in lanes
    ]
    weights = [jnp.exp(s - jnp.max(s, axis=1, keepdims=True)) for s in scores]
    mixed = [
        jnp.dot(
            w.astype(jnp.bfloat16),
            rows(key_refs, keys, part + lane),
            preferred_element_type=jnp.float32,
        )
        for w, lane in zip(weights, lanes)
    ]
    for w, m, lane in zip(weights, mixed, lanes):
        result = (m / jnp.sum(w, axis=1, keepdims=True)).astype(jnp.bfloat16)
        for block, ref in enumerate(out_refs):
            ref[:, lane : lane + HD] = result[block * tokens : (block + 1) * tokens]


def unpack_kernel(order, part, *refs):
    ins, out_ref, sems = refs[:-2], refs[-2], refs[-1]
    me = lax.axis_index("blk")
    pairs = []
    for s, ref in zip(order, ins):
        columns = pl.ds(pl.multiple_of((me ^ s) * part, 128), part)
        pairs.append((ref, out_ref.at[0, :, columns]))
    run_copies(pairs, sems)


def local_blocks(query_rows, key_rows, value_rows):
    blocks, columns_of = lax.axis_size("blk"), lax.axis_size("uly")
    tokens, width = query_rows.shape[1:]
    part = width // blocks
    heads = part // HD
    kind = query_rows.dtype
    far = list(range(blocks - 1, 1, -1))

    kv, q = (("k", 0, part), ("v", 0, part)), (("q", 0, part),)
    messages = [(s, kv) for s in far] + [(1, kv + q)] + [(s, q) for s in far] + [(0, kv), (0, q)]
    packed = pl.pallas_call(
        functools.partial(pack_kernel, messages, part),
        out_shape=[
            jax.ShapeDtypeStruct((tokens, sum(piece[2] for piece in pieces)), kind)
            for s, pieces in messages
        ],
        in_specs=[HBM] * 3,
        out_specs=[VMEM] * len(messages),
        scratch_shapes=[pltpu.SemaphoreType.DMA((sum(len(m[1]) for m in messages),))],
        compiler_params=SMALL,
        cost_estimate=pl.CostEstimate(
            flops=0, bytes_accessed=6 * tokens * width * 2, transcendentals=0
        ),
        name="pack",
    )(*[pltpu.with_memory_space_constraint(x, pltpu.HBM) for x in (query_rows, key_rows, value_rows)])

    def to_block(array, s):
        return lax.ppermute(array, "blk", [(i, i ^ s) for i in range(blocks)])

    def to_column(array, t):
        return lax.ppermute(array, "uly", [(i, (i + t) % columns_of) for i in range(columns_of)])

    sent = {message: array for message, array in zip(messages, packed)}
    own_kv, own_q = packed[-2:]
    far_kv = [to_block(sent[s, kv], s) for s in far]
    near_kvq = to_block(sent[1, kv + q], 1)
    near_kv = join([own_kv, near_kvq], [0, 0], 2 * part)
    groups = [near_kv] + [join([array], [0], 2 * part) for array in far_kv]
    far_q = [to_block(hold([sent[s, q]], [group])[0], s) for s, group in zip(far, groups[1:])]
    crossed = [to_column(group, t) for group in groups for t in range(1, columns_of)]
    far_q[0] = join(far_q[:1], [0], part, EFFORT)
    near_q = join([own_q, near_kvq], [0, 2 * part], part, EFFORT, crossed[: columns_of - 1])

    holders = [near_kvq, own_kv] + far_kv
    keys = [(at, None) for at in range(len(holders))]
    for array in crossed:
        keys += [(len(holders), at) for at in range(array.shape[0])]
        holders.append(array)

    def attend(query_arrays, query_places):
        rows = tokens * len(query_places)
        pairs = heads * rows * tokens * len(keys)
        return pl.pallas_call(
            functools.partial(attend_kernel, len(holders), keys, query_places),
            out_shape=[jax.ShapeDtypeStruct((tokens, part), kind)] * len(query_places),
            in_specs=[VMEM] * (len(holders) + len(query_arrays)),
            out_specs=[VMEM] * len(query_places),
            compiler_params=pltpu.CompilerParams(vmem_limit_bytes=24 * 1024 * 1024),
            cost_estimate=pl.CostEstimate(
                flops=4 * HD * pairs,
                bytes_accessed=4 * part * (rows + tokens * len(keys)),
                transcendentals=pairs,
            ),
            name="attend",
        )(*holders, *query_arrays)

    mixed = dict(zip([0, 1] + far[:-1], attend([near_q] + far_q[:-1], [(0, 0), (0, 1), (1, 0)])))
    last_q = hold([far_q[-1]], [mixed[0]])
    mixed[far[-1]] = attend(last_q, [(0, None)])[0]
    mixed[1] = hold([mixed[1]], [mixed[far[-1]]])[0]
    back = {s: to_block(mixed[s], s) for s in far + [1]}
    early = far[:-1]
    back.update(zip(early, hold([back[s] for s in early], effort=EFFORT)))
    back[0] = mixed[0]
    order = [0] + far + [1]
    back = [back[s] for s in order]
    return pl.pallas_call(
        functools.partial(unpack_kernel, order, part),
        out_shape=jax.ShapeDtypeStruct((1, tokens, width), kind),
        in_specs=[VMEM] * blocks,
        out_specs=HBM,
        scratch_shapes=[pltpu.SemaphoreType.DMA((blocks,))],
        compiler_params=SMALL,
        cost_estimate=pl.CostEstimate(
            flops=0, bytes_accessed=2 * tokens * width * 2, transcendentals=0
        ),
        name="unpack",
    )(*back)


def local(query_rows, key_rows, value_rows):
    blocks = lax.axis_size("blk")
    heads = query_rows.shape[2] // HD
    few = blocks == 4 and heads % blocks == 0
    plan = local_blocks if few else local_generic
    return plan(query_rows, key_rows, value_rows)


def solution(mesh):
    in_specs = (
        P("cfg", ("groups", "blk", "uly"), None),
        P("cfg", ("groups", "blk", "uly"), None),
        P("cfg", ("groups", "blk", "uly"), None),
    )
    out_specs = P("cfg", ("groups", "blk", "uly"), None)
    return jax.shard_map(local, mesh=mesh, in_specs=in_specs, out_specs=out_specs, check_vma=False)
```

```python
import functools
import math

import jax
import jax.numpy as jnp
from jax import lax
from jax.experimental import pallas as pl
from jax.experimental.pallas import tpu as pltpu
from jax.sharding import PartitionSpec as P

HD = 128
EFFORT = 10**9
EFFORT_OWN = 3 * 10**8
EFFORT_FIRST = 10**9
EFFORT_SECOND = 2 * 10**9
ANY = pl.BlockSpec(memory_space=pl.ANY)
HBM = pl.BlockSpec(memory_space=pltpu.HBM)
VMEM = pl.BlockSpec(memory_space=pltpu.VMEM)
SMALL = pltpu.CompilerParams(vmem_limit_bytes=4 * 1024 * 1024)


def attend(queries, key_part, value_part):
    query_mat = queries[0, :, 0]
    row_count, head_count, head_size = query_mat.shape
    score_scale = 1.0 / math.sqrt(head_size)
    start_state = (
        jnp.full((head_count, row_count), -1e30, jnp.float32),
        jnp.zeros((head_count, row_count), jnp.float32),
        jnp.zeros((row_count, head_count, head_size), jnp.float32),
    )

    def absorb(state, pieces):
        key_piece = pieces[0][0, :, 0]
        value_piece = pieces[1][0, :, 0]
        scores = (
            jnp.einsum("qhd,khd->hqk", query_mat, key_piece, preferred_element_type=jnp.float32)
            * score_scale
        )
        running, totals, accumulated = state
        new_max = jnp.maximum(running, jnp.max(scores, axis=2))
        weights = jnp.exp(scores - new_max[:, :, None])
        factor = jnp.exp(running - new_max)
        totals = totals * factor + jnp.sum(weights, axis=2)
        probabilities = weights.astype(jnp.bfloat16)
        contrib = jnp.einsum(
            "hqk,khd->qhd", probabilities, value_piece, preferred_element_type=jnp.float32
        )
        accumulated = accumulated * factor.T[:, :, None] + contrib
        return (new_max, totals, accumulated)

    whole_keys, whole_values = (
        lax.all_gather(key_part, "blk", axis=1, tiled=True),
        lax.all_gather(value_part, "blk", axis=1, tiled=True),
    )
    key_count = whole_keys.shape[1]
    block_rows = math.gcd(key_count, 1024)

    def one_block(state, counter):
        offset = counter * block_rows
        key_block = lax.dynamic_slice_in_dim(whole_keys, offset, block_rows, 1)
        value_block = lax.dynamic_slice_in_dim(whole_values, offset, block_rows, 1)
        return (absorb(state, (key_block, value_block)), None)

    result, unused = lax.scan(
        one_block, start_state, jnp.arange(key_count // block_rows, dtype=jnp.int32)
    )
    output = (result[2] / result[1].T[:, :, None]).astype(jnp.bfloat16)
    return output.reshape(1, row_count, 1, head_count, head_size)


def local_generic(query_rows, key_rows, value_rows):
    ulysses = lax.axis_size("uly")
    tokens = query_rows.shape[1]
    width = query_rows.shape[2]
    heads_local = width // HD // ulysses

    def split_heads(array):
        array = array.reshape(1, tokens, ulysses, heads_local, HD)
        return lax.all_to_all(array, "uly", split_axis=2, concat_axis=1, tiled=True)

    mixed = attend(split_heads(query_rows), split_heads(key_rows), split_heads(value_rows))
    merged = lax.all_to_all(mixed, "uly", split_axis=1, concat_axis=2, tiled=True)
    return merged.reshape(1, tokens, width)


def run_copies(pairs, sems):
    started = [pltpu.make_async_copy(src, dst, sems.at[at]) for at, (src, dst) in enumerate(pairs)]
    for copy in started:
        copy.start()
    for copy in started:
        copy.wait()


def pack_kernel(messages, part, q_ref, k_ref, v_ref, *refs):
    outs, sems = refs[:-1], refs[-1]
    sources = {"q": q_ref, "k": k_ref, "v": v_ref}
    me = lax.axis_index("blk")
    pairs = []
    for (s, pieces), out in zip(messages, outs):
        start = 0
        for name, first, lanes in pieces:
            columns = pl.ds(pl.multiple_of((me ^ s) * part + first, 128), lanes)
            pairs.append((sources[name].at[0, :, columns], out.at[:, pl.ds(start, lanes)]))
            start += lanes
    run_copies(pairs, sems)


def join_kernel(pieces, *refs):
    lanes = refs[-1].shape[2]
    for at, (source, start) in enumerate(pieces):
        refs[-1][at] = refs[source][:, start : start + lanes]


def join(arrays, starts, lanes, effort=0, after=()):
    shape = (len(arrays), arrays[0].shape[0], lanes)
    return pl.pallas_call(
        functools.partial(join_kernel, list(enumerate(starts))),
        out_shape=jax.ShapeDtypeStruct(shape, arrays[0].dtype),
        in_specs=[VMEM] * (len(arrays) + len(after)),
        out_specs=VMEM,
        compiler_params=SMALL,
        cost_estimate=pl.CostEstimate(
            flops=effort, bytes_accessed=4 * math.prod(shape), transcendentals=0
        ),
        name="join",
    )(*arrays, *after)


def hold_kernel(*refs):
    pass


def hold(arrays, until=(), effort=0):
    return pl.pallas_call(
        hold_kernel,
        out_shape=[jax.ShapeDtypeStruct(array.shape, array.dtype) for array in arrays],
        in_specs=[ANY] * (len(arrays) + len(until)),
        out_specs=[ANY] * len(arrays),
        input_output_aliases={at: at for at in range(len(arrays))},
        compiler_params=SMALL,
        cost_estimate=pl.CostEstimate(flops=effort, bytes_accessed=0, transcendentals=0),
        name="hold",
    )(*arrays, *until)


def attend_kernel(held, keys, queries, *refs):
    key_refs, query_refs, out_refs = refs[:held], refs[held : -len(queries)], refs[-len(queries) :]
    tokens, part = out_refs[0].shape
    scale = 1.0 / math.sqrt(HD)

    def rows(sources, places, first):
        lanes = slice(first, first + HD)
        pieces = [
            sources[at][:, lanes] if row is None else sources[at][row, :, lanes]
            for at, row in places
        ]
        return jnp.concatenate(pieces, axis=0)

    lanes = range(0, part, HD)
    scores = [
        lax.dot_general(
            rows(query_refs, queries, lane),
            rows(key_refs, keys, lane),
            (((1,), (1,)), ((), ())),
            preferred_element_type=jnp.float32,
        )
        * scale
        for lane in lanes
    ]
    weights = [jnp.exp(s - jnp.max(s, axis=1, keepdims=True)) for s in scores]
    mixed = [
        jnp.dot(
            w.astype(jnp.bfloat16),
            rows(key_refs, keys, part + lane),
            preferred_element_type=jnp.float32,
        )
        for w, lane in zip(weights, lanes)
    ]
    for w, m, lane in zip(weights, mixed, lanes):
        result = (m / jnp.sum(w, axis=1, keepdims=True)).astype(jnp.bfloat16)
        for block, ref in enumerate(out_refs):
            ref[:, lane : lane + HD] = result[block * tokens : (block + 1) * tokens]


def unpack_kernel(order, part, *refs):
    ins, out_ref, sems = refs[:-2], refs[-2], refs[-1]
    me = lax.axis_index("blk")
    pairs = []
    for s, ref in zip(order, ins):
        columns = pl.ds(pl.multiple_of((me ^ s) * part, 128), part)
        pairs.append((ref, out_ref.at[0, :, columns]))
    run_copies(pairs, sems)


def local_blocks(query_rows, key_rows, value_rows):
    blocks, columns_of = lax.axis_size("blk"), lax.axis_size("uly")
    tokens, width = query_rows.shape[1:]
    part = width // blocks
    heads = part // HD
    kind = query_rows.dtype
    far = list(range(blocks - 1, 1, -1))

    kv, q = (("k", 0, part), ("v", 0, part)), (("q", 0, part),)
    messages = [(s, kv) for s in far] + [(1, kv + q)] + [(s, q) for s in far] + [(0, kv), (0, q)]
    packed = pl.pallas_call(
        functools.partial(pack_kernel, messages, part),
        out_shape=[
            jax.ShapeDtypeStruct((tokens, sum(piece[2] for piece in pieces)), kind)
            for s, pieces in messages
        ],
        in_specs=[HBM] * 3,
        out_specs=[VMEM] * len(messages),
        scratch_shapes=[pltpu.SemaphoreType.DMA((sum(len(m[1]) for m in messages),))],
        compiler_params=SMALL,
        cost_estimate=pl.CostEstimate(
            flops=0, bytes_accessed=6 * tokens * width * 2, transcendentals=0
        ),
        name="pack",
    )(*[pltpu.with_memory_space_constraint(x, pltpu.HBM) for x in (query_rows, key_rows, value_rows)])

    def to_block(array, s):
        return lax.ppermute(array, "blk", [(i, i ^ s) for i in range(blocks)])

    def to_column(array, t):
        return lax.ppermute(array, "uly", [(i, (i + t) % columns_of) for i in range(columns_of)])

    sent = {message: array for message, array in zip(messages, packed)}
    own_kv, own_q = packed[-2:]
    far_kv = [to_block(sent[s, kv], s) for s in far]
    near_kvq = to_block(sent[1, kv + q], 1)
    far_kv[0] = hold(far_kv[:1], effort=EFFORT_FIRST)[0]
    far_kv[1] = hold(far_kv[1:], effort=EFFORT_SECOND)[0]
    groups = [own_kv, join([near_kvq, far_kv[0]], [0, 0], 2 * part)] + far_kv[1:]
    far_q = [to_block(hold([sent[s, q]], [group])[0], s) for s, group in zip(far, groups[1:])]
    hops = columns_of - 1
    crossed = [to_column(group, t) for group in groups for t in range(1, columns_of)]
    crossed[:hops] = hold(crossed[:hops], effort=EFFORT_OWN)
    near_q = join([own_q, near_kvq], [0, 2 * part], part)
    far_q[0] = join(far_q[:1], [0], part, EFFORT, crossed[: 2 * hops])

    holders = [near_kvq, own_kv] + far_kv + crossed
    keys = []
    for at, array in enumerate(holders):
        keys += [(at, None)] if array.ndim == 2 else [(at, row) for row in range(array.shape[0])]

    def attend(query_arrays, query_places):
        rows = tokens * len(query_places)
        pairs = heads * rows * tokens * len(keys)
        return pl.pallas_call(
            functools.partial(attend_kernel, len(holders), keys, query_places),
            out_shape=[jax.ShapeDtypeStruct((tokens, part), kind)] * len(query_places),
            in_specs=[VMEM] * (len(holders) + len(query_arrays)),
            out_specs=[VMEM] * len(query_places),
            compiler_params=pltpu.CompilerParams(vmem_limit_bytes=24 * 1024 * 1024),
            cost_estimate=pl.CostEstimate(
                flops=4 * HD * pairs,
                bytes_accessed=4 * part * (rows + tokens * len(keys)),
                transcendentals=pairs,
            ),
            name="attend",
        )(*holders, *query_arrays)

    mixed = dict(zip([0, 1] + far[:-1], attend([near_q] + far_q[:-1], [(0, 0), (0, 1), (1, 0)])))
    last_q = hold([far_q[-1]], [mixed[0]])
    mixed[far[-1]] = attend(last_q, [(0, None)])[0]
    mixed[1] = hold([mixed[1]], [mixed[far[-1]]])[0]
    back = {s: to_block(mixed[s], s) for s in far + [1]}
    early = far[:-1]
    back.update(zip(early, hold([back[s] for s in early], effort=EFFORT)))
    back[0] = mixed[0]
    order = [0] + far + [1]
    back = [back[s] for s in order]
    return pl.pallas_call(
        functools.partial(unpack_kernel, order, part),
        out_shape=jax.ShapeDtypeStruct((1, tokens, width), kind),
        in_specs=[VMEM] * blocks,
        out_specs=HBM,
        scratch_shapes=[pltpu.SemaphoreType.DMA((blocks,))],
        compiler_params=SMALL,
        cost_estimate=pl.CostEstimate(
            flops=0, bytes_accessed=2 * tokens * width * 2, transcendentals=0
        ),
        name="unpack",
    )(*back)


def local(query_rows, key_rows, value_rows):
    blocks = lax.axis_size("blk")
    heads = query_rows.shape[2] // HD
    few = blocks == 4 and heads % blocks == 0
    plan = local_blocks if few else local_generic
    return plan(query_rows, key_rows, value_rows)


def solution(mesh):
    in_specs = (
        P("cfg", ("groups", "blk", "uly"), None),
        P("cfg", ("groups", "blk", "uly"), None),
        P("cfg", ("groups", "blk", "uly"), None),
    )
    out_specs = P("cfg", ("groups", "blk", "uly"), None)
    return jax.shard_map(local, mesh=mesh, in_specs=in_specs, out_specs=out_specs, check_vma=False)
```

```python
import functools
import math

import jax
import jax.numpy as jnp
from jax import lax
from jax.experimental import pallas as pl
from jax.experimental.pallas import tpu as pltpu
from jax.sharding import PartitionSpec as P

HD = 128
EFFORT = 10**9
EFFORT_OWN = 3 * 10**8
EFFORT_NEAR = 0
EFFORT_FAR = (10**9, 2 * 10**9)
ANY = pl.BlockSpec(memory_space=pl.ANY)
HBM = pl.BlockSpec(memory_space=pltpu.HBM)
VMEM = pl.BlockSpec(memory_space=pltpu.VMEM)
SMALL = pltpu.CompilerParams(vmem_limit_bytes=4 * 1024 * 1024)


def attend(queries, key_part, value_part):
    query_mat = queries[0, :, 0]
    row_count, head_count, head_size = query_mat.shape
    score_scale = 1.0 / math.sqrt(head_size)
    start_state = (
        jnp.full((head_count, row_count), -1e30, jnp.float32),
        jnp.zeros((head_count, row_count), jnp.float32),
        jnp.zeros((row_count, head_count, head_size), jnp.float32),
    )

    def absorb(state, pieces):
        key_piece = pieces[0][0, :, 0]
        value_piece = pieces[1][0, :, 0]
        scores = (
            jnp.einsum("qhd,khd->hqk", query_mat, key_piece, preferred_element_type=jnp.float32)
            * score_scale
        )
        running, totals, accumulated = state
        new_max = jnp.maximum(running, jnp.max(scores, axis=2))
        weights = jnp.exp(scores - new_max[:, :, None])
        factor = jnp.exp(running - new_max)
        totals = totals * factor + jnp.sum(weights, axis=2)
        probabilities = weights.astype(jnp.bfloat16)
        contrib = jnp.einsum(
            "hqk,khd->qhd", probabilities, value_piece, preferred_element_type=jnp.float32
        )
        accumulated = accumulated * factor.T[:, :, None] + contrib
        return (new_max, totals, accumulated)

    whole_keys, whole_values = (
        lax.all_gather(key_part, "blk", axis=1, tiled=True),
        lax.all_gather(value_part, "blk", axis=1, tiled=True),
    )
    key_count = whole_keys.shape[1]
    block_rows = math.gcd(key_count, 1024)

    def one_block(state, counter):
        offset = counter * block_rows
        key_block = lax.dynamic_slice_in_dim(whole_keys, offset, block_rows, 1)
        value_block = lax.dynamic_slice_in_dim(whole_values, offset, block_rows, 1)
        return (absorb(state, (key_block, value_block)), None)

    result, unused = lax.scan(
        one_block, start_state, jnp.arange(key_count // block_rows, dtype=jnp.int32)
    )
    output = (result[2] / result[1].T[:, :, None]).astype(jnp.bfloat16)
    return output.reshape(1, row_count, 1, head_count, head_size)


def local_generic(query_rows, key_rows, value_rows):
    ulysses = lax.axis_size("uly")
    tokens = query_rows.shape[1]
    width = query_rows.shape[2]
    heads_local = width // HD // ulysses

    def split_heads(array):
        array = array.reshape(1, tokens, ulysses, heads_local, HD)
        return lax.all_to_all(array, "uly", split_axis=2, concat_axis=1, tiled=True)

    mixed = attend(split_heads(query_rows), split_heads(key_rows), split_heads(value_rows))
    merged = lax.all_to_all(mixed, "uly", split_axis=1, concat_axis=2, tiled=True)
    return merged.reshape(1, tokens, width)


def run_copies(pairs, sems):
    started = [pltpu.make_async_copy(src, dst, sems.at[at]) for at, (src, dst) in enumerate(pairs)]
    for copy in started:
        copy.start()
    for copy in started:
        copy.wait()


def pack_kernel(messages, part, q_ref, k_ref, v_ref, *refs):
    outs, sems = refs[:-1], refs[-1]
    sources = {"q": q_ref, "k": k_ref, "v": v_ref}
    me = lax.axis_index("blk")
    pairs = []
    for (s, pieces), out in zip(messages, outs):
        start = 0
        for name, first, lanes in pieces:
            columns = pl.ds(pl.multiple_of((me ^ s) * part + first, 128), lanes)
            pairs.append((sources[name].at[0, :, columns], out.at[:, pl.ds(start, lanes)]))
            start += lanes
    run_copies(pairs, sems)


def join_kernel(pieces, *refs):
    lanes = refs[-1].shape[2]
    for at, (source, start) in enumerate(pieces):
        refs[-1][at] = refs[source][:, start : start + lanes]


def join(arrays, starts, lanes, effort=0, after=()):
    shape = (len(arrays), arrays[0].shape[0], lanes)
    return pl.pallas_call(
        functools.partial(join_kernel, list(enumerate(starts))),
        out_shape=jax.ShapeDtypeStruct(shape, arrays[0].dtype),
        in_specs=[VMEM] * (len(arrays) + len(after)),
        out_specs=VMEM,
        compiler_params=SMALL,
        cost_estimate=pl.CostEstimate(
            flops=effort, bytes_accessed=4 * math.prod(shape), transcendentals=0
        ),
        name="join",
    )(*arrays, *after)


def hold_kernel(*refs):
    pass


def hold(arrays, until=(), effort=0):
    return pl.pallas_call(
        hold_kernel,
        out_shape=[jax.ShapeDtypeStruct(array.shape, array.dtype) for array in arrays],
        in_specs=[ANY] * (len(arrays) + len(until)),
        out_specs=[ANY] * len(arrays),
        input_output_aliases={at: at for at in range(len(arrays))},
        compiler_params=SMALL,
        cost_estimate=pl.CostEstimate(flops=effort, bytes_accessed=0, transcendentals=0),
        name="hold",
    )(*arrays, *until)


def attend_kernel(held, keys, queries, *refs):
    key_refs, query_refs, out_refs = refs[:held], refs[held : -len(queries)], refs[-len(queries) :]
    tokens, part = out_refs[0].shape
    scale = 1.0 / math.sqrt(HD)

    def rows(sources, places, first):
        lanes = slice(first, first + HD)
        pieces = [
            sources[at][:, lanes] if row is None else sources[at][row, :, lanes]
            for at, row in places
        ]
        return jnp.concatenate(pieces, axis=0)

    lanes = range(0, part, HD)
    scores = [
        lax.dot_general(
            rows(query_refs, queries, lane),
            rows(key_refs, keys, lane),
            (((1,), (1,)), ((), ())),
            preferred_element_type=jnp.float32,
        )
        * scale
        for lane in lanes
    ]
    weights = [jnp.exp(s - jnp.max(s, axis=1, keepdims=True)) for s in scores]
    mixed = [
        jnp.dot(
            w.astype(jnp.bfloat16),
            rows(key_refs, keys, part + lane),
            preferred_element_type=jnp.float32,
        )
        for w, lane in zip(weights, lanes)
    ]
    for w, m, lane in zip(weights, mixed, lanes):
        result = (m / jnp.sum(w, axis=1, keepdims=True)).astype(jnp.bfloat16)
        for block, ref in enumerate(out_refs):
            ref[:, lane : lane + HD] = result[block * tokens : (block + 1) * tokens]


def unpack_kernel(order, part, *refs):
    ins, out_ref, sems = refs[:-2], refs[-2], refs[-1]
    me = lax.axis_index("blk")
    pairs = []
    for s, ref in zip(order, ins):
        columns = pl.ds(pl.multiple_of((me ^ s) * part, 128), part)
        pairs.append((ref, out_ref.at[0, :, columns]))
    run_copies(pairs, sems)


def local_blocks(query_rows, key_rows, value_rows):
    blocks, columns_of = lax.axis_size("blk"), lax.axis_size("uly")
    tokens, width = query_rows.shape[1:]
    part = width // blocks
    heads = part // HD
    kind = query_rows.dtype
    far = list(range(blocks - 1, 1, -1))

    kv, q = (("k", 0, part), ("v", 0, part)), (("q", 0, part),)
    messages = [(s, kv) for s in far] + [(1, kv + q)] + [(s, q) for s in far] + [(0, kv), (0, q)]
    packed = pl.pallas_call(
        functools.partial(pack_kernel, messages, part),
        out_shape=[
            jax.ShapeDtypeStruct((tokens, sum(piece[2] for piece in pieces)), kind)
            for s, pieces in messages
        ],
        in_specs=[HBM] * 3,
        out_specs=[VMEM] * len(messages),
        scratch_shapes=[pltpu.SemaphoreType.DMA((sum(len(m[1]) for m in messages),))],
        compiler_params=SMALL,
        cost_estimate=pl.CostEstimate(
            flops=0, bytes_accessed=6 * tokens * width * 2, transcendentals=0
        ),
        name="pack",
    )(*[pltpu.with_memory_space_constraint(x, pltpu.HBM) for x in (query_rows, key_rows, value_rows)])

    def to_block(array, s):
        return lax.ppermute(array, "blk", [(i, i ^ s) for i in range(blocks)])

    def to_column(array, t):
        return lax.ppermute(array, "uly", [(i, (i + t) % columns_of) for i in range(columns_of)])

    sent = {message: array for message, array in zip(messages, packed)}
    own_kv, own_q = packed[-2:]
    far_kv = [to_block(sent[s, kv], s) for s in far]
    near_kvq = to_block(sent[1, kv + q], 1)
    far_kv = [hold([array], (), effort)[0] for array, effort in zip(far_kv, EFFORT_FAR)]
    near_kv = join([near_kvq], [0], 2 * part, EFFORT_NEAR)
    far_q = [to_block(hold([sent[s, q]], [array])[0], s) for s, array in zip(far, far_kv)]
    own_kv_x, first_x, near_x, second_x = (
        [to_column(group, t) for t in range(1, columns_of)]
        for group in (own_kv, far_kv[0], near_kv[0], far_kv[1])
    )
    own_kv_x = hold(own_kv_x, effort=EFFORT_OWN)
    near_q = join([own_q, near_kvq], [0, 2 * part], part)
    far_q[0] = join(far_q[:1], [0], part, EFFORT, [*own_kv_x, *first_x, *near_x])

    holders = [near_kvq, own_kv, *far_kv, *own_kv_x, *first_x, *near_x, *second_x]
    keys = [(at, None) for at in range(len(holders))]

    def attend(query_arrays, query_places):
        rows = tokens * len(query_places)
        pairs = heads * rows * tokens * len(keys)
        return pl.pallas_call(
            functools.partial(attend_kernel, len(holders), keys, query_places),
            out_shape=[jax.ShapeDtypeStruct((tokens, part), kind)] * len(query_places),
            in_specs=[VMEM] * (len(holders) + len(query_arrays)),
            out_specs=[VMEM] * len(query_places),
            compiler_params=pltpu.CompilerParams(vmem_limit_bytes=24 * 1024 * 1024),
            cost_estimate=pl.CostEstimate(
                flops=4 * HD * pairs,
                bytes_accessed=4 * part * (rows + tokens * len(keys)),
                transcendentals=pairs,
            ),
            name="attend",
        )(*holders, *query_arrays)

    mixed = dict(zip([0, 1] + far[:-1], attend([near_q] + far_q[:-1], [(0, 0), (0, 1), (1, 0)])))
    last_q = hold([far_q[-1]], [mixed[0]])
    mixed[far[-1]] = attend(last_q, [(0, None)])[0]
    mixed[1] = hold([mixed[1]], [mixed[far[-1]]])[0]
    back = {s: to_block(mixed[s], s) for s in far + [1]}
    early = far[:-1]
    back.update(zip(early, hold([back[s] for s in early], effort=EFFORT)))
    back[0] = mixed[0]
    order = [0] + far + [1]
    back = [back[s] for s in order]
    return pl.pallas_call(
        functools.partial(unpack_kernel, order, part),
        out_shape=jax.ShapeDtypeStruct((1, tokens, width), kind),
        in_specs=[VMEM] * blocks,
        out_specs=HBM,
        scratch_shapes=[pltpu.SemaphoreType.DMA((blocks,))],
        compiler_params=SMALL,
        cost_estimate=pl.CostEstimate(
            flops=0, bytes_accessed=2 * tokens * width * 2, transcendentals=0
        ),
        name="unpack",
    )(*back)


def local(query_rows, key_rows, value_rows):
    blocks = lax.axis_size("blk")
    heads = query_rows.shape[2] // HD
    few = blocks == 4 and heads % blocks == 0
    plan = local_blocks if few else local_generic
    return plan(query_rows, key_rows, value_rows)


def solution(mesh):
    in_specs = (
        P("cfg", ("groups", "blk", "uly"), None),
        P("cfg", ("groups", "blk", "uly"), None),
        P("cfg", ("groups", "blk", "uly"), None),
    )
    out_specs = P("cfg", ("groups", "blk", "uly"), None)
    return jax.shard_map(local, mesh=mesh, in_specs=in_specs, out_specs=out_specs, check_vma=False)
```

```python
import functools
import math

import jax
import jax.numpy as jnp
from jax import lax
from jax.experimental import pallas as pl
from jax.experimental.pallas import tpu as pltpu
from jax.sharding import PartitionSpec as P

HD = 128
EFFORT = 0
EFFORT_OWN = 10**9
EFFORT_QUERIES = 2 * 10**8
EFFORT_NEAR = 0
EFFORT_FAR = (10**9, 5 * 10**8)
ANY = pl.BlockSpec(memory_space=pl.ANY)
HBM = pl.BlockSpec(memory_space=pltpu.HBM)
VMEM = pl.BlockSpec(memory_space=pltpu.VMEM)
SMALL = pltpu.CompilerParams(vmem_limit_bytes=4 * 1024 * 1024)


def attend(queries, key_part, value_part):
    query_mat = queries[0, :, 0]
    row_count, head_count, head_size = query_mat.shape
    score_scale = 1.0 / math.sqrt(head_size)
    start_state = (
        jnp.full((head_count, row_count), -1e30, jnp.float32),
        jnp.zeros((head_count, row_count), jnp.float32),
        jnp.zeros((row_count, head_count, head_size), jnp.float32),
    )

    def absorb(state, pieces):
        key_piece = pieces[0][0, :, 0]
        value_piece = pieces[1][0, :, 0]
        scores = (
            jnp.einsum("qhd,khd->hqk", query_mat, key_piece, preferred_element_type=jnp.float32)
            * score_scale
        )
        running, totals, accumulated = state
        new_max = jnp.maximum(running, jnp.max(scores, axis=2))
        weights = jnp.exp(scores - new_max[:, :, None])
        factor = jnp.exp(running - new_max)
        totals = totals * factor + jnp.sum(weights, axis=2)
        probabilities = weights.astype(jnp.bfloat16)
        contrib = jnp.einsum(
            "hqk,khd->qhd", probabilities, value_piece, preferred_element_type=jnp.float32
        )
        accumulated = accumulated * factor.T[:, :, None] + contrib
        return (new_max, totals, accumulated)

    whole_keys, whole_values = (
        lax.all_gather(key_part, "blk", axis=1, tiled=True),
        lax.all_gather(value_part, "blk", axis=1, tiled=True),
    )
    key_count = whole_keys.shape[1]
    block_rows = math.gcd(key_count, 1024)

    def one_block(state, counter):
        offset = counter * block_rows
        key_block = lax.dynamic_slice_in_dim(whole_keys, offset, block_rows, 1)
        value_block = lax.dynamic_slice_in_dim(whole_values, offset, block_rows, 1)
        return (absorb(state, (key_block, value_block)), None)

    result, unused = lax.scan(
        one_block, start_state, jnp.arange(key_count // block_rows, dtype=jnp.int32)
    )
    output = (result[2] / result[1].T[:, :, None]).astype(jnp.bfloat16)
    return output.reshape(1, row_count, 1, head_count, head_size)


def local_generic(query_rows, key_rows, value_rows):
    ulysses = lax.axis_size("uly")
    tokens = query_rows.shape[1]
    width = query_rows.shape[2]
    heads_local = width // HD // ulysses

    def split_heads(array):
        array = array.reshape(1, tokens, ulysses, heads_local, HD)
        return lax.all_to_all(array, "uly", split_axis=2, concat_axis=1, tiled=True)

    mixed = attend(split_heads(query_rows), split_heads(key_rows), split_heads(value_rows))
    merged = lax.all_to_all(mixed, "uly", split_axis=1, concat_axis=2, tiled=True)
    return merged.reshape(1, tokens, width)


def run_copies(pairs, sems):
    started = [pltpu.make_async_copy(src, dst, sems.at[at]) for at, (src, dst) in enumerate(pairs)]
    for copy in started:
        copy.start()
    for copy in started:
        copy.wait()


def pack_kernel(messages, part, q_ref, k_ref, v_ref, *refs):
    outs, sems = refs[:-1], refs[-1]
    sources = {"q": q_ref, "k": k_ref, "v": v_ref}
    me = lax.axis_index("blk")
    pairs = []
    for (s, pieces), out in zip(messages, outs):
        start = 0
        for name, first, lanes in pieces:
            columns = pl.ds(pl.multiple_of((me ^ s) * part + first, 128), lanes)
            pairs.append((sources[name].at[0, :, columns], out.at[:, pl.ds(start, lanes)]))
            start += lanes
    run_copies(pairs, sems)


def join_kernel(pieces, *refs):
    lanes = refs[-1].shape[2]
    for at, (source, start) in enumerate(pieces):
        refs[-1][at] = refs[source][:, start : start + lanes]


def join(arrays, starts, lanes, effort=0, after=()):
    shape = (len(arrays), arrays[0].shape[0], lanes)
    return pl.pallas_call(
        functools.partial(join_kernel, list(enumerate(starts))),
        out_shape=jax.ShapeDtypeStruct(shape, arrays[0].dtype),
        in_specs=[VMEM] * (len(arrays) + len(after)),
        out_specs=VMEM,
        compiler_params=SMALL,
        cost_estimate=pl.CostEstimate(
            flops=effort, bytes_accessed=4 * math.prod(shape), transcendentals=0
        ),
        name="join",
    )(*arrays, *after)


def hold_kernel(*refs):
    pass


def hold(arrays, until=(), effort=0):
    return pl.pallas_call(
        hold_kernel,
        out_shape=[jax.ShapeDtypeStruct(array.shape, array.dtype) for array in arrays],
        in_specs=[ANY] * (len(arrays) + len(until)),
        out_specs=[ANY] * len(arrays),
        input_output_aliases={at: at for at in range(len(arrays))},
        compiler_params=SMALL,
        cost_estimate=pl.CostEstimate(flops=effort, bytes_accessed=0, transcendentals=0),
        name="hold",
    )(*arrays, *until)


def attend_kernel(held, keys, queries, *refs):
    key_refs, query_refs, out_refs = refs[:held], refs[held : -len(queries)], refs[-len(queries) :]
    tokens, part = out_refs[0].shape
    scale = 1.0 / math.sqrt(HD)

    def rows(sources, places, first):
        lanes = slice(first, first + HD)
        pieces = [
            sources[at][:, lanes] if row is None else sources[at][row, :, lanes]
            for at, row in places
        ]
        return jnp.concatenate(pieces, axis=0)

    lanes = range(0, part, HD)
    scores = [
        lax.dot_general(
            rows(query_refs, queries, lane),
            rows(key_refs, keys, lane),
            (((1,), (1,)), ((), ())),
            preferred_element_type=jnp.float32,
        )
        * scale
        for lane in lanes
    ]
    weights = [jnp.exp(s - jnp.max(s, axis=1, keepdims=True)) for s in scores]
    mixed = [
        jnp.dot(
            w.astype(jnp.bfloat16),
            rows(key_refs, keys, part + lane),
            preferred_element_type=jnp.float32,
        )
        for w, lane in zip(weights, lanes)
    ]
    for w, m, lane in zip(weights, mixed, lanes):
        result = (m / jnp.sum(w, axis=1, keepdims=True)).astype(jnp.bfloat16)
        for block, ref in enumerate(out_refs):
            ref[:, lane : lane + HD] = result[block * tokens : (block + 1) * tokens]


def unpack_kernel(order, part, *refs):
    ins, out_ref, sems = refs[:-2], refs[-2], refs[-1]
    me = lax.axis_index("blk")
    pairs = []
    for s, ref in zip(order, ins):
        columns = pl.ds(pl.multiple_of((me ^ s) * part, 128), part)
        pairs.append((ref, out_ref.at[0, :, columns]))
    run_copies(pairs, sems)


def local_blocks(query_rows, key_rows, value_rows):
    blocks, columns_of = lax.axis_size("blk"), lax.axis_size("uly")
    tokens, width = query_rows.shape[1:]
    part = width // blocks
    heads = part // HD
    kind = query_rows.dtype
    far = list(range(blocks - 1, 1, -1))

    kv, q = (("k", 0, part), ("v", 0, part)), (("q", 0, part),)
    messages = [(s, kv) for s in far] + [(1, kv + q)] + [(s, q) for s in far] + [(0, kv), (0, q)]
    packed = pl.pallas_call(
        functools.partial(pack_kernel, messages, part),
        out_shape=[
            jax.ShapeDtypeStruct((tokens, sum(piece[2] for piece in pieces)), kind)
            for s, pieces in messages
        ],
        in_specs=[HBM] * 3,
        out_specs=[VMEM] * len(messages),
        scratch_shapes=[pltpu.SemaphoreType.DMA((sum(len(m[1]) for m in messages),))],
        compiler_params=SMALL,
        cost_estimate=pl.CostEstimate(
            flops=0, bytes_accessed=6 * tokens * width * 2, transcendentals=0
        ),
        name="pack",
    )(*[pltpu.with_memory_space_constraint(x, pltpu.HBM) for x in (query_rows, key_rows, value_rows)])

    def to_block(array, s):
        return lax.ppermute(array, "blk", [(i, i ^ s) for i in range(blocks)])

    def to_column(array, t):
        return lax.ppermute(array, "uly", [(i, (i + t) % columns_of) for i in range(columns_of)])

    sent = {message: array for message, array in zip(messages, packed)}
    own_kv, own_q = packed[-2:]
    far_kv = [to_block(sent[s, kv], s) for s in far]
    near_kvq = to_block(sent[1, kv + q], 1)
    far_kv = [hold([array], (), effort)[0] for array, effort in zip(far_kv, EFFORT_FAR)]
    near_kv = join([near_kvq], [0], 2 * part, EFFORT_NEAR)
    far_q = [to_block(sent[far[0], q], far[0])]
    far_q += [to_block(hold([sent[s, q]], [array])[0], s) for s, array in zip(far[1:], far_kv[1:])]
    own_kv_x, first_x, near_x, second_x = (
        [to_column(group, t) for t in range(1, columns_of)]
        for group in (own_kv, far_kv[0], near_kv[0], far_kv[1])
    )
    own_kv_x = hold(own_kv_x, effort=EFFORT_OWN)
    near_q = join([own_q, near_kvq], [0, 2 * part], part)
    far_q[:1] = hold(far_q[:1], [*own_kv_x, *first_x, *near_x], EFFORT)
    far_q[:1] = hold(far_q[:1], (), EFFORT_QUERIES)

    holders = [near_kvq, own_kv, *far_kv, *own_kv_x, *first_x, *near_x, *second_x]
    keys = [(at, None) for at in range(len(holders))]

    def attend(query_arrays, query_places):
        rows = tokens * len(query_places)
        pairs = heads * rows * tokens * len(keys)
        return pl.pallas_call(
            functools.partial(attend_kernel, len(holders), keys, query_places),
            out_shape=[jax.ShapeDtypeStruct((tokens, part), kind)] * len(query_places),
            in_specs=[VMEM] * (len(holders) + len(query_arrays)),
            out_specs=[VMEM] * len(query_places),
            compiler_params=pltpu.CompilerParams(vmem_limit_bytes=24 * 1024 * 1024),
            cost_estimate=pl.CostEstimate(
                flops=4 * HD * pairs,
                bytes_accessed=4 * part * (rows + tokens * len(keys)),
                transcendentals=pairs,
            ),
            name="attend",
        )(*holders, *query_arrays)

    mixed = dict(zip([0, 1] + far[:-1], attend([near_q] + far_q[:-1], [(0, 0), (0, 1), (1, None)])))
    last_q = hold([far_q[-1]], [mixed[0]])
    mixed[far[-1]] = attend(last_q, [(0, None)])[0]
    mixed[1] = hold([mixed[1]], [mixed[far[-1]]])[0]
    back = {s: to_block(mixed[s], s) for s in far + [1]}
    early = far[:-1]
    back.update(zip(early, hold([back[s] for s in early], effort=EFFORT)))
    back[0] = mixed[0]
    order = [0] + far + [1]
    back = [back[s] for s in order]
    return pl.pallas_call(
        functools.partial(unpack_kernel, order, part),
        out_shape=jax.ShapeDtypeStruct((1, tokens, width), kind),
        in_specs=[VMEM] * blocks,
        out_specs=HBM,
        scratch_shapes=[pltpu.SemaphoreType.DMA((blocks,))],
        compiler_params=SMALL,
        cost_estimate=pl.CostEstimate(
            flops=0, bytes_accessed=2 * tokens * width * 2, transcendentals=0
        ),
        name="unpack",
    )(*back)


def local(query_rows, key_rows, value_rows):
    blocks = lax.axis_size("blk")
    heads = query_rows.shape[2] // HD
    few = blocks == 4 and heads % blocks == 0
    plan = local_blocks if few else local_generic
    return plan(query_rows, key_rows, value_rows)


def solution(mesh):
    in_specs = (
        P("cfg", ("groups", "blk", "uly"), None),
        P("cfg", ("groups", "blk", "uly"), None),
        P("cfg", ("groups", "blk", "uly"), None),
    )
    out_specs = P("cfg", ("groups", "blk", "uly"), None)
    return jax.shard_map(local, mesh=mesh, in_specs=in_specs, out_specs=out_specs, check_vma=False)
```

```python
import functools
import math

import jax
import jax.numpy as jnp
from jax import lax
from jax.experimental import pallas as pl
from jax.experimental.pallas import tpu as pltpu
from jax.sharding import PartitionSpec as P

HD = 128
EFFORT_BACK = 10**9
EFFORT_OWN = 10**9
EFFORT_QUERIES = 2 * 10**8
EFFORT_NEAR = 0
EFFORT_FAR = (10**9, 5 * 10**8)
ANY = pl.BlockSpec(memory_space=pl.ANY)
HBM = pl.BlockSpec(memory_space=pltpu.HBM)
VMEM = pl.BlockSpec(memory_space=pltpu.VMEM)
SMALL = pltpu.CompilerParams(vmem_limit_bytes=4 * 1024 * 1024)


def attend(queries, key_part, value_part):
    query_mat = queries[0, :, 0]
    row_count, head_count, head_size = query_mat.shape
    score_scale = 1.0 / math.sqrt(head_size)
    start_state = (
        jnp.full((head_count, row_count), -1e30, jnp.float32),
        jnp.zeros((head_count, row_count), jnp.float32),
        jnp.zeros((row_count, head_count, head_size), jnp.float32),
    )

    def absorb(state, pieces):
        key_piece = pieces[0][0, :, 0]
        value_piece = pieces[1][0, :, 0]
        scores = (
            jnp.einsum("qhd,khd->hqk", query_mat, key_piece, preferred_element_type=jnp.float32)
            * score_scale
        )
        running, totals, accumulated = state
        new_max = jnp.maximum(running, jnp.max(scores, axis=2))
        weights = jnp.exp(scores - new_max[:, :, None])
        factor = jnp.exp(running - new_max)
        totals = totals * factor + jnp.sum(weights, axis=2)
        probabilities = weights.astype(jnp.bfloat16)
        contrib = jnp.einsum(
            "hqk,khd->qhd", probabilities, value_piece, preferred_element_type=jnp.float32
        )
        accumulated = accumulated * factor.T[:, :, None] + contrib
        return (new_max, totals, accumulated)

    whole_keys, whole_values = (
        lax.all_gather(key_part, "blk", axis=1, tiled=True),
        lax.all_gather(value_part, "blk", axis=1, tiled=True),
    )
    key_count = whole_keys.shape[1]
    block_rows = math.gcd(key_count, 1024)

    def one_block(state, counter):
        offset = counter * block_rows
        key_block = lax.dynamic_slice_in_dim(whole_keys, offset, block_rows, 1)
        value_block = lax.dynamic_slice_in_dim(whole_values, offset, block_rows, 1)
        return (absorb(state, (key_block, value_block)), None)

    result, unused = lax.scan(
        one_block, start_state, jnp.arange(key_count // block_rows, dtype=jnp.int32)
    )
    output = (result[2] / result[1].T[:, :, None]).astype(jnp.bfloat16)
    return output.reshape(1, row_count, 1, head_count, head_size)


def local_generic(query_rows, key_rows, value_rows):
    ulysses = lax.axis_size("uly")
    tokens = query_rows.shape[1]
    width = query_rows.shape[2]
    heads_local = width // HD // ulysses

    def split_heads(array):
        array = array.reshape(1, tokens, ulysses, heads_local, HD)
        return lax.all_to_all(array, "uly", split_axis=2, concat_axis=1, tiled=True)

    mixed = attend(split_heads(query_rows), split_heads(key_rows), split_heads(value_rows))
    merged = lax.all_to_all(mixed, "uly", split_axis=1, concat_axis=2, tiled=True)
    return merged.reshape(1, tokens, width)


def run_copies(pairs, sems):
    started = [pltpu.make_async_copy(src, dst, sems.at[at]) for at, (src, dst) in enumerate(pairs)]
    for copy in started:
        copy.start()
    for copy in started:
        copy.wait()


def pack_kernel(messages, part, q_ref, k_ref, v_ref, *refs):
    outs, sems = refs[:-1], refs[-1]
    sources = {"q": q_ref, "k": k_ref, "v": v_ref}
    me = lax.axis_index("blk")
    pairs = []
    for (s, pieces), out in zip(messages, outs):
        start = 0
        for name, first, lanes in pieces:
            columns = pl.ds(pl.multiple_of((me ^ s) * part + first, 128), lanes)
            pairs.append((sources[name].at[0, :, columns], out.at[:, pl.ds(start, lanes)]))
            start += lanes
    run_copies(pairs, sems)


def hold_kernel(*refs):
    pass


def hold(arrays, until=(), effort=0):
    return pl.pallas_call(
        hold_kernel,
        out_shape=[jax.ShapeDtypeStruct(array.shape, array.dtype) for array in arrays],
        in_specs=[ANY] * (len(arrays) + len(until)),
        out_specs=[ANY] * len(arrays),
        input_output_aliases={at: at for at in range(len(arrays))},
        compiler_params=SMALL,
        cost_estimate=pl.CostEstimate(flops=effort, bytes_accessed=0, transcendentals=0),
        name="hold",
    )(*arrays, *until)


def attend_kernel(held, keys, queries, *refs):
    key_refs, query_refs, out_refs = refs[:held], refs[held : -len(queries)], refs[-len(queries) :]
    tokens, part = out_refs[0].shape
    scale = 1.0 / math.sqrt(HD)

    def rows(sources, places, first):
        lanes = slice(first, first + HD)
        pieces = [
            sources[at][:, lanes] if row is None else sources[at][row, :, lanes]
            for at, row in places
        ]
        return jnp.concatenate(pieces, axis=0)

    lanes = range(0, part, HD)
    scores = [
        lax.dot_general(
            rows(query_refs, queries, lane),
            rows(key_refs, keys, lane),
            (((1,), (1,)), ((), ())),
            preferred_element_type=jnp.float32,
        )
        * scale
        for lane in lanes
    ]
    weights = [jnp.exp(s - jnp.max(s, axis=1, keepdims=True)) for s in scores]
    mixed = [
        jnp.dot(
            w.astype(jnp.bfloat16),
            rows(key_refs, keys, part + lane),
            preferred_element_type=jnp.float32,
        )
        for w, lane in zip(weights, lanes)
    ]
    for w, m, lane in zip(weights, mixed, lanes):
        result = (m / jnp.sum(w, axis=1, keepdims=True)).astype(jnp.bfloat16)
        for block, ref in enumerate(out_refs):
            ref[:, lane : lane + HD] = result[block * tokens : (block + 1) * tokens]


def unpack_kernel(order, part, *refs):
    ins, out_ref, sems = refs[:-2], refs[-2], refs[-1]
    me = lax.axis_index("blk")
    pairs = []
    for s, ref in zip(order, ins):
        columns = pl.ds(pl.multiple_of((me ^ s) * part, 128), part)
        pairs.append((ref, out_ref.at[0, :, columns]))
    run_copies(pairs, sems)


def local_blocks(query_rows, key_rows, value_rows):
    blocks, columns_of = lax.axis_size("blk"), lax.axis_size("uly")
    tokens, width = query_rows.shape[1:]
    part = width // blocks
    heads = part // HD
    kind = query_rows.dtype
    far = list(range(blocks - 1, 1, -1))

    kv, q = (("k", 0, part), ("v", 0, part)), (("q", 0, part),)
    messages = [(s, names) for names in (kv, q) for s in far + [1, 0]]
    packed = pl.pallas_call(
        functools.partial(pack_kernel, messages, part),
        out_shape=[
            jax.ShapeDtypeStruct((tokens, sum(piece[2] for piece in pieces)), kind)
            for s, pieces in messages
        ],
        in_specs=[HBM] * 3,
        out_specs=[VMEM] * len(messages),
        scratch_shapes=[pltpu.SemaphoreType.DMA((sum(len(m[1]) for m in messages),))],
        compiler_params=SMALL,
        cost_estimate=pl.CostEstimate(
            flops=0, bytes_accessed=6 * tokens * width * 2, transcendentals=0
        ),
        name="pack",
    )(*[pltpu.with_memory_space_constraint(x, pltpu.HBM) for x in (query_rows, key_rows, value_rows)])

    def to_block(array, s):
        return lax.ppermute(array, "blk", [(i, i ^ s) for i in range(blocks)])

    def to_column(array, t):
        return lax.ppermute(array, "uly", [(i, (i + t) % columns_of) for i in range(columns_of)])

    sent = {message: array for message, array in zip(messages, packed)}
    own_kv, own_q = sent[0, kv], sent[0, q]
    far_kv = [to_block(sent[s, kv], s) for s in far]
    far_kv = [hold([array], (), effort)[0] for array, effort in zip(far_kv, EFFORT_FAR)]
    near_kv = hold([to_block(sent[1, kv], 1)], (), EFFORT_NEAR)[0]

    own_kv_x, first_x, near_x, second_x = (
        [to_column(group, t) for t in range(1, columns_of)]
        for group in (own_kv, far_kv[0], near_kv, far_kv[1])
    )
    own_kv_x = hold(own_kv_x, effort=EFFORT_OWN)
    first_q = to_block(sent[far[0], q], far[0])
    first_q = hold([first_q], [*own_kv_x, *first_x, *near_x], EFFORT_QUERIES)[0]
    second_q, near_q = (to_block(hold([sent[s, q]], far_kv[1:])[0], s) for s in (far[1], 1))

    holders = [near_kv, own_kv, *far_kv, *own_kv_x, *first_x, *near_x, *second_x]
    keys = [(at, None) for at in range(len(holders))]

    def attend(query_arrays, query_places):
        rows = tokens * len(query_places)
        pairs = heads * rows * tokens * len(keys)
        return pl.pallas_call(
            functools.partial(attend_kernel, len(holders), keys, query_places),
            out_shape=[jax.ShapeDtypeStruct((tokens, part), kind)] * len(query_places),
            in_specs=[VMEM] * (len(holders) + len(query_arrays)),
            out_specs=[VMEM] * len(query_places),
            compiler_params=pltpu.CompilerParams(vmem_limit_bytes=24 * 1024 * 1024),
            cost_estimate=pl.CostEstimate(
                flops=4 * HD * pairs,
                bytes_accessed=4 * part * (rows + tokens * len(keys)),
                transcendentals=pairs,
            ),
            name="attend",
        )(*holders, *query_arrays)

    mixed = dict(zip((0, far[0]), attend([own_q, first_q], [(0, None), (1, None)])))
    last_q = hold([second_q, near_q], [mixed[0]])
    mixed.update(zip((far[1], 1), attend(last_q, [(0, None), (1, None)])))
    back = {s: to_block(mixed[s], s) for s in far + [1]}
    early = far[:-1]
    back.update(zip(early, hold([back[s] for s in early], effort=EFFORT_BACK)))
    back[0] = mixed[0]
    order = [0] + far + [1]
    back = [back[s] for s in order]
    return pl.pallas_call(
        functools.partial(unpack_kernel, order, part),
        out_shape=jax.ShapeDtypeStruct((1, tokens, width), kind),
        in_specs=[VMEM] * blocks,
        out_specs=HBM,
        scratch_shapes=[pltpu.SemaphoreType.DMA((blocks,))],
        compiler_params=SMALL,
        cost_estimate=pl.CostEstimate(
            flops=0, bytes_accessed=2 * tokens * width * 2, transcendentals=0
        ),
        name="unpack",
    )(*back)


def local(query_rows, key_rows, value_rows):
    blocks = lax.axis_size("blk")
    heads = query_rows.shape[2] // HD
    few = blocks == 4 and heads % blocks == 0
    plan = local_blocks if few else local_generic
    return plan(query_rows, key_rows, value_rows)


def solution(mesh):
    in_specs = (
        P("cfg", ("groups", "blk", "uly"), None),
        P("cfg", ("groups", "blk", "uly"), None),
        P("cfg", ("groups", "blk", "uly"), None),
    )
    out_specs = P("cfg", ("groups", "blk", "uly"), None)
    return jax.shard_map(local, mesh=mesh, in_specs=in_specs, out_specs=out_specs, check_vma=False)
```

```python
import functools
import math

import jax
import jax.numpy as jnp
from jax import lax
from jax.experimental import pallas as pl
from jax.experimental.pallas import tpu as pltpu
from jax.sharding import PartitionSpec as P

HD = 128
EFFORT_BACK = 10**9
EFFORT_OWN = 10**9
EFFORT_QUERIES = 2 * 10**8
EFFORT_NEAR = 0
EFFORT_FAR = (5 * 10**8, 5 * 10**8)
ANY = pl.BlockSpec(memory_space=pl.ANY)
HBM = pl.BlockSpec(memory_space=pltpu.HBM)
VMEM = pl.BlockSpec(memory_space=pltpu.VMEM)
SMALL = pltpu.CompilerParams(vmem_limit_bytes=4 * 1024 * 1024)


def attend(queries, key_part, value_part):
    query_mat = queries[0, :, 0]
    row_count, head_count, head_size = query_mat.shape
    score_scale = 1.0 / math.sqrt(head_size)
    start_state = (
        jnp.full((head_count, row_count), -1e30, jnp.float32),
        jnp.zeros((head_count, row_count), jnp.float32),
        jnp.zeros((row_count, head_count, head_size), jnp.float32),
    )

    def absorb(state, pieces):
        key_piece = pieces[0][0, :, 0]
        value_piece = pieces[1][0, :, 0]
        scores = (
            jnp.einsum("qhd,khd->hqk", query_mat, key_piece, preferred_element_type=jnp.float32)
            * score_scale
        )
        running, totals, accumulated = state
        new_max = jnp.maximum(running, jnp.max(scores, axis=2))
        weights = jnp.exp(scores - new_max[:, :, None])
        factor = jnp.exp(running - new_max)
        totals = totals * factor + jnp.sum(weights, axis=2)
        probabilities = weights.astype(jnp.bfloat16)
        contrib = jnp.einsum(
            "hqk,khd->qhd", probabilities, value_piece, preferred_element_type=jnp.float32
        )
        accumulated = accumulated * factor.T[:, :, None] + contrib
        return (new_max, totals, accumulated)

    whole_keys, whole_values = (
        lax.all_gather(key_part, "blk", axis=1, tiled=True),
        lax.all_gather(value_part, "blk", axis=1, tiled=True),
    )
    key_count = whole_keys.shape[1]
    block_rows = math.gcd(key_count, 1024)

    def one_block(state, counter):
        offset = counter * block_rows
        key_block = lax.dynamic_slice_in_dim(whole_keys, offset, block_rows, 1)
        value_block = lax.dynamic_slice_in_dim(whole_values, offset, block_rows, 1)
        return (absorb(state, (key_block, value_block)), None)

    result, unused = lax.scan(
        one_block, start_state, jnp.arange(key_count // block_rows, dtype=jnp.int32)
    )
    output = (result[2] / result[1].T[:, :, None]).astype(jnp.bfloat16)
    return output.reshape(1, row_count, 1, head_count, head_size)


def local_generic(query_rows, key_rows, value_rows):
    ulysses = lax.axis_size("uly")
    tokens = query_rows.shape[1]
    width = query_rows.shape[2]
    heads_local = width // HD // ulysses

    def split_heads(array):
        array = array.reshape(1, tokens, ulysses, heads_local, HD)
        return lax.all_to_all(array, "uly", split_axis=2, concat_axis=1, tiled=True)

    mixed = attend(split_heads(query_rows), split_heads(key_rows), split_heads(value_rows))
    merged = lax.all_to_all(mixed, "uly", split_axis=1, concat_axis=2, tiled=True)
    return merged.reshape(1, tokens, width)


def run_copies(pairs, sems):
    started = [pltpu.make_async_copy(src, dst, sems.at[at]) for at, (src, dst) in enumerate(pairs)]
    for copy in started:
        copy.start()
    for copy in started:
        copy.wait()


def pack_kernel(messages, part, q_ref, k_ref, v_ref, *refs):
    outs, sems = refs[:-1], refs[-1]
    sources = {"q": q_ref, "k": k_ref, "v": v_ref}
    me = lax.axis_index("blk")
    pairs = []
    for (s, pieces), out in zip(messages, outs):
        start = 0
        for name, first, lanes in pieces:
            columns = pl.ds(pl.multiple_of((me ^ s) * part + first, 128), lanes)
            pairs.append((sources[name].at[0, :, columns], out.at[:, pl.ds(start, lanes)]))
            start += lanes
    run_copies(pairs, sems)


def hold_kernel(*refs):
    pass


def hold(arrays, until=(), effort=0):
    return pl.pallas_call(
        hold_kernel,
        out_shape=[jax.ShapeDtypeStruct(array.shape, array.dtype) for array in arrays],
        in_specs=[ANY] * (len(arrays) + len(until)),
        out_specs=[ANY] * len(arrays),
        input_output_aliases={at: at for at in range(len(arrays))},
        compiler_params=SMALL,
        cost_estimate=pl.CostEstimate(flops=effort, bytes_accessed=0, transcendentals=0),
        name="hold",
    )(*arrays, *until)


def attend_kernel(held, keys, queries, *refs):
    key_refs, query_refs, out_refs = refs[:held], refs[held : -len(queries)], refs[-len(queries) :]
    tokens, part = out_refs[0].shape
    scale = 1.0 / math.sqrt(HD)

    def rows(sources, places, first):
        lanes = slice(first, first + HD)
        pieces = [
            sources[at][:, lanes] if row is None else sources[at][row, :, lanes]
            for at, row in places
        ]
        return jnp.concatenate(pieces, axis=0)

    lanes = range(0, part, HD)
    scores = [
        lax.dot_general(
            rows(query_refs, queries, lane),
            rows(key_refs, keys, lane),
            (((1,), (1,)), ((), ())),
            preferred_element_type=jnp.float32,
        )
        * scale
        for lane in lanes
    ]
    weights = [jnp.exp(s - jnp.max(s, axis=1, keepdims=True)) for s in scores]
    mixed = [
        jnp.dot(
            w.astype(jnp.bfloat16),
            rows(key_refs, keys, part + lane),
            preferred_element_type=jnp.float32,
        )
        for w, lane in zip(weights, lanes)
    ]
    for w, m, lane in zip(weights, mixed, lanes):
        result = (m / jnp.sum(w, axis=1, keepdims=True)).astype(jnp.bfloat16)
        for block, ref in enumerate(out_refs):
            ref[:, lane : lane + HD] = result[block * tokens : (block + 1) * tokens]


def unpack_kernel(order, part, *refs):
    ins, out_ref, sems = refs[:-2], refs[-2], refs[-1]
    me = lax.axis_index("blk")
    pairs = []
    for s, ref in zip(order, ins):
        columns = pl.ds(pl.multiple_of((me ^ s) * part, 128), part)
        pairs.append((ref, out_ref.at[0, :, columns]))
    run_copies(pairs, sems)


def local_blocks(query_rows, key_rows, value_rows):
    blocks, columns_of = lax.axis_size("blk"), lax.axis_size("uly")
    tokens, width = query_rows.shape[1:]
    part = width // blocks
    heads = part // HD
    kind = query_rows.dtype
    far = list(range(blocks - 1, 1, -1))

    kv, q = (("k", 0, part), ("v", 0, part)), (("q", 0, part),)
    messages = [(s, names) for names in (kv, q) for s in far + [1, 0]]
    packed = pl.pallas_call(
        functools.partial(pack_kernel, messages, part),
        out_shape=[
            jax.ShapeDtypeStruct((tokens, sum(piece[2] for piece in pieces)), kind)
            for s, pieces in messages
        ],
        in_specs=[HBM] * 3,
        out_specs=[VMEM] * len(messages),
        scratch_shapes=[pltpu.SemaphoreType.DMA((sum(len(m[1]) for m in messages),))],
        compiler_params=SMALL,
        cost_estimate=pl.CostEstimate(
            flops=0, bytes_accessed=6 * tokens * width * 2, transcendentals=0
        ),
        name="pack",
    )(*[pltpu.with_memory_space_constraint(x, pltpu.HBM) for x in (query_rows, key_rows, value_rows)])

    def to_block(array, s):
        return lax.ppermute(array, "blk", [(i, i ^ s) for i in range(blocks)])

    def to_column(array, t):
        return lax.ppermute(array, "uly", [(i, (i + t) % columns_of) for i in range(columns_of)])

    sent = {message: array for message, array in zip(messages, packed)}
    own_kv, own_q = sent[0, kv], sent[0, q]
    far_kv = [to_block(sent[s, kv], s) for s in far]
    far_kv = [hold([array], (), effort)[0] for array, effort in zip(far_kv, EFFORT_FAR)]
    near_kv = hold([to_block(sent[1, kv], 1)], far_kv[:1], EFFORT_NEAR)[0]

    own_kv_x, first_x, near_x, second_x = (
        [to_column(group, t) for t in range(1, columns_of)]
        for group in (own_kv, far_kv[0], near_kv, far_kv[1])
    )
    own_kv_x = hold(own_kv_x, effort=EFFORT_OWN)
    first_q = to_block(sent[far[0], q], far[0])
    first_q = hold([first_q], [*own_kv_x, *first_x, *near_x], EFFORT_QUERIES)[0]
    second_q, near_q = (to_block(hold([sent[s, q]], far_kv[1:])[0], s) for s in (far[1], 1))

    holders = [near_kv, own_kv, *far_kv, *own_kv_x, *first_x, *near_x, *second_x]
    keys = [(at, None) for at in range(len(holders))]

    def attend(query_arrays, query_places):
        rows = tokens * len(query_places)
        pairs = heads * rows * tokens * len(keys)
        return pl.pallas_call(
            functools.partial(attend_kernel, len(holders), keys, query_places),
            out_shape=[jax.ShapeDtypeStruct((tokens, part), kind)] * len(query_places),
            in_specs=[VMEM] * (len(holders) + len(query_arrays)),
            out_specs=[VMEM] * len(query_places),
            compiler_params=pltpu.CompilerParams(vmem_limit_bytes=24 * 1024 * 1024),
            cost_estimate=pl.CostEstimate(
                flops=4 * HD * pairs,
                bytes_accessed=4 * part * (rows + tokens * len(keys)),
                transcendentals=pairs,
            ),
            name="attend",
        )(*holders, *query_arrays)

    mixed = dict(zip((0, far[0]), attend([own_q, first_q], [(0, None), (1, None)])))
    last_q = hold([second_q, near_q], [mixed[0]])
    mixed.update(zip((far[1], 1), attend(last_q, [(0, None), (1, None)])))
    back = {s: to_block(mixed[s], s) for s in far + [1]}
    early = far[:-1]
    back.update(zip(early, hold([back[s] for s in early], effort=EFFORT_BACK)))
    back[0] = mixed[0]
    order = [0] + far + [1]
    back = [back[s] for s in order]
    return pl.pallas_call(
        functools.partial(unpack_kernel, order, part),
        out_shape=jax.ShapeDtypeStruct((1, tokens, width), kind),
        in_specs=[VMEM] * blocks,
        out_specs=HBM,
        scratch_shapes=[pltpu.SemaphoreType.DMA((blocks,))],
        compiler_params=SMALL,
        cost_estimate=pl.CostEstimate(
            flops=0, bytes_accessed=2 * tokens * width * 2, transcendentals=0
        ),
        name="unpack",
    )(*back)


def local(query_rows, key_rows, value_rows):
    blocks = lax.axis_size("blk")
    heads = query_rows.shape[2] // HD
    few = blocks == 4 and heads % blocks == 0
    plan = local_blocks if few else local_generic
    return plan(query_rows, key_rows, value_rows)


def solution(mesh):
    in_specs = (
        P("cfg", ("groups", "blk", "uly"), None),
        P("cfg", ("groups", "blk", "uly"), None),
        P("cfg", ("groups", "blk", "uly"), None),
    )
    out_specs = P("cfg", ("groups", "blk", "uly"), None)
    return jax.shard_map(local, mesh=mesh, in_specs=in_specs, out_specs=out_specs, check_vma=False)
```

```python
import functools
import math

import jax
import jax.numpy as jnp
from jax import lax
from jax.experimental import pallas as pl
from jax.experimental.pallas import tpu as pltpu
from jax.sharding import PartitionSpec as P

HD = 128
EFFORT = 0
EFFORT_BACK = 10**9
EFFORT_OWN = 10**9
EFFORT_QUERIES = 2 * 10**8
EFFORT_NEAR = 0
EFFORT_FAR = (10**9, 5 * 10**8)
ANY = pl.BlockSpec(memory_space=pl.ANY)
HBM = pl.BlockSpec(memory_space=pltpu.HBM)
VMEM = pl.BlockSpec(memory_space=pltpu.VMEM)
SMALL = pltpu.CompilerParams(vmem_limit_bytes=4 * 1024 * 1024)


def attend(queries, key_part, value_part):
    query_mat = queries[0, :, 0]
    row_count, head_count, head_size = query_mat.shape
    score_scale = 1.0 / math.sqrt(head_size)
    start_state = (
        jnp.full((head_count, row_count), -1e30, jnp.float32),
        jnp.zeros((head_count, row_count), jnp.float32),
        jnp.zeros((row_count, head_count, head_size), jnp.float32),
    )

    def absorb(state, pieces):
        key_piece = pieces[0][0, :, 0]
        value_piece = pieces[1][0, :, 0]
        scores = (
            jnp.einsum("qhd,khd->hqk", query_mat, key_piece, preferred_element_type=jnp.float32)
            * score_scale
        )
        running, totals, accumulated = state
        new_max = jnp.maximum(running, jnp.max(scores, axis=2))
        weights = jnp.exp(scores - new_max[:, :, None])
        factor = jnp.exp(running - new_max)
        totals = totals * factor + jnp.sum(weights, axis=2)
        probabilities = weights.astype(jnp.bfloat16)
        contrib = jnp.einsum(
            "hqk,khd->qhd", probabilities, value_piece, preferred_element_type=jnp.float32
        )
        accumulated = accumulated * factor.T[:, :, None] + contrib
        return (new_max, totals, accumulated)

    whole_keys, whole_values = (
        lax.all_gather(key_part, "blk", axis=1, tiled=True),
        lax.all_gather(value_part, "blk", axis=1, tiled=True),
    )
    key_count = whole_keys.shape[1]
    block_rows = math.gcd(key_count, 1024)

    def one_block(state, counter):
        offset = counter * block_rows
        key_block = lax.dynamic_slice_in_dim(whole_keys, offset, block_rows, 1)
        value_block = lax.dynamic_slice_in_dim(whole_values, offset, block_rows, 1)
        return (absorb(state, (key_block, value_block)), None)

    result, unused = lax.scan(
        one_block, start_state, jnp.arange(key_count // block_rows, dtype=jnp.int32)
    )
    output = (result[2] / result[1].T[:, :, None]).astype(jnp.bfloat16)
    return output.reshape(1, row_count, 1, head_count, head_size)


def local_generic(query_rows, key_rows, value_rows):
    ulysses = lax.axis_size("uly")
    tokens = query_rows.shape[1]
    width = query_rows.shape[2]
    heads_local = width // HD // ulysses

    def split_heads(array):
        array = array.reshape(1, tokens, ulysses, heads_local, HD)
        return lax.all_to_all(array, "uly", split_axis=2, concat_axis=1, tiled=True)

    mixed = attend(split_heads(query_rows), split_heads(key_rows), split_heads(value_rows))
    merged = lax.all_to_all(mixed, "uly", split_axis=1, concat_axis=2, tiled=True)
    return merged.reshape(1, tokens, width)


def run_copies(pairs, sems):
    started = [pltpu.make_async_copy(src, dst, sems.at[at]) for at, (src, dst) in enumerate(pairs)]
    for copy in started:
        copy.start()
    for copy in started:
        copy.wait()


def pack_kernel(messages, part, q_ref, k_ref, v_ref, *refs):
    outs, sems = refs[:-1], refs[-1]
    sources = {"q": q_ref, "k": k_ref, "v": v_ref}
    me = lax.axis_index("blk")
    pairs = []
    for (s, pieces), out in zip(messages, outs):
        start = 0
        for name, first, lanes in pieces:
            columns = pl.ds(pl.multiple_of((me ^ s) * part + first, 128), lanes)
            pairs.append((sources[name].at[0, :, columns], out.at[:, pl.ds(start, lanes)]))
            start += lanes
    run_copies(pairs, sems)


def join_kernel(pieces, *refs):
    lanes = refs[-1].shape[2]
    for at, (source, start) in enumerate(pieces):
        refs[-1][at] = refs[source][:, start : start + lanes]


def join(arrays, starts, lanes, effort=0, after=()):
    shape = (len(arrays), arrays[0].shape[0], lanes)
    return pl.pallas_call(
        functools.partial(join_kernel, list(enumerate(starts))),
        out_shape=jax.ShapeDtypeStruct(shape, arrays[0].dtype),
        in_specs=[VMEM] * (len(arrays) + len(after)),
        out_specs=VMEM,
        compiler_params=SMALL,
        cost_estimate=pl.CostEstimate(
            flops=effort, bytes_accessed=4 * math.prod(shape), transcendentals=0
        ),
        name="join",
    )(*arrays, *after)


def hold_kernel(*refs):
    pass


def hold(arrays, until=(), effort=0):
    return pl.pallas_call(
        hold_kernel,
        out_shape=[jax.ShapeDtypeStruct(array.shape, array.dtype) for array in arrays],
        in_specs=[ANY] * (len(arrays) + len(until)),
        out_specs=[ANY] * len(arrays),
        input_output_aliases={at: at for at in range(len(arrays))},
        compiler_params=SMALL,
        cost_estimate=pl.CostEstimate(flops=effort, bytes_accessed=0, transcendentals=0),
        name="hold",
    )(*arrays, *until)


def attend_kernel(held, keys, queries, *refs):
    key_refs, query_refs, out_refs = refs[:held], refs[held : -len(queries)], refs[-len(queries) :]
    tokens, part = out_refs[0].shape
    scale = 1.0 / math.sqrt(HD)

    def rows(sources, places, first):
        lanes = slice(first, first + HD)
        pieces = [
            sources[at][:, lanes] if row is None else sources[at][row, :, lanes]
            for at, row in places
        ]
        return jnp.concatenate(pieces, axis=0)

    lanes = range(0, part, HD)
    scores = [
        lax.dot_general(
            rows(query_refs, queries, lane),
            rows(key_refs, keys, lane),
            (((1,), (1,)), ((), ())),
            preferred_element_type=jnp.float32,
        )
        * scale
        for lane in lanes
    ]
    weights = [jnp.exp(s - jnp.max(s, axis=1, keepdims=True)) for s in scores]
    mixed = [
        jnp.dot(
            w.astype(jnp.bfloat16),
            rows(key_refs, keys, part + lane),
            preferred_element_type=jnp.float32,
        )
        for w, lane in zip(weights, lanes)
    ]
    for w, m, lane in zip(weights, mixed, lanes):
        result = (m / jnp.sum(w, axis=1, keepdims=True)).astype(jnp.bfloat16)
        for block, ref in enumerate(out_refs):
            ref[:, lane : lane + HD] = result[block * tokens : (block + 1) * tokens]


def unpack_kernel(order, part, *refs):
    ins, out_ref, sems = refs[:-2], refs[-2], refs[-1]
    me = lax.axis_index("blk")
    pairs = []
    for s, ref in zip(order, ins):
        columns = pl.ds(pl.multiple_of((me ^ s) * part, 128), part)
        pairs.append((ref, out_ref.at[0, :, columns]))
    run_copies(pairs, sems)


def local_blocks(query_rows, key_rows, value_rows):
    blocks, columns_of = lax.axis_size("blk"), lax.axis_size("uly")
    tokens, width = query_rows.shape[1:]
    part = width // blocks
    heads = part // HD
    kind = query_rows.dtype
    far = list(range(blocks - 1, 1, -1))

    kv, q = (("k", 0, part), ("v", 0, part)), (("q", 0, part),)
    messages = [(s, kv) for s in far] + [(1, kv + q)] + [(s, q) for s in far] + [(0, kv), (0, q)]
    packed = pl.pallas_call(
        functools.partial(pack_kernel, messages, part),
        out_shape=[
            jax.ShapeDtypeStruct((tokens, sum(piece[2] for piece in pieces)), kind)
            for s, pieces in messages
        ],
        in_specs=[HBM] * 3,
        out_specs=[VMEM] * len(messages),
        scratch_shapes=[pltpu.SemaphoreType.DMA((sum(len(m[1]) for m in messages),))],
        compiler_params=SMALL,
        cost_estimate=pl.CostEstimate(
            flops=0, bytes_accessed=6 * tokens * width * 2, transcendentals=0
        ),
        name="pack",
    )(*[pltpu.with_memory_space_constraint(x, pltpu.HBM) for x in (query_rows, key_rows, value_rows)])

    def to_block(array, s):
        return lax.ppermute(array, "blk", [(i, i ^ s) for i in range(blocks)])

    def to_column(array, t):
        return lax.ppermute(array, "uly", [(i, (i + t) % columns_of) for i in range(columns_of)])

    sent = {message: array for message, array in zip(messages, packed)}
    own_kv, own_q = packed[-2:]
    far_kv = [to_block(sent[s, kv], s) for s in far]
    near_kvq = to_block(sent[1, kv + q], 1)
    far_kv = [hold([array], (), effort)[0] for array, effort in zip(far_kv, EFFORT_FAR)]
    near_kv = join([near_kvq], [0], 2 * part, EFFORT_NEAR, far_kv[:1])
    far_q = [to_block(sent[far[0], q], far[0])]
    far_q += [to_block(hold([sent[s, q]], [array])[0], s) for s, array in zip(far[1:], far_kv[1:])]
    own_kv_x, first_x, near_x, second_x = (
        [to_column(group, t) for t in range(1, columns_of)]
        for group in (own_kv, far_kv[0], near_kv[0], far_kv[1])
    )
    own_kv_x = hold(own_kv_x, effort=EFFORT_OWN)
    near_q = join([own_q, near_kvq], [0, 2 * part], part)
    far_q[:1] = hold(far_q[:1], [*own_kv_x, *first_x, *near_x], EFFORT)
    far_q[:1] = hold(far_q[:1], (), EFFORT_QUERIES)

    holders = [near_kvq, own_kv, *far_kv, *own_kv_x, *first_x, *near_x, *second_x]
    keys = [(at, None) for at in range(len(holders))]

    def attend(query_arrays, query_places):
        rows = tokens * len(query_places)
        pairs = heads * rows * tokens * len(keys)
        return pl.pallas_call(
            functools.partial(attend_kernel, len(holders), keys, query_places),
            out_shape=[jax.ShapeDtypeStruct((tokens, part), kind)] * len(query_places),
            in_specs=[VMEM] * (len(holders) + len(query_arrays)),
            out_specs=[VMEM] * len(query_places),
            compiler_params=pltpu.CompilerParams(vmem_limit_bytes=24 * 1024 * 1024),
            cost_estimate=pl.CostEstimate(
                flops=4 * HD * pairs,
                bytes_accessed=4 * part * (rows + tokens * len(keys)),
                transcendentals=pairs,
            ),
            name="attend",
        )(*holders, *query_arrays)

    mixed = dict(zip([0, 1] + far[:-1], attend([near_q] + far_q[:-1], [(0, 0), (0, 1), (1, None)])))
    last_q = hold([far_q[-1]], [mixed[0]])
    mixed[far[-1]] = attend(last_q, [(0, None)])[0]
    back = {s: to_block(mixed[s], s) for s in far + [1]}
    back[1] = hold([back[1]], effort=EFFORT_BACK)[0]
    back[1], back[far[0]] = hold([back[1], back[far[0]]], effort=EFFORT_BACK)
    back[0] = mixed[0]
    order = [0] + far + [1]
    back = [back[s] for s in order]
    return pl.pallas_call(
        functools.partial(unpack_kernel, order, part),
        out_shape=jax.ShapeDtypeStruct((1, tokens, width), kind),
        in_specs=[VMEM] * blocks,
        out_specs=HBM,
        scratch_shapes=[pltpu.SemaphoreType.DMA((blocks,))],
        compiler_params=SMALL,
        cost_estimate=pl.CostEstimate(
            flops=0, bytes_accessed=2 * tokens * width * 2, transcendentals=0
        ),
        name="unpack",
    )(*back)


def local(query_rows, key_rows, value_rows):
    blocks = lax.axis_size("blk")
    heads = query_rows.shape[2] // HD
    few = blocks == 4 and heads % blocks == 0
    plan = local_blocks if few else local_generic
    return plan(query_rows, key_rows, value_rows)


def solution(mesh):
    in_specs = (
        P("cfg", ("groups", "blk", "uly"), None),
        P("cfg", ("groups", "blk", "uly"), None),
        P("cfg", ("groups", "blk", "uly"), None),
    )
    out_specs = P("cfg", ("groups", "blk", "uly"), None)
    return jax.shard_map(local, mesh=mesh, in_specs=in_specs, out_specs=out_specs, check_vma=False)
```

```python
import functools
import math

import jax
import jax.numpy as jnp
from jax import lax
from jax.experimental import pallas as pl
from jax.experimental.pallas import tpu as pltpu
from jax.sharding import PartitionSpec as P

HD = 128
EFFORT = 0
EFFORT_OWN = 10**9
EFFORT_QUERIES = 2 * 10**8
EFFORT_NEAR = 0
EFFORT_FAR = (10**9, 5 * 10**8)
ANY = pl.BlockSpec(memory_space=pl.ANY)
HBM = pl.BlockSpec(memory_space=pltpu.HBM)
VMEM = pl.BlockSpec(memory_space=pltpu.VMEM)
SMALL = pltpu.CompilerParams(vmem_limit_bytes=4 * 1024 * 1024)


def attend(queries, key_part, value_part):
    query_mat = queries[0, :, 0]
    row_count, head_count, head_size = query_mat.shape
    score_scale = 1.0 / math.sqrt(head_size)
    start_state = (
        jnp.full((head_count, row_count), -1e30, jnp.float32),
        jnp.zeros((head_count, row_count), jnp.float32),
        jnp.zeros((row_count, head_count, head_size), jnp.float32),
    )

    def absorb(state, pieces):
        key_piece = pieces[0][0, :, 0]
        value_piece = pieces[1][0, :, 0]
        scores = (
            jnp.einsum("qhd,khd->hqk", query_mat, key_piece, preferred_element_type=jnp.float32)
            * score_scale
        )
        running, totals, accumulated = state
        new_max = jnp.maximum(running, jnp.max(scores, axis=2))
        weights = jnp.exp(scores - new_max[:, :, None])
        factor = jnp.exp(running - new_max)
        totals = totals * factor + jnp.sum(weights, axis=2)
        probabilities = weights.astype(jnp.bfloat16)
        contrib = jnp.einsum(
            "hqk,khd->qhd", probabilities, value_piece, preferred_element_type=jnp.float32
        )
        accumulated = accumulated * factor.T[:, :, None] + contrib
        return (new_max, totals, accumulated)

    whole_keys, whole_values = (
        lax.all_gather(key_part, "blk", axis=1, tiled=True),
        lax.all_gather(value_part, "blk", axis=1, tiled=True),
    )
    key_count = whole_keys.shape[1]
    block_rows = math.gcd(key_count, 1024)

    def one_block(state, counter):
        offset = counter * block_rows
        key_block = lax.dynamic_slice_in_dim(whole_keys, offset, block_rows, 1)
        value_block = lax.dynamic_slice_in_dim(whole_values, offset, block_rows, 1)
        return (absorb(state, (key_block, value_block)), None)

    result, unused = lax.scan(
        one_block, start_state, jnp.arange(key_count // block_rows, dtype=jnp.int32)
    )
    output = (result[2] / result[1].T[:, :, None]).astype(jnp.bfloat16)
    return output.reshape(1, row_count, 1, head_count, head_size)


def local_generic(query_rows, key_rows, value_rows):
    ulysses = lax.axis_size("uly")
    tokens = query_rows.shape[1]
    width = query_rows.shape[2]
    heads_local = width // HD // ulysses

    def split_heads(array):
        array = array.reshape(1, tokens, ulysses, heads_local, HD)
        return lax.all_to_all(array, "uly", split_axis=2, concat_axis=1, tiled=True)

    mixed = attend(split_heads(query_rows), split_heads(key_rows), split_heads(value_rows))
    merged = lax.all_to_all(mixed, "uly", split_axis=1, concat_axis=2, tiled=True)
    return merged.reshape(1, tokens, width)


def run_copies(pairs, sems):
    started = [pltpu.make_async_copy(src, dst, sems.at[at]) for at, (src, dst) in enumerate(pairs)]
    for copy in started:
        copy.start()
    for copy in started:
        copy.wait()


def pack_kernel(messages, part, q_ref, k_ref, v_ref, *refs):
    outs, sems = refs[:-1], refs[-1]
    sources = {"q": q_ref, "k": k_ref, "v": v_ref}
    me = lax.axis_index("blk")
    pairs = []
    for (s, pieces), out in zip(messages, outs):
        start = 0
        for name, first, lanes in pieces:
            columns = pl.ds(pl.multiple_of((me ^ s) * part + first, 128), lanes)
            pairs.append((sources[name].at[0, :, columns], out.at[:, pl.ds(start, lanes)]))
            start += lanes
    run_copies(pairs, sems)


def join_kernel(pieces, *refs):
    lanes = refs[-1].shape[2]
    for at, (source, start) in enumerate(pieces):
        refs[-1][at] = refs[source][:, start : start + lanes]


def join(arrays, starts, lanes, effort=0, after=()):
    shape = (len(arrays), arrays[0].shape[0], lanes)
    return pl.pallas_call(
        functools.partial(join_kernel, list(enumerate(starts))),
        out_shape=jax.ShapeDtypeStruct(shape, arrays[0].dtype),
        in_specs=[VMEM] * (len(arrays) + len(after)),
        out_specs=VMEM,
        compiler_params=SMALL,
        cost_estimate=pl.CostEstimate(
            flops=effort, bytes_accessed=4 * math.prod(shape), transcendentals=0
        ),
        name="join",
    )(*arrays, *after)


def hold_kernel(*refs):
    pass


def hold(arrays, until=(), effort=0):
    return pl.pallas_call(
        hold_kernel,
        out_shape=[jax.ShapeDtypeStruct(array.shape, array.dtype) for array in arrays],
        in_specs=[ANY] * (len(arrays) + len(until)),
        out_specs=[ANY] * len(arrays),
        input_output_aliases={at: at for at in range(len(arrays))},
        compiler_params=SMALL,
        cost_estimate=pl.CostEstimate(flops=effort, bytes_accessed=0, transcendentals=0),
        name="hold",
    )(*arrays, *until)


def attend_kernel(held, keys, queries, *refs):
    key_refs, query_refs, out_refs = refs[:held], refs[held : -len(queries)], refs[-len(queries) :]
    tokens, part = out_refs[0].shape
    scale = 1.0 / math.sqrt(HD)

    def rows(sources, places, first):
        lanes = slice(first, first + HD)
        pieces = [
            sources[at][:, lanes] if row is None else sources[at][row, :, lanes]
            for at, row in places
        ]
        return jnp.concatenate(pieces, axis=0)

    lanes = range(0, part, HD)
    scores = [
        lax.dot_general(
            rows(query_refs, queries, lane),
            rows(key_refs, keys, lane),
            (((1,), (1,)), ((), ())),
            preferred_element_type=jnp.float32,
        )
        * scale
        for lane in lanes
    ]
    weights = [jnp.exp(s - jnp.max(s, axis=1, keepdims=True)) for s in scores]
    mixed = [
        jnp.dot(
            w.astype(jnp.bfloat16),
            rows(key_refs, keys, part + lane),
            preferred_element_type=jnp.float32,
        )
        for w, lane in zip(weights, lanes)
    ]
    for w, m, lane in zip(weights, mixed, lanes):
        result = (m / jnp.sum(w, axis=1, keepdims=True)).astype(jnp.bfloat16)
        for block, ref in enumerate(out_refs):
            ref[:, lane : lane + HD] = result[block * tokens : (block + 1) * tokens]


def unpack_kernel(order, part, *refs):
    ins, out_ref, sems = refs[:-2], refs[-2], refs[-1]
    me = lax.axis_index("blk")
    pairs = []
    for s, ref in zip(order, ins):
        columns = pl.ds(pl.multiple_of((me ^ s) * part, 128), part)
        pairs.append((ref, out_ref.at[0, :, columns]))
    run_copies(pairs, sems)


def local_blocks(query_rows, key_rows, value_rows):
    blocks, columns_of = lax.axis_size("blk"), lax.axis_size("uly")
    tokens, width = query_rows.shape[1:]
    part = width // blocks
    heads = part // HD
    kind = query_rows.dtype
    far = list(range(blocks - 1, 1, -1))

    kv, q = (("k", 0, part), ("v", 0, part)), (("q", 0, part),)
    messages = [(s, kv) for s in far] + [(1, kv + q)] + [(s, q) for s in far] + [(0, kv), (0, q)]
    packed = pl.pallas_call(
        functools.partial(pack_kernel, messages, part),
        out_shape=[
            jax.ShapeDtypeStruct((tokens, sum(piece[2] for piece in pieces)), kind)
            for s, pieces in messages
        ],
        in_specs=[HBM] * 3,
        out_specs=[VMEM] * len(messages),
        scratch_shapes=[pltpu.SemaphoreType.DMA((sum(len(m[1]) for m in messages),))],
        compiler_params=SMALL,
        cost_estimate=pl.CostEstimate(
            flops=0, bytes_accessed=6 * tokens * width * 2, transcendentals=0
        ),
        name="pack",
    )(*[pltpu.with_memory_space_constraint(x, pltpu.HBM) for x in (query_rows, key_rows, value_rows)])

    def to_block(array, s):
        return lax.ppermute(array, "blk", [(i, i ^ s) for i in range(blocks)])

    def to_column(array, t):
        return lax.ppermute(array, "uly", [(i, (i + t) % columns_of) for i in range(columns_of)])

    sent = {message: array for message, array in zip(messages, packed)}
    own_kv, own_q = packed[-2:]
    far_kv = [to_block(sent[s, kv], s) for s in far[::-1]]
    near_kvq = to_block(sent[1, kv + q], 1)
    far_kv = [hold([array], (), effort)[0] for array, effort in zip(far_kv, EFFORT_FAR)]
    near_kv = join([near_kvq], [0], 2 * part, EFFORT_NEAR)
    far_q = [to_block(sent[far[0], q], far[0])]
    far_q += [to_block(hold([sent[s, q]], [array])[0], s) for s, array in zip(far[1:], far_kv[1:])]
    own_kv_x, first_x, near_x, second_x = (
        [to_column(group, t) for t in range(1, columns_of)]
        for group in (own_kv, far_kv[0], near_kv[0], far_kv[1])
    )
    own_kv_x = hold(own_kv_x, effort=EFFORT_OWN)
    near_q = join([own_q, near_kvq], [0, 2 * part], part)
    far_q[:1] = hold(far_q[:1], [*own_kv_x, *first_x, *near_x], EFFORT)
    far_q[:1] = hold(far_q[:1], (), EFFORT_QUERIES)

    holders = [near_kvq, own_kv, *far_kv, *own_kv_x, *first_x, *near_x, *second_x]
    keys = [(at, None) for at in range(len(holders))]

    def attend(query_arrays, query_places):
        rows = tokens * len(query_places)
        pairs = heads * rows * tokens * len(keys)
        return pl.pallas_call(
            functools.partial(attend_kernel, len(holders), keys, query_places),
            out_shape=[jax.ShapeDtypeStruct((tokens, part), kind)] * len(query_places),
            in_specs=[VMEM] * (len(holders) + len(query_arrays)),
            out_specs=[VMEM] * len(query_places),
            compiler_params=pltpu.CompilerParams(vmem_limit_bytes=24 * 1024 * 1024),
            cost_estimate=pl.CostEstimate(
                flops=4 * HD * pairs,
                bytes_accessed=4 * part * (rows + tokens * len(keys)),
                transcendentals=pairs,
            ),
            name="attend",
        )(*holders, *query_arrays)

    mixed = dict(zip([0, 1] + far[:-1], attend([near_q] + far_q[:-1], [(0, 0), (0, 1), (1, None)])))
    last_q = hold([far_q[-1]], [mixed[0]])
    mixed[far[-1]] = attend(last_q, [(0, None)])[0]
    mixed[1] = hold([mixed[1]], [mixed[far[-1]]])[0]
    back = {s: to_block(mixed[s], s) for s in far + [1]}
    early = far[:-1]
    back.update(zip(early, hold([back[s] for s in early], effort=EFFORT)))
    back[0] = mixed[0]
    order = [0] + far + [1]
    back = [back[s] for s in order]
    return pl.pallas_call(
        functools.partial(unpack_kernel, order, part),
        out_shape=jax.ShapeDtypeStruct((1, tokens, width), kind),
        in_specs=[VMEM] * blocks,
        out_specs=HBM,
        scratch_shapes=[pltpu.SemaphoreType.DMA((blocks,))],
        compiler_params=SMALL,
        cost_estimate=pl.CostEstimate(
            flops=0, bytes_accessed=2 * tokens * width * 2, transcendentals=0
        ),
        name="unpack",
    )(*back)


def local(query_rows, key_rows, value_rows):
    blocks = lax.axis_size("blk")
    heads = query_rows.shape[2] // HD
    few = blocks == 4 and heads % blocks == 0
    plan = local_blocks if few else local_generic
    return plan(query_rows, key_rows, value_rows)


def solution(mesh):
    in_specs = (
        P("cfg", ("groups", "blk", "uly"), None),
        P("cfg", ("groups", "blk", "uly"), None),
        P("cfg", ("groups", "blk", "uly"), None),
    )
    out_specs = P("cfg", ("groups", "blk", "uly"), None)
    return jax.shard_map(local, mesh=mesh, in_specs=in_specs, out_specs=out_specs, check_vma=False)
```

```python
import functools
import math

import jax
import jax.numpy as jnp
from jax import lax
from jax.experimental import pallas as pl
from jax.experimental.pallas import tpu as pltpu
from jax.sharding import PartitionSpec as P

HD = 128
EFFORT_BACK = 10**9
EFFORT_OWN = 10**9
EFFORT_QUERIES = 2 * 10**8
EFFORT_NEAR = 0
EFFORT_FAR = (10**9, 5 * 10**8)
ANY = pl.BlockSpec(memory_space=pl.ANY)
HBM = pl.BlockSpec(memory_space=pltpu.HBM)
VMEM = pl.BlockSpec(memory_space=pltpu.VMEM)
SMALL = pltpu.CompilerParams(vmem_limit_bytes=4 * 1024 * 1024)


def attend(queries, key_part, value_part):
    query_mat = queries[0, :, 0]
    row_count, head_count, head_size = query_mat.shape
    score_scale = 1.0 / math.sqrt(head_size)
    start_state = (
        jnp.full((head_count, row_count), -1e30, jnp.float32),
        jnp.zeros((head_count, row_count), jnp.float32),
        jnp.zeros((row_count, head_count, head_size), jnp.float32),
    )

    def absorb(state, pieces):
        key_piece = pieces[0][0, :, 0]
        value_piece = pieces[1][0, :, 0]
        scores = (
            jnp.einsum("qhd,khd->hqk", query_mat, key_piece, preferred_element_type=jnp.float32)
            * score_scale
        )
        running, totals, accumulated = state
        new_max = jnp.maximum(running, jnp.max(scores, axis=2))
        weights = jnp.exp(scores - new_max[:, :, None])
        factor = jnp.exp(running - new_max)
        totals = totals * factor + jnp.sum(weights, axis=2)
        probabilities = weights.astype(jnp.bfloat16)
        contrib = jnp.einsum(
            "hqk,khd->qhd", probabilities, value_piece, preferred_element_type=jnp.float32
        )
        accumulated = accumulated * factor.T[:, :, None] + contrib
        return (new_max, totals, accumulated)

    whole_keys, whole_values = (
        lax.all_gather(key_part, "blk", axis=1, tiled=True),
        lax.all_gather(value_part, "blk", axis=1, tiled=True),
    )
    key_count = whole_keys.shape[1]
    block_rows = math.gcd(key_count, 1024)

    def one_block(state, counter):
        offset = counter * block_rows
        key_block = lax.dynamic_slice_in_dim(whole_keys, offset, block_rows, 1)
        value_block = lax.dynamic_slice_in_dim(whole_values, offset, block_rows, 1)
        return (absorb(state, (key_block, value_block)), None)

    result, unused = lax.scan(
        one_block, start_state, jnp.arange(key_count // block_rows, dtype=jnp.int32)
    )
    output = (result[2] / result[1].T[:, :, None]).astype(jnp.bfloat16)
    return output.reshape(1, row_count, 1, head_count, head_size)


def local_generic(query_rows, key_rows, value_rows):
    ulysses = lax.axis_size("uly")
    tokens = query_rows.shape[1]
    width = query_rows.shape[2]
    heads_local = width // HD // ulysses

    def split_heads(array):
        array = array.reshape(1, tokens, ulysses, heads_local, HD)
        return lax.all_to_all(array, "uly", split_axis=2, concat_axis=1, tiled=True)

    mixed = attend(split_heads(query_rows), split_heads(key_rows), split_heads(value_rows))
    merged = lax.all_to_all(mixed, "uly", split_axis=1, concat_axis=2, tiled=True)
    return merged.reshape(1, tokens, width)


def run_copies(pairs, sems):
    started = [pltpu.make_async_copy(src, dst, sems.at[at]) for at, (src, dst) in enumerate(pairs)]
    for copy in started:
        copy.start()
    for copy in started:
        copy.wait()


def pack_kernel(messages, part, q_ref, k_ref, v_ref, *refs):
    outs, sems = refs[:-1], refs[-1]
    sources = {"q": q_ref, "k": k_ref, "v": v_ref}
    me = lax.axis_index("blk")
    pairs = []
    for (s, pieces), out in zip(messages, outs):
        start = 0
        for name, first, lanes in pieces:
            columns = pl.ds(pl.multiple_of((me ^ s) * part + first, 128), lanes)
            pairs.append((sources[name].at[0, :, columns], out.at[:, pl.ds(start, lanes)]))
            start += lanes
    run_copies(pairs, sems)


def hold_kernel(*refs):
    pass


def hold(arrays, until=(), effort=0):
    return pl.pallas_call(
        hold_kernel,
        out_shape=[jax.ShapeDtypeStruct(array.shape, array.dtype) for array in arrays],
        in_specs=[ANY] * (len(arrays) + len(until)),
        out_specs=[ANY] * len(arrays),
        input_output_aliases={at: at for at in range(len(arrays))},
        compiler_params=SMALL,
        cost_estimate=pl.CostEstimate(flops=effort, bytes_accessed=0, transcendentals=0),
        name="hold",
    )(*arrays, *until)


def attend_kernel(held, keys, queries, *refs):
    key_refs, query_refs, out_refs = refs[:held], refs[held : -len(queries)], refs[-len(queries) :]
    tokens, part = out_refs[0].shape
    scale = 1.0 / math.sqrt(HD)

    def rows(sources, places, first):
        lanes = slice(first, first + HD)
        pieces = [
            sources[at][:, lanes] if row is None else sources[at][row, :, lanes]
            for at, row in places
        ]
        return jnp.concatenate(pieces, axis=0)

    lanes = range(0, part, HD)
    scores = [
        lax.dot_general(
            rows(query_refs, queries, lane),
            rows(key_refs, keys, lane),
            (((1,), (1,)), ((), ())),
            preferred_element_type=jnp.float32,
        )
        * scale
        for lane in lanes
    ]
    weights = [jnp.exp(s - jnp.max(s, axis=1, keepdims=True)) for s in scores]
    mixed = [
        jnp.dot(
            w.astype(jnp.bfloat16),
            rows(key_refs, keys, part + lane),
            preferred_element_type=jnp.float32,
        )
        for w, lane in zip(weights, lanes)
    ]
    for w, m, lane in zip(weights, mixed, lanes):
        result = (m / jnp.sum(w, axis=1, keepdims=True)).astype(jnp.bfloat16)
        for block, ref in enumerate(out_refs):
            ref[:, lane : lane + HD] = result[block * tokens : (block + 1) * tokens]


def unpack_kernel(order, part, *refs):
    ins, out_ref, sems = refs[:-2], refs[-2], refs[-1]
    me = lax.axis_index("blk")
    pairs = []
    for s, ref in zip(order, ins):
        columns = pl.ds(pl.multiple_of((me ^ s) * part, 128), part)
        pairs.append((ref, out_ref.at[0, :, columns]))
    run_copies(pairs, sems)


def local_blocks(query_rows, key_rows, value_rows):
    blocks, columns_of = lax.axis_size("blk"), lax.axis_size("uly")
    tokens, width = query_rows.shape[1:]
    part = width // blocks
    heads = part // HD
    kind = query_rows.dtype
    far = list(range(blocks - 1, 1, -1))

    kv, q = (("k", 0, part), ("v", 0, part)), (("q", 0, part),)
    messages = [(s, names) for names in (kv, q) for s in far + [1, 0]]
    packed = pl.pallas_call(
        functools.partial(pack_kernel, messages, part),
        out_shape=[
            jax.ShapeDtypeStruct((tokens, sum(piece[2] for piece in pieces)), kind)
            for s, pieces in messages
        ],
        in_specs=[HBM] * 3,
        out_specs=[VMEM] * len(messages),
        scratch_shapes=[pltpu.SemaphoreType.DMA((sum(len(m[1]) for m in messages),))],
        compiler_params=SMALL,
        cost_estimate=pl.CostEstimate(
            flops=0, bytes_accessed=6 * tokens * width * 2, transcendentals=0
        ),
        name="pack",
    )(*[pltpu.with_memory_space_constraint(x, pltpu.HBM) for x in (query_rows, key_rows, value_rows)])

    def to_block(array, s):
        return lax.ppermute(array, "blk", [(i, i ^ s) for i in range(blocks)])

    def to_column(array, t):
        return lax.ppermute(array, "uly", [(i, (i + t) % columns_of) for i in range(columns_of)])

    sent = {message: array for message, array in zip(messages, packed)}
    own_kv, own_q = sent[0, kv], sent[0, q]
    far_kv = [to_block(sent[s, kv], s) for s in far]
    far_kv = [hold([array], (), effort)[0] for array, effort in zip(far_kv, EFFORT_FAR)]
    near_q = to_block(sent[1, q], 1)
    near_kv = hold([to_block(sent[1, kv], 1)], [far_kv[0], near_q], EFFORT_NEAR)[0]

    own_kv_x, first_x, near_x, second_x = (
        [to_column(group, t) for t in range(1, columns_of)]
        for group in (own_kv, far_kv[0], near_kv, far_kv[1])
    )
    own_kv_x = hold(own_kv_x, effort=EFFORT_OWN)
    early_q = hold([to_block(sent[far[0], q], far[0]), near_q], [*own_kv_x, *first_x, *near_x], EFFORT_QUERIES)
    second_q = to_block(hold([sent[far[1], q]], far_kv[1:])[0], far[1])

    holders = [near_kv, own_kv, *far_kv, *own_kv_x, *first_x, *near_x, *second_x]
    keys = [(at, None) for at in range(len(holders))]

    def attend(query_arrays, query_places):
        rows = tokens * len(query_places)
        pairs = heads * rows * tokens * len(keys)
        return pl.pallas_call(
            functools.partial(attend_kernel, len(holders), keys, query_places),
            out_shape=[jax.ShapeDtypeStruct((tokens, part), kind)] * len(query_places),
            in_specs=[VMEM] * (len(holders) + len(query_arrays)),
            out_specs=[VMEM] * len(query_places),
            compiler_params=pltpu.CompilerParams(vmem_limit_bytes=24 * 1024 * 1024),
            cost_estimate=pl.CostEstimate(
                flops=4 * HD * pairs,
                bytes_accessed=4 * part * (rows + tokens * len(keys)),
                transcendentals=pairs,
            ),
            name="attend",
        )(*holders, *query_arrays)

    places = [(at, None) for at in range(3)]
    mixed = dict(zip((0, far[0], 1), attend([own_q, *early_q], places)))
    mixed[far[1]] = attend(hold([second_q], [mixed[0]]), places[:1])[0]
    mixed[1] = hold([mixed[1]], [mixed[far[1]]])[0]
    back = {s: to_block(mixed[s], s) for s in far + [1]}
    early = far[:-1]
    back.update(zip(early, hold([back[s] for s in early], effort=EFFORT_BACK)))
    back[0] = mixed[0]
    order = [0] + far + [1]
    back = [back[s] for s in order]
    return pl.pallas_call(
        functools.partial(unpack_kernel, order, part),
        out_shape=jax.ShapeDtypeStruct((1, tokens, width), kind),
        in_specs=[VMEM] * blocks,
        out_specs=HBM,
        scratch_shapes=[pltpu.SemaphoreType.DMA((blocks,))],
        compiler_params=SMALL,
        cost_estimate=pl.CostEstimate(
            flops=0, bytes_accessed=2 * tokens * width * 2, transcendentals=0
        ),
        name="unpack",
    )(*back)


def local(query_rows, key_rows, value_rows):
    blocks = lax.axis_size("blk")
    heads = query_rows.shape[2] // HD
    few = blocks == 4 and heads % blocks == 0
    plan = local_blocks if few else local_generic
    return plan(query_rows, key_rows, value_rows)


def solution(mesh):
    in_specs = (
        P("cfg", ("groups", "blk", "uly"), None),
        P("cfg", ("groups", "blk", "uly"), None),
        P("cfg", ("groups", "blk", "uly"), None),
    )
    out_specs = P("cfg", ("groups", "blk", "uly"), None)
    return jax.shard_map(local, mesh=mesh, in_specs=in_specs, out_specs=out_specs, check_vma=False)
```

```python
import functools
import math

import jax
import jax.numpy as jnp
from jax import lax
from jax.experimental import pallas as pl
from jax.experimental.pallas import tpu as pltpu
from jax.sharding import PartitionSpec as P

HD = 128
EFFORT = 10**9
EFFORT_OWN = 3 * 10**8
EFFORT_NEAR = 0
EFFORT_FAR = (10**9, 2 * 10**9)
ANY = pl.BlockSpec(memory_space=pl.ANY)
HBM = pl.BlockSpec(memory_space=pltpu.HBM)
VMEM = pl.BlockSpec(memory_space=pltpu.VMEM)
SMALL = pltpu.CompilerParams(vmem_limit_bytes=4 * 1024 * 1024)


def attend(queries, key_part, value_part):
    query_mat = queries[0, :, 0]
    row_count, head_count, head_size = query_mat.shape
    score_scale = 1.0 / math.sqrt(head_size)
    start_state = (
        jnp.full((head_count, row_count), -1e30, jnp.float32),
        jnp.zeros((head_count, row_count), jnp.float32),
        jnp.zeros((row_count, head_count, head_size), jnp.float32),
    )

    def absorb(state, pieces):
        key_piece = pieces[0][0, :, 0]
        value_piece = pieces[1][0, :, 0]
        scores = (
            jnp.einsum("qhd,khd->hqk", query_mat, key_piece, preferred_element_type=jnp.float32)
            * score_scale
        )
        running, totals, accumulated = state
        new_max = jnp.maximum(running, jnp.max(scores, axis=2))
        weights = jnp.exp(scores - new_max[:, :, None])
        factor = jnp.exp(running - new_max)
        totals = totals * factor + jnp.sum(weights, axis=2)
        probabilities = weights.astype(jnp.bfloat16)
        contrib = jnp.einsum(
            "hqk,khd->qhd", probabilities, value_piece, preferred_element_type=jnp.float32
        )
        accumulated = accumulated * factor.T[:, :, None] + contrib
        return (new_max, totals, accumulated)

    whole_keys, whole_values = (
        lax.all_gather(key_part, "blk", axis=1, tiled=True),
        lax.all_gather(value_part, "blk", axis=1, tiled=True),
    )
    key_count = whole_keys.shape[1]
    block_rows = math.gcd(key_count, 1024)

    def one_block(state, counter):
        offset = counter * block_rows
        key_block = lax.dynamic_slice_in_dim(whole_keys, offset, block_rows, 1)
        value_block = lax.dynamic_slice_in_dim(whole_values, offset, block_rows, 1)
        return (absorb(state, (key_block, value_block)), None)

    result, unused = lax.scan(
        one_block, start_state, jnp.arange(key_count // block_rows, dtype=jnp.int32)
    )
    output = (result[2] / result[1].T[:, :, None]).astype(jnp.bfloat16)
    return output.reshape(1, row_count, 1, head_count, head_size)


def local_generic(query_rows, key_rows, value_rows):
    ulysses = lax.axis_size("uly")
    tokens = query_rows.shape[1]
    width = query_rows.shape[2]
    heads_local = width // HD // ulysses

    def split_heads(array):
        array = array.reshape(1, tokens, ulysses, heads_local, HD)
        return lax.all_to_all(array, "uly", split_axis=2, concat_axis=1, tiled=True)

    mixed = attend(split_heads(query_rows), split_heads(key_rows), split_heads(value_rows))
    merged = lax.all_to_all(mixed, "uly", split_axis=1, concat_axis=2, tiled=True)
    return merged.reshape(1, tokens, width)


def run_copies(pairs, sems):
    started = [pltpu.make_async_copy(src, dst, sems.at[at]) for at, (src, dst) in enumerate(pairs)]
    for copy in started:
        copy.start()
    for copy in started:
        copy.wait()


def pack_kernel(messages, part, q_ref, k_ref, v_ref, *refs):
    outs, sems = refs[:-1], refs[-1]
    sources = {"q": q_ref, "k": k_ref, "v": v_ref}
    me = lax.axis_index("blk")
    pairs = []
    for (s, pieces), out in zip(messages, outs):
        start = 0
        for name, first, lanes in pieces:
            columns = pl.ds(pl.multiple_of((me ^ s) * part + first, 128), lanes)
            pairs.append((sources[name].at[0, :, columns], out.at[:, pl.ds(start, lanes)]))
            start += lanes
    run_copies(pairs, sems)


def join_kernel(pieces, *refs):
    lanes = refs[-1].shape[2]
    for at, (source, start) in enumerate(pieces):
        refs[-1][at] = refs[source][:, start : start + lanes]


def join(arrays, starts, lanes, effort=0, after=()):
    shape = (len(arrays), arrays[0].shape[0], lanes)
    return pl.pallas_call(
        functools.partial(join_kernel, list(enumerate(starts))),
        out_shape=jax.ShapeDtypeStruct(shape, arrays[0].dtype),
        in_specs=[VMEM] * (len(arrays) + len(after)),
        out_specs=VMEM,
        compiler_params=SMALL,
        cost_estimate=pl.CostEstimate(
            flops=effort, bytes_accessed=4 * math.prod(shape), transcendentals=0
        ),
        name="join",
    )(*arrays, *after)


def hold_kernel(*refs):
    pass


def hold(arrays, until=(), effort=0):
    return pl.pallas_call(
        hold_kernel,
        out_shape=[jax.ShapeDtypeStruct(array.shape, array.dtype) for array in arrays],
        in_specs=[ANY] * (len(arrays) + len(until)),
        out_specs=[ANY] * len(arrays),
        input_output_aliases={at: at for at in range(len(arrays))},
        compiler_params=SMALL,
        cost_estimate=pl.CostEstimate(flops=effort, bytes_accessed=0, transcendentals=0),
        name="hold",
    )(*arrays, *until)


def attend_kernel(held, keys, queries, *refs):
    key_refs, query_refs, out_refs = refs[:held], refs[held : -len(queries)], refs[-len(queries) :]
    tokens, part = out_refs[0].shape
    scale = 1.0 / math.sqrt(HD)

    def rows(sources, places, first):
        lanes = slice(first, first + HD)
        pieces = [
            sources[at][:, lanes] if row is None else sources[at][row, :, lanes]
            for at, row in places
        ]
        return jnp.concatenate(pieces, axis=0)

    lanes = range(0, part, HD)
    scores = [
        lax.dot_general(
            rows(query_refs, queries, lane),
            rows(key_refs, keys, lane),
            (((1,), (1,)), ((), ())),
            preferred_element_type=jnp.float32,
        )
        * scale
        for lane in lanes
    ]
    weights = [jnp.exp(s - jnp.max(s, axis=1, keepdims=True)) for s in scores]
    mixed = [
        jnp.dot(
            w.astype(jnp.bfloat16),
            rows(key_refs, keys, part + lane),
            preferred_element_type=jnp.float32,
        )
        for w, lane in zip(weights, lanes)
    ]
    for w, m, lane in zip(weights, mixed, lanes):
        result = (m / jnp.sum(w, axis=1, keepdims=True)).astype(jnp.bfloat16)
        for block, ref in enumerate(out_refs):
            ref[:, lane : lane + HD] = result[block * tokens : (block + 1) * tokens]


def unpack_kernel(order, part, *refs):
    ins, out_ref, sems = refs[:-2], refs[-2], refs[-1]
    me = lax.axis_index("blk")
    pairs = []
    for s, ref in zip(order, ins):
        columns = pl.ds(pl.multiple_of((me ^ s) * part, 128), part)
        pairs.append((ref, out_ref.at[0, :, columns]))
    run_copies(pairs, sems)


def local_blocks(query_rows, key_rows, value_rows):
    blocks, columns_of = lax.axis_size("blk"), lax.axis_size("uly")
    tokens, width = query_rows.shape[1:]
    part = width // blocks
    heads = part // HD
    kind = query_rows.dtype
    far = list(range(blocks - 1, 1, -1))

    kv, q = (("k", 0, part), ("v", 0, part)), (("q", 0, part),)
    messages = [(s, kv) for s in far] + [(1, kv + q)] + [(s, q) for s in far] + [(0, kv), (0, q)]
    packed = pl.pallas_call(
        functools.partial(pack_kernel, messages, part),
        out_shape=[
            jax.ShapeDtypeStruct((tokens, sum(piece[2] for piece in pieces)), kind)
            for s, pieces in messages
        ],
        in_specs=[HBM] * 3,
        out_specs=[VMEM] * len(messages),
        scratch_shapes=[pltpu.SemaphoreType.DMA((sum(len(m[1]) for m in messages),))],
        compiler_params=SMALL,
        cost_estimate=pl.CostEstimate(
            flops=0, bytes_accessed=6 * tokens * width * 2, transcendentals=0
        ),
        name="pack",
    )(*[pltpu.with_memory_space_constraint(x, pltpu.HBM) for x in (query_rows, key_rows, value_rows)])

    def to_block(array, s):
        return lax.ppermute(array, "blk", [(i, i ^ s) for i in range(blocks)])

    def to_column(array, t):
        return lax.ppermute(array, "uly", [(i, (i + t) % columns_of) for i in range(columns_of)])

    sent = {message: array for message, array in zip(messages, packed)}
    own_kv, own_q = packed[-2:]
    far_kv = [to_block(sent[s, kv], s) for s in far]
    near_kvq = to_block(sent[1, kv + q], 1)
    far_kv = [hold([array], (), effort)[0] for array, effort in zip(far_kv, EFFORT_FAR)]
    near_kv = join([near_kvq], [0], 2 * part, EFFORT_NEAR)
    far_q = [to_block(hold([sent[s, q]], [array])[0], s) for s, array in zip(far, far_kv)]
    own_kv_x, first_x, near_x, second_x = (
        [to_column(group, t) for t in range(1, columns_of)]
        for group in (own_kv, far_kv[0], near_kv[0], far_kv[1])
    )
    own_kv_x = hold(own_kv_x, effort=EFFORT_OWN)
    near_q = join([own_q, near_kvq], [0, 2 * part], part)
    far_q[0] = join(far_q[:1], [0], part, EFFORT, [*own_kv_x, *first_x, *near_x])

    holders = [near_kvq, own_kv, *far_kv, *own_kv_x, *first_x, *near_x, *second_x]
    keys = [(at, None) for at in range(len(holders))]

    def attend(query_arrays, query_places):
        rows = tokens * len(query_places)
        pairs = heads * rows * tokens * len(keys)
        return pl.pallas_call(
            functools.partial(attend_kernel, len(holders), keys, query_places),
            out_shape=[jax.ShapeDtypeStruct((tokens, part), kind)] * len(query_places),
            in_specs=[VMEM] * (len(holders) + len(query_arrays)),
            out_specs=[VMEM] * len(query_places),
            compiler_params=pltpu.CompilerParams(vmem_limit_bytes=24 * 1024 * 1024),
            cost_estimate=pl.CostEstimate(
                flops=4 * HD * pairs,
                bytes_accessed=4 * part * (rows + tokens * len(keys)),
                transcendentals=pairs,
            ),
            name="attend",
        )(*holders, *query_arrays)

    mixed = dict(zip([0, 1] + far[:-1], attend([near_q] + far_q[:-1], [(0, 0), (0, 1), (1, 0)])))
    last_q = hold([far_q[-1]], [mixed[0]])
    mixed[far[-1]] = attend(last_q, [(0, None)])[0]
    mixed[1] = hold([mixed[1]], [mixed[far[-1]]])[0]
    back = {s: to_block(mixed[s], s) for s in far + [1]}
    early = far[:-1]
    back.update(zip(early, hold([back[s] for s in early])))
    back[0] = mixed[0]
    order = [0] + far + [1]
    back = [back[s] for s in order]
    return pl.pallas_call(
        functools.partial(unpack_kernel, order, part),
        out_shape=jax.ShapeDtypeStruct((1, tokens, width), kind),
        in_specs=[VMEM] * blocks,
        out_specs=HBM,
        scratch_shapes=[pltpu.SemaphoreType.DMA((blocks,))],
        compiler_params=SMALL,
        cost_estimate=pl.CostEstimate(
            flops=0, bytes_accessed=2 * tokens * width * 2, transcendentals=0
        ),
        name="unpack",
    )(*back)


def local(query_rows, key_rows, value_rows):
    blocks = lax.axis_size("blk")
    heads = query_rows.shape[2] // HD
    few = blocks == 4 and heads % blocks == 0
    plan = local_blocks if few else local_generic
    return plan(query_rows, key_rows, value_rows)


def solution(mesh):
    in_specs = (
        P("cfg", ("groups", "blk", "uly"), None),
        P("cfg", ("groups", "blk", "uly"), None),
        P("cfg", ("groups", "blk", "uly"), None),
    )
    out_specs = P("cfg", ("groups", "blk", "uly"), None)
    return jax.shard_map(local, mesh=mesh, in_specs=in_specs, out_specs=out_specs, check_vma=False)
```

```python
import functools
import math

import jax
import jax.numpy as jnp
from jax import lax
from jax.experimental import pallas as pl
from jax.experimental.pallas import tpu as pltpu
from jax.sharding import PartitionSpec as P

HD = 128
EFFORT = 0
EFFORT_OWN = 10**9
EFFORT_QUERIES = 2 * 10**8
EFFORT_NEAR = 0
EFFORT_FAR = (10**9, 5 * 10**8)
ANY = pl.BlockSpec(memory_space=pl.ANY)
HBM = pl.BlockSpec(memory_space=pltpu.HBM)
VMEM = pl.BlockSpec(memory_space=pltpu.VMEM)
SMALL = pltpu.CompilerParams(vmem_limit_bytes=4 * 1024 * 1024)


def attend(queries, key_part, value_part):
    query_mat = queries[0, :, 0]
    row_count, head_count, head_size = query_mat.shape
    score_scale = 1.0 / math.sqrt(head_size)
    start_state = (
        jnp.full((head_count, row_count), -1e30, jnp.float32),
        jnp.zeros((head_count, row_count), jnp.float32),
        jnp.zeros((row_count, head_count, head_size), jnp.float32),
    )

    def absorb(state, pieces):
        key_piece = pieces[0][0, :, 0]
        value_piece = pieces[1][0, :, 0]
        scores = (
            jnp.einsum("qhd,khd->hqk", query_mat, key_piece, preferred_element_type=jnp.float32)
            * score_scale
        )
        running, totals, accumulated = state
        new_max = jnp.maximum(running, jnp.max(scores, axis=2))
        weights = jnp.exp(scores - new_max[:, :, None])
        factor = jnp.exp(running - new_max)
        totals = totals * factor + jnp.sum(weights, axis=2)
        probabilities = weights.astype(jnp.bfloat16)
        contrib = jnp.einsum(
            "hqk,khd->qhd", probabilities, value_piece, preferred_element_type=jnp.float32
        )
        accumulated = accumulated * factor.T[:, :, None] + contrib
        return (new_max, totals, accumulated)

    whole_keys, whole_values = (
        lax.all_gather(key_part, "blk", axis=1, tiled=True),
        lax.all_gather(value_part, "blk", axis=1, tiled=True),
    )
    key_count = whole_keys.shape[1]
    block_rows = math.gcd(key_count, 1024)

    def one_block(state, counter):
        offset = counter * block_rows
        key_block = lax.dynamic_slice_in_dim(whole_keys, offset, block_rows, 1)
        value_block = lax.dynamic_slice_in_dim(whole_values, offset, block_rows, 1)
        return (absorb(state, (key_block, value_block)), None)

    result, unused = lax.scan(
        one_block, start_state, jnp.arange(key_count // block_rows, dtype=jnp.int32)
    )
    output = (result[2] / result[1].T[:, :, None]).astype(jnp.bfloat16)
    return output.reshape(1, row_count, 1, head_count, head_size)


def local_generic(query_rows, key_rows, value_rows):
    ulysses = lax.axis_size("uly")
    tokens = query_rows.shape[1]
    width = query_rows.shape[2]
    heads_local = width // HD // ulysses

    def split_heads(array):
        array = array.reshape(1, tokens, ulysses, heads_local, HD)
        return lax.all_to_all(array, "uly", split_axis=2, concat_axis=1, tiled=True)

    mixed = attend(split_heads(query_rows), split_heads(key_rows), split_heads(value_rows))
    merged = lax.all_to_all(mixed, "uly", split_axis=1, concat_axis=2, tiled=True)
    return merged.reshape(1, tokens, width)


def run_copies(pairs, sems):
    started = [pltpu.make_async_copy(src, dst, sems.at[at]) for at, (src, dst) in enumerate(pairs)]
    for copy in started:
        copy.start()
    for copy in started:
        copy.wait()


def pack_kernel(messages, part, q_ref, k_ref, v_ref, *refs):
    outs, sems = refs[:-1], refs[-1]
    sources = {"q": q_ref, "k": k_ref, "v": v_ref}
    me = lax.axis_index("blk")
    pairs = []
    for (s, pieces), out in zip(messages, outs):
        start = 0
        for name, first, lanes in pieces:
            columns = pl.ds(pl.multiple_of((me ^ s) * part + first, 128), lanes)
            pairs.append((sources[name].at[0, :, columns], out.at[:, pl.ds(start, lanes)]))
            start += lanes
    run_copies(pairs, sems)


def join_kernel(pieces, *refs):
    lanes = refs[-1].shape[2]
    for at, (source, start) in enumerate(pieces):
        refs[-1][at] = refs[source][:, start : start + lanes]


def join(arrays, starts, lanes, effort=0, after=()):
    shape = (len(arrays), arrays[0].shape[0], lanes)
    return pl.pallas_call(
        functools.partial(join_kernel, list(enumerate(starts))),
        out_shape=jax.ShapeDtypeStruct(shape, arrays[0].dtype),
        in_specs=[VMEM] * (len(arrays) + len(after)),
        out_specs=VMEM,
        compiler_params=SMALL,
        cost_estimate=pl.CostEstimate(
            flops=effort, bytes_accessed=4 * math.prod(shape), transcendentals=0
        ),
        name="join",
    )(*arrays, *after)


def hold_kernel(*refs):
    pass


def hold(arrays, until=(), effort=0):
    return pl.pallas_call(
        hold_kernel,
        out_shape=[jax.ShapeDtypeStruct(array.shape, array.dtype) for array in arrays],
        in_specs=[ANY] * (len(arrays) + len(until)),
        out_specs=[ANY] * len(arrays),
        input_output_aliases={at: at for at in range(len(arrays))},
        compiler_params=SMALL,
        cost_estimate=pl.CostEstimate(flops=effort, bytes_accessed=0, transcendentals=0),
        name="hold",
    )(*arrays, *until)


def attend_kernel(held, keys, queries, *refs):
    key_refs, query_refs, out_refs = refs[:held], refs[held : -len(queries)], refs[-len(queries) :]
    tokens, part = out_refs[0].shape
    scale = 1.0 / math.sqrt(HD)

    def rows(sources, places, first):
        lanes = slice(first, first + HD)
        pieces = [
            sources[at][:, lanes] if row is None else sources[at][row, :, lanes]
            for at, row in places
        ]
        return jnp.concatenate(pieces, axis=0)

    lanes = range(0, part, HD)
    scores = [
        lax.dot_general(
            rows(query_refs, queries, lane),
            rows(key_refs, keys, lane),
            (((1,), (1,)), ((), ())),
            preferred_element_type=jnp.float32,
        )
        * scale
        for lane in lanes
    ]
    weights = [jnp.exp(s - jnp.max(s, axis=1, keepdims=True)) for s in scores]
    mixed = [
        jnp.dot(
            w.astype(jnp.bfloat16),
            rows(key_refs, keys, part + lane),
            preferred_element_type=jnp.float32,
        )
        for w, lane in zip(weights, lanes)
    ]
    for w, m, lane in zip(weights, mixed, lanes):
        result = (m / jnp.sum(w, axis=1, keepdims=True)).astype(jnp.bfloat16)
        for block, ref in enumerate(out_refs):
            ref[:, lane : lane + HD] = result[block * tokens : (block + 1) * tokens]


def unpack_kernel(order, part, *refs):
    ins, out_ref, sems = refs[:-2], refs[-2], refs[-1]
    me = lax.axis_index("blk")
    pairs = []
    for s, ref in zip(order, ins):
        columns = pl.ds(pl.multiple_of((me ^ s) * part, 128), part)
        pairs.append((ref, out_ref.at[0, :, columns]))
    run_copies(pairs, sems)


def local_blocks(query_rows, key_rows, value_rows):
    blocks, columns_of = lax.axis_size("blk"), lax.axis_size("uly")
    tokens, width = query_rows.shape[1:]
    part = width // blocks
    heads = part // HD
    kind = query_rows.dtype
    far = list(range(blocks - 1, 1, -1))

    kv, q = (("k", 0, part), ("v", 0, part)), (("q", 0, part),)
    messages = [(s, kv) for s in far] + [(1, kv + q)] + [(s, q) for s in far] + [(0, kv), (0, q)]
    inputs = [pltpu.with_memory_space_constraint(x, pltpu.HBM) for x in (query_rows, key_rows, value_rows)]

    def pack(cut):
        copies = sum(len(names) for s, names in cut)
        size = 2 * tokens * part * copies
        return pl.pallas_call(
            functools.partial(pack_kernel, cut, part),
            out_shape=[
                jax.ShapeDtypeStruct((tokens, sum(piece[2] for piece in names)), kind)
                for s, names in cut
            ],
            in_specs=[HBM] * 3,
            out_specs=[VMEM] * len(cut),
            scratch_shapes=[pltpu.SemaphoreType.DMA((copies,))],
            compiler_params=SMALL,
            cost_estimate=pl.CostEstimate(flops=0, bytes_accessed=2 * size, transcendentals=0),
            name="pack",
        )(*inputs)

    first = len(far) + 1
    packed = [*pack(messages[:first]), *pack(messages[first:])]

    def to_block(array, s):
        return lax.ppermute(array, "blk", [(i, i ^ s) for i in range(blocks)])

    def to_column(array, t):
        return lax.ppermute(array, "uly", [(i, (i + t) % columns_of) for i in range(columns_of)])

    sent = {message: array for message, array in zip(messages, packed)}
    own_kv, own_q = packed[-2:]
    far_kv = [to_block(sent[s, kv], s) for s in far]
    near_kvq = to_block(sent[1, kv + q], 1)
    far_kv = [hold([array], (), effort)[0] for array, effort in zip(far_kv, EFFORT_FAR)]
    near_kv = join([near_kvq], [0], 2 * part, EFFORT_NEAR)
    far_q = [to_block(sent[far[0], q], far[0])]
    far_q += [to_block(hold([sent[s, q]], [array])[0], s) for s, array in zip(far[1:], far_kv[1:])]
    own_kv_x, first_x, near_x, second_x = (
        [to_column(group, t) for t in range(1, columns_of)]
        for group in (own_kv, far_kv[0], near_kv[0], far_kv[1])
    )
    own_kv_x = hold(own_kv_x, effort=EFFORT_OWN)
    near_q = join([own_q, near_kvq], [0, 2 * part], part)
    far_q[:1] = hold(far_q[:1], [*own_kv_x, *first_x, *near_x], EFFORT)
    far_q[:1] = hold(far_q[:1], (), EFFORT_QUERIES)

    holders = [near_kvq, own_kv, *far_kv, *own_kv_x, *first_x, *near_x, *second_x]
    keys = [(at, None) for at in range(len(holders))]

    def attend(query_arrays, query_places):
        rows = tokens * len(query_places)
        pairs = heads * rows * tokens * len(keys)
        return pl.pallas_call(
            functools.partial(attend_kernel, len(holders), keys, query_places),
            out_shape=[jax.ShapeDtypeStruct((tokens, part), kind)] * len(query_places),
            in_specs=[VMEM] * (len(holders) + len(query_arrays)),
            out_specs=[VMEM] * len(query_places),
            compiler_params=pltpu.CompilerParams(vmem_limit_bytes=24 * 1024 * 1024),
            cost_estimate=pl.CostEstimate(
                flops=4 * HD * pairs,
                bytes_accessed=4 * part * (rows + tokens * len(keys)),
                transcendentals=pairs,
            ),
            name="attend",
        )(*holders, *query_arrays)

    mixed = dict(zip([0, 1] + far[:-1], attend([near_q] + far_q[:-1], [(0, 0), (0, 1), (1, None)])))
    last_q = hold([far_q[-1]], [mixed[0]])
    mixed[far[-1]] = attend(last_q, [(0, None)])[0]
    mixed[1] = hold([mixed[1]], [mixed[far[-1]]])[0]
    back = {s: to_block(mixed[s], s) for s in far + [1]}
    early = far[:-1]
    back.update(zip(early, hold([back[s] for s in early], effort=EFFORT)))
    back[0] = mixed[0]
    order = [0] + far + [1]
    back = [back[s] for s in order]
    return pl.pallas_call(
        functools.partial(unpack_kernel, order, part),
        out_shape=jax.ShapeDtypeStruct((1, tokens, width), kind),
        in_specs=[VMEM] * blocks,
        out_specs=HBM,
        scratch_shapes=[pltpu.SemaphoreType.DMA((blocks,))],
        compiler_params=SMALL,
        cost_estimate=pl.CostEstimate(
            flops=0, bytes_accessed=2 * tokens * width * 2, transcendentals=0
        ),
        name="unpack",
    )(*back)


def local(query_rows, key_rows, value_rows):
    blocks = lax.axis_size("blk")
    heads = query_rows.shape[2] // HD
    few = blocks == 4 and heads % blocks == 0
    plan = local_blocks if few else local_generic
    return plan(query_rows, key_rows, value_rows)


def solution(mesh):
    in_specs = (
        P("cfg", ("groups", "blk", "uly"), None),
        P("cfg", ("groups", "blk", "uly"), None),
        P("cfg", ("groups", "blk", "uly"), None),
    )
    out_specs = P("cfg", ("groups", "blk", "uly"), None)
    return jax.shard_map(local, mesh=mesh, in_specs=in_specs, out_specs=out_specs, check_vma=False)
```

```python
import functools
import math

import jax
import jax.numpy as jnp
from jax import lax
from jax.experimental import pallas as pl
from jax.experimental.pallas import tpu as pltpu
from jax.sharding import PartitionSpec as P

HD = 128
EFFORT = 10**9
EFFORT_OWN = 3 * 10**8
EFFORT_NEAR = 0
EFFORT_FAR = (10**9, 2 * 10**9)
ANY = pl.BlockSpec(memory_space=pl.ANY)
HBM = pl.BlockSpec(memory_space=pltpu.HBM)
VMEM = pl.BlockSpec(memory_space=pltpu.VMEM)
SMALL = pltpu.CompilerParams(vmem_limit_bytes=4 * 1024 * 1024)


def attend(queries, key_part, value_part):
    query_mat = queries[0, :, 0]
    row_count, head_count, head_size = query_mat.shape
    score_scale = 1.0 / math.sqrt(head_size)
    start_state = (
        jnp.full((head_count, row_count), -1e30, jnp.float32),
        jnp.zeros((head_count, row_count), jnp.float32),
        jnp.zeros((row_count, head_count, head_size), jnp.float32),
    )

    def absorb(state, pieces):
        key_piece = pieces[0][0, :, 0]
        value_piece = pieces[1][0, :, 0]
        scores = (
            jnp.einsum("qhd,khd->hqk", query_mat, key_piece, preferred_element_type=jnp.float32)
            * score_scale
        )
        running, totals, accumulated = state
        new_max = jnp.maximum(running, jnp.max(scores, axis=2))
        weights = jnp.exp(scores - new_max[:, :, None])
        factor = jnp.exp(running - new_max)
        totals = totals * factor + jnp.sum(weights, axis=2)
        probabilities = weights.astype(jnp.bfloat16)
        contrib = jnp.einsum(
            "hqk,khd->qhd", probabilities, value_piece, preferred_element_type=jnp.float32
        )
        accumulated = accumulated * factor.T[:, :, None] + contrib
        return (new_max, totals, accumulated)

    whole_keys, whole_values = (
        lax.all_gather(key_part, "blk", axis=1, tiled=True),
        lax.all_gather(value_part, "blk", axis=1, tiled=True),
    )
    key_count = whole_keys.shape[1]
    block_rows = math.gcd(key_count, 1024)

    def one_block(state, counter):
        offset = counter * block_rows
        key_block = lax.dynamic_slice_in_dim(whole_keys, offset, block_rows, 1)
        value_block = lax.dynamic_slice_in_dim(whole_values, offset, block_rows, 1)
        return (absorb(state, (key_block, value_block)), None)

    result, unused = lax.scan(
        one_block, start_state, jnp.arange(key_count // block_rows, dtype=jnp.int32)
    )
    output = (result[2] / result[1].T[:, :, None]).astype(jnp.bfloat16)
    return output.reshape(1, row_count, 1, head_count, head_size)


def local_generic(query_rows, key_rows, value_rows):
    ulysses = lax.axis_size("uly")
    tokens = query_rows.shape[1]
    width = query_rows.shape[2]
    heads_local = width // HD // ulysses

    def split_heads(array):
        array = array.reshape(1, tokens, ulysses, heads_local, HD)
        return lax.all_to_all(array, "uly", split_axis=2, concat_axis=1, tiled=True)

    mixed = attend(split_heads(query_rows), split_heads(key_rows), split_heads(value_rows))
    merged = lax.all_to_all(mixed, "uly", split_axis=1, concat_axis=2, tiled=True)
    return merged.reshape(1, tokens, width)


def run_copies(pairs, sems):
    started = [pltpu.make_async_copy(src, dst, sems.at[at]) for at, (src, dst) in enumerate(pairs)]
    for copy in started:
        copy.start()
    for copy in started:
        copy.wait()


def pack_kernel(messages, part, q_ref, k_ref, v_ref, *refs):
    outs, sems = refs[:-1], refs[-1]
    sources = {"q": q_ref, "k": k_ref, "v": v_ref}
    me = lax.axis_index("blk")
    pairs = []
    for (s, pieces), out in zip(messages, outs):
        start = 0
        for name, first, lanes in pieces:
            columns = pl.ds(pl.multiple_of((me ^ s) * part + first, 128), lanes)
            pairs.append((sources[name].at[0, :, columns], out.at[:, pl.ds(start, lanes)]))
            start += lanes
    run_copies(pairs, sems)


def join_kernel(pieces, *refs):
    lanes = refs[-1].shape[2]
    for at, (source, start) in enumerate(pieces):
        refs[-1][at] = refs[source][:, start : start + lanes]


def join(arrays, starts, lanes, effort=0, after=()):
    shape = (len(arrays), arrays[0].shape[0], lanes)
    return pl.pallas_call(
        functools.partial(join_kernel, list(enumerate(starts))),
        out_shape=jax.ShapeDtypeStruct(shape, arrays[0].dtype),
        in_specs=[VMEM] * (len(arrays) + len(after)),
        out_specs=VMEM,
        compiler_params=SMALL,
        cost_estimate=pl.CostEstimate(
            flops=effort, bytes_accessed=4 * math.prod(shape), transcendentals=0
        ),
        name="join",
    )(*arrays, *after)


def hold_kernel(*refs):
    pass


def hold(arrays, until=(), effort=0):
    return pl.pallas_call(
        hold_kernel,
        out_shape=[jax.ShapeDtypeStruct(array.shape, array.dtype) for array in arrays],
        in_specs=[ANY] * (len(arrays) + len(until)),
        out_specs=[ANY] * len(arrays),
        input_output_aliases={at: at for at in range(len(arrays))},
        compiler_params=SMALL,
        cost_estimate=pl.CostEstimate(flops=effort, bytes_accessed=0, transcendentals=0),
        name="hold",
    )(*arrays, *until)


def attend_kernel(held, keys, queries, *refs):
    key_refs, query_refs, out_refs = refs[:held], refs[held : -len(queries)], refs[-len(queries) :]
    tokens, part = out_refs[0].shape
    scale = 1.0 / math.sqrt(HD)

    def rows(sources, places, first):
        lanes = slice(first, first + HD)
        pieces = [
            sources[at][:, lanes] if row is None else sources[at][row, :, lanes]
            for at, row in places
        ]
        return jnp.concatenate(pieces, axis=0)

    lanes = range(0, part, HD)
    scores = [
        lax.dot_general(
            rows(query_refs, queries, lane),
            rows(key_refs, keys, lane),
            (((1,), (1,)), ((), ())),
            preferred_element_type=jnp.float32,
        )
        * scale
        for lane in lanes
    ]
    weights = [jnp.exp(s - jnp.max(s, axis=1, keepdims=True)) for s in scores]
    mixed = [
        jnp.dot(
            w.astype(jnp.bfloat16),
            rows(key_refs, keys, part + lane),
            preferred_element_type=jnp.float32,
        )
        for w, lane in zip(weights, lanes)
    ]
    for w, m, lane in zip(weights, mixed, lanes):
        result = (m / jnp.sum(w, axis=1, keepdims=True)).astype(jnp.bfloat16)
        for block, ref in enumerate(out_refs):
            ref[:, lane : lane + HD] = result[block * tokens : (block + 1) * tokens]


def unpack_kernel(order, part, *refs):
    ins, out_ref, sems = refs[:-2], refs[-2], refs[-1]
    me = lax.axis_index("blk")
    pairs = []
    for s, ref in zip(order, ins):
        columns = pl.ds(pl.multiple_of((me ^ s) * part, 128), part)
        pairs.append((ref, out_ref.at[0, :, columns]))
    run_copies(pairs, sems)


def local_blocks(query_rows, key_rows, value_rows):
    blocks, columns_of = lax.axis_size("blk"), lax.axis_size("uly")
    tokens, width = query_rows.shape[1:]
    part = width // blocks
    heads = part // HD
    kind = query_rows.dtype
    far = list(range(blocks - 1, 1, -1))

    kv, q = (("k", 0, part), ("v", 0, part)), (("q", 0, part),)
    messages = [(s, kv) for s in far] + [(1, kv + q), (0, kv)] + [(s, q) for s in far + [0]]
    inputs = [pltpu.with_memory_space_constraint(x, pltpu.HBM) for x in (query_rows, key_rows, value_rows)]

    def pack(cut):
        copies = sum(len(names) for s, names in cut)
        size = 2 * tokens * part * copies
        return pl.pallas_call(
            functools.partial(pack_kernel, cut, part),
            out_shape=[
                jax.ShapeDtypeStruct((tokens, sum(piece[2] for piece in names)), kind)
                for s, names in cut
            ],
            in_specs=[HBM] * 3,
            out_specs=[VMEM] * len(cut),
            scratch_shapes=[pltpu.SemaphoreType.DMA((copies,))],
            compiler_params=SMALL,
            cost_estimate=pl.CostEstimate(flops=0, bytes_accessed=2 * size, transcendentals=0),
            name="pack",
        )(*inputs)

    first = len(far) + 2
    packed = [*pack(messages[:first]), *pack(messages[first:])]

    def to_block(array, s):
        return lax.ppermute(array, "blk", [(i, i ^ s) for i in range(blocks)])

    def to_column(array, t):
        return lax.ppermute(array, "uly", [(i, (i + t) % columns_of) for i in range(columns_of)])

    sent = {message: array for message, array in zip(messages, packed)}
    own_kv, own_q = sent[0, kv], sent[0, q]
    far_kv = [to_block(sent[s, kv], s) for s in far]
    near_kvq = to_block(sent[1, kv + q], 1)
    far_kv = [hold([array], (), effort)[0] for array, effort in zip(far_kv, EFFORT_FAR)]
    near_kv = join([near_kvq], [0], 2 * part, EFFORT_NEAR)
    far_q = [to_block(hold([sent[s, q]], [array])[0], s) for s, array in zip(far, far_kv)]
    own_kv_x, first_x, near_x, second_x = (
        [to_column(group, t) for t in range(1, columns_of)]
        for group in (own_kv, far_kv[0], near_kv[0], far_kv[1])
    )
    own_kv_x = hold(own_kv_x, effort=EFFORT_OWN)
    near_q = join([own_q, near_kvq], [0, 2 * part], part)
    far_q[0] = join(far_q[:1], [0], part, EFFORT, [*own_kv_x, *first_x, *near_x])

    holders = [near_kvq, own_kv, *far_kv, *own_kv_x, *first_x, *near_x, *second_x]
    keys = [(at, None) for at in range(len(holders))]

    def attend(query_arrays, query_places):
        rows = tokens * len(query_places)
        pairs = heads * rows * tokens * len(keys)
        return pl.pallas_call(
            functools.partial(attend_kernel, len(holders), keys, query_places),
            out_shape=[jax.ShapeDtypeStruct((tokens, part), kind)] * len(query_places),
            in_specs=[VMEM] * (len(holders) + len(query_arrays)),
            out_specs=[VMEM] * len(query_places),
            compiler_params=pltpu.CompilerParams(vmem_limit_bytes=24 * 1024 * 1024),
            cost_estimate=pl.CostEstimate(
                flops=4 * HD * pairs,
                bytes_accessed=4 * part * (rows + tokens * len(keys)),
                transcendentals=pairs,
            ),
            name="attend",
        )(*holders, *query_arrays)

    mixed = dict(zip([0, 1] + far[:-1], attend([near_q] + far_q[:-1], [(0, 0), (0, 1), (1, 0)])))
    last_q = hold([far_q[-1]], [mixed[0]])
    mixed[far[-1]] = attend(last_q, [(0, None)])[0]
    mixed[1] = hold([mixed[1]], [mixed[far[-1]]])[0]
    back = {s: to_block(mixed[s], s) for s in far + [1]}
    early = far[:-1]
    back.update(zip(early, hold([back[s] for s in early])))
    back[0] = mixed[0]
    order = [0] + far + [1]
    back = [back[s] for s in order]
    return pl.pallas_call(
        functools.partial(unpack_kernel, order, part),
        out_shape=jax.ShapeDtypeStruct((1, tokens, width), kind),
        in_specs=[VMEM] * blocks,
        out_specs=HBM,
        scratch_shapes=[pltpu.SemaphoreType.DMA((blocks,))],
        compiler_params=SMALL,
        cost_estimate=pl.CostEstimate(
            flops=0, bytes_accessed=2 * tokens * width * 2, transcendentals=0
        ),
        name="unpack",
    )(*back)


def local(query_rows, key_rows, value_rows):
    blocks = lax.axis_size("blk")
    heads = query_rows.shape[2] // HD
    few = blocks == 4 and heads % blocks == 0
    plan = local_blocks if few else local_generic
    return plan(query_rows, key_rows, value_rows)


def solution(mesh):
    in_specs = (
        P("cfg", ("groups", "blk", "uly"), None),
        P("cfg", ("groups", "blk", "uly"), None),
        P("cfg", ("groups", "blk", "uly"), None),
    )
    out_specs = P("cfg", ("groups", "blk", "uly"), None)
    return jax.shard_map(local, mesh=mesh, in_specs=in_specs, out_specs=out_specs, check_vma=False)
```

```python
import functools
import math

import jax
import jax.numpy as jnp
from jax import lax
from jax.experimental import pallas as pl
from jax.experimental.pallas import tpu as pltpu
from jax.sharding import PartitionSpec as P

HD = 128
EFFORT = 0
EFFORT_OWN = 10**9
EFFORT_QUERIES = 2 * 10**8
EFFORT_NEAR = 0
EFFORT_FAR = (53 * 10**7, 5 * 10**8)
ANY = pl.BlockSpec(memory_space=pl.ANY)
HBM = pl.BlockSpec(memory_space=pltpu.HBM)
VMEM = pl.BlockSpec(memory_space=pltpu.VMEM)
SMALL = pltpu.CompilerParams(vmem_limit_bytes=4 * 1024 * 1024)


def attend(queries, key_part, value_part):
    query_mat = queries[0, :, 0]
    row_count, head_count, head_size = query_mat.shape
    score_scale = 1.0 / math.sqrt(head_size)
    start_state = (
        jnp.full((head_count, row_count), -1e30, jnp.float32),
        jnp.zeros((head_count, row_count), jnp.float32),
        jnp.zeros((row_count, head_count, head_size), jnp.float32),
    )

    def absorb(state, pieces):
        key_piece = pieces[0][0, :, 0]
        value_piece = pieces[1][0, :, 0]
        scores = (
            jnp.einsum("qhd,khd->hqk", query_mat, key_piece, preferred_element_type=jnp.float32)
            * score_scale
        )
        running, totals, accumulated = state
        new_max = jnp.maximum(running, jnp.max(scores, axis=2))
        weights = jnp.exp(scores - new_max[:, :, None])
        factor = jnp.exp(running - new_max)
        totals = totals * factor + jnp.sum(weights, axis=2)
        probabilities = weights.astype(jnp.bfloat16)
        contrib = jnp.einsum(
            "hqk,khd->qhd", probabilities, value_piece, preferred_element_type=jnp.float32
        )
        accumulated = accumulated * factor.T[:, :, None] + contrib
        return (new_max, totals, accumulated)

    whole_keys, whole_values = (
        lax.all_gather(key_part, "blk", axis=1, tiled=True),
        lax.all_gather(value_part, "blk", axis=1, tiled=True),
    )
    key_count = whole_keys.shape[1]
    block_rows = math.gcd(key_count, 1024)

    def one_block(state, counter):
        offset = counter * block_rows
        key_block = lax.dynamic_slice_in_dim(whole_keys, offset, block_rows, 1)
        value_block = lax.dynamic_slice_in_dim(whole_values, offset, block_rows, 1)
        return (absorb(state, (key_block, value_block)), None)

    result, unused = lax.scan(
        one_block, start_state, jnp.arange(key_count // block_rows, dtype=jnp.int32)
    )
    output = (result[2] / result[1].T[:, :, None]).astype(jnp.bfloat16)
    return output.reshape(1, row_count, 1, head_count, head_size)


def local_generic(query_rows, key_rows, value_rows):
    ulysses = lax.axis_size("uly")
    tokens = query_rows.shape[1]
    width = query_rows.shape[2]
    heads_local = width // HD // ulysses

    def split_heads(array):
        array = array.reshape(1, tokens, ulysses, heads_local, HD)
        return lax.all_to_all(array, "uly", split_axis=2, concat_axis=1, tiled=True)

    mixed = attend(split_heads(query_rows), split_heads(key_rows), split_heads(value_rows))
    merged = lax.all_to_all(mixed, "uly", split_axis=1, concat_axis=2, tiled=True)
    return merged.reshape(1, tokens, width)


def run_copies(pairs, sems):
    started = [pltpu.make_async_copy(src, dst, sems.at[at]) for at, (src, dst) in enumerate(pairs)]
    for copy in started:
        copy.start()
    for copy in started:
        copy.wait()


def pack_kernel(messages, part, q_ref, k_ref, v_ref, *refs):
    outs, sems = refs[:-1], refs[-1]
    sources = {"q": q_ref, "k": k_ref, "v": v_ref}
    me = lax.axis_index("blk")
    pairs = []
    for (s, pieces), out in zip(messages, outs):
        start = 0
        for name, first, lanes in pieces:
            columns = pl.ds(pl.multiple_of((me ^ s) * part + first, 128), lanes)
            pairs.append((sources[name].at[0, :, columns], out.at[:, pl.ds(start, lanes)]))
            start += lanes
    run_copies(pairs, sems)


def join_kernel(pieces, *refs):
    lanes = refs[-1].shape[2]
    for at, (source, start) in enumerate(pieces):
        refs[-1][at] = refs[source][:, start : start + lanes]


def join(arrays, starts, lanes, effort=0, after=()):
    shape = (len(arrays), arrays[0].shape[0], lanes)
    return pl.pallas_call(
        functools.partial(join_kernel, list(enumerate(starts))),
        out_shape=jax.ShapeDtypeStruct(shape, arrays[0].dtype),
        in_specs=[VMEM] * (len(arrays) + len(after)),
        out_specs=VMEM,
        compiler_params=SMALL,
        cost_estimate=pl.CostEstimate(
            flops=effort, bytes_accessed=4 * math.prod(shape), transcendentals=0
        ),
        name="join",
    )(*arrays, *after)


def hold_kernel(*refs):
    pass


def hold(arrays, until=(), effort=0):
    return pl.pallas_call(
        hold_kernel,
        out_shape=[jax.ShapeDtypeStruct(array.shape, array.dtype) for array in arrays],
        in_specs=[ANY] * (len(arrays) + len(until)),
        out_specs=[ANY] * len(arrays),
        input_output_aliases={at: at for at in range(len(arrays))},
        compiler_params=SMALL,
        cost_estimate=pl.CostEstimate(flops=effort, bytes_accessed=0, transcendentals=0),
        name="hold",
    )(*arrays, *until)


def attend_kernel(held, keys, queries, *refs):
    key_refs, query_refs, out_refs = refs[:held], refs[held : -len(queries)], refs[-len(queries) :]
    tokens, part = out_refs[0].shape
    scale = 1.0 / math.sqrt(HD)

    def rows(sources, places, first):
        lanes = slice(first, first + HD)
        pieces = [
            sources[at][:, lanes] if row is None else sources[at][row, :, lanes]
            for at, row in places
        ]
        return jnp.concatenate(pieces, axis=0)

    lanes = range(0, part, HD)
    scores = [
        lax.dot_general(
            rows(query_refs, queries, lane),
            rows(key_refs, keys, lane),
            (((1,), (1,)), ((), ())),
            preferred_element_type=jnp.float32,
        )
        * scale
        for lane in lanes
    ]
    weights = [jnp.exp(s - jnp.max(s, axis=1, keepdims=True)) for s in scores]
    mixed = [
        jnp.dot(
            w.astype(jnp.bfloat16),
            rows(key_refs, keys, part + lane),
            preferred_element_type=jnp.float32,
        )
        for w, lane in zip(weights, lanes)
    ]
    for w, m, lane in zip(weights, mixed, lanes):
        result = (m / jnp.sum(w, axis=1, keepdims=True)).astype(jnp.bfloat16)
        for block, ref in enumerate(out_refs):
            ref[:, lane : lane + HD] = result[block * tokens : (block + 1) * tokens]


def unpack_kernel(order, part, *refs):
    ins, out_ref, sems = refs[:-2], refs[-2], refs[-1]
    me = lax.axis_index("blk")
    pairs = []
    for s, ref in zip(order, ins):
        columns = pl.ds(pl.multiple_of((me ^ s) * part, 128), part)
        pairs.append((ref, out_ref.at[0, :, columns]))
    run_copies(pairs, sems)


def local_blocks(query_rows, key_rows, value_rows):
    blocks, columns_of = lax.axis_size("blk"), lax.axis_size("uly")
    tokens, width = query_rows.shape[1:]
    part = width // blocks
    heads = part // HD
    kind = query_rows.dtype
    far = list(range(blocks - 1, 1, -1))

    kv, q = (("k", 0, part), ("v", 0, part)), (("q", 0, part),)
    messages = [(s, kv) for s in far] + [(1, kv + q), (0, kv)] + [(s, q) for s in far + [0]]
    inputs = [pltpu.with_memory_space_constraint(x, pltpu.HBM) for x in (query_rows, key_rows, value_rows)]

    def pack(cut):
        copies = sum(len(names) for s, names in cut)
        size = 2 * tokens * part * copies
        return pl.pallas_call(
            functools.partial(pack_kernel, cut, part),
            out_shape=[
                jax.ShapeDtypeStruct((tokens, sum(piece[2] for piece in names)), kind)
                for s, names in cut
            ],
            in_specs=[HBM] * 3,
            out_specs=[VMEM] * len(cut),
            scratch_shapes=[pltpu.SemaphoreType.DMA((copies,))],
            compiler_params=SMALL,
            cost_estimate=pl.CostEstimate(flops=0, bytes_accessed=2 * size, transcendentals=0),
            name="pack",
        )(*inputs)

    first = len(far) + 2
    packed = [*pack(messages[:first]), *pack(messages[first:])]

    def to_block(array, s):
        return lax.ppermute(array, "blk", [(i, i ^ s) for i in range(blocks)])

    def to_column(array, t):
        return lax.ppermute(array, "uly", [(i, (i + t) % columns_of) for i in range(columns_of)])

    sent = {message: array for message, array in zip(messages, packed)}
    own_kv, own_q = sent[0, kv], sent[0, q]
    far_kv = [to_block(sent[s, kv], s) for s in far]
    near_kvq = to_block(sent[1, kv + q], 1)
    far_kv = [hold([array], (), effort)[0] for array, effort in zip(far_kv, EFFORT_FAR)]
    near_kv = join([near_kvq], [0], 2 * part, EFFORT_NEAR, far_kv[:1])
    far_q = [to_block(sent[far[0], q], far[0])]
    far_q += [to_block(hold([sent[s, q]], [array])[0], s) for s, array in zip(far[1:], far_kv[1:])]
    own_kv_x, first_x, near_x, second_x = (
        [to_column(group, t) for t in range(1, columns_of)]
        for group in (own_kv, far_kv[0], near_kv[0], far_kv[1])
    )
    own_kv_x = hold(own_kv_x, effort=EFFORT_OWN)
    near_q = join([own_q, near_kvq], [0, 2 * part], part)
    far_q[:1] = hold(far_q[:1], [*own_kv_x, *first_x, *near_x], EFFORT)
    far_q[:1] = hold(far_q[:1], (), EFFORT_QUERIES)

    holders = [near_kvq, own_kv, *far_kv, *own_kv_x, *first_x, *near_x, *second_x]
    keys = [(at, None) for at in range(len(holders))]

    def attend(query_arrays, query_places):
        rows = tokens * len(query_places)
        pairs = heads * rows * tokens * len(keys)
        return pl.pallas_call(
            functools.partial(attend_kernel, len(holders), keys, query_places),
            out_shape=[jax.ShapeDtypeStruct((tokens, part), kind)] * len(query_places),
            in_specs=[VMEM] * (len(holders) + len(query_arrays)),
            out_specs=[VMEM] * len(query_places),
            compiler_params=pltpu.CompilerParams(vmem_limit_bytes=24 * 1024 * 1024),
            cost_estimate=pl.CostEstimate(
                flops=4 * HD * pairs,
                bytes_accessed=4 * part * (rows + tokens * len(keys)),
                transcendentals=pairs,
            ),
            name="attend",
        )(*holders, *query_arrays)

    mixed = dict(zip([0, 1] + far[:-1], attend([near_q] + far_q[:-1], [(0, 0), (0, 1), (1, None)])))
    last_q = hold([far_q[-1]], [mixed[0]])
    mixed[far[-1]] = attend(last_q, [(0, None)])[0]
    mixed[1] = hold([mixed[1]], [mixed[far[-1]]])[0]
    back = {s: to_block(mixed[s], s) for s in far + [1]}
    early = far[:-1]
    back.update(zip(early, hold([back[s] for s in early], effort=EFFORT)))
    back[0] = mixed[0]
    order = [0] + far + [1]
    back = [back[s] for s in order]
    return pl.pallas_call(
        functools.partial(unpack_kernel, order, part),
        out_shape=jax.ShapeDtypeStruct((1, tokens, width), kind),
        in_specs=[VMEM] * blocks,
        out_specs=HBM,
        scratch_shapes=[pltpu.SemaphoreType.DMA((blocks,))],
        compiler_params=SMALL,
        cost_estimate=pl.CostEstimate(
            flops=0, bytes_accessed=2 * tokens * width * 2, transcendentals=0
        ),
        name="unpack",
    )(*back)


def local(query_rows, key_rows, value_rows):
    blocks = lax.axis_size("blk")
    heads = query_rows.shape[2] // HD
    few = blocks == 4 and heads % blocks == 0
    plan = local_blocks if few else local_generic
    return plan(query_rows, key_rows, value_rows)


def solution(mesh):
    in_specs = (
        P("cfg", ("groups", "blk", "uly"), None),
        P("cfg", ("groups", "blk", "uly"), None),
        P("cfg", ("groups", "blk", "uly"), None),
    )
    out_specs = P("cfg", ("groups", "blk", "uly"), None)
    return jax.shard_map(local, mesh=mesh, in_specs=in_specs, out_specs=out_specs, check_vma=False)
```

```python
import functools
import math

import jax
import jax.numpy as jnp
from jax import lax
from jax.experimental import pallas as pl
from jax.experimental.pallas import tpu as pltpu
from jax.sharding import PartitionSpec as P

HD = 128
EFFORT = 0
EFFORT_OWN = 10**9
EFFORT_QUERIES = 2 * 10**8
EFFORT_NEAR = 0
EFFORT_FAR = (53 * 10**7, 5 * 10**8)
ANY = pl.BlockSpec(memory_space=pl.ANY)
HBM = pl.BlockSpec(memory_space=pltpu.HBM)
VMEM = pl.BlockSpec(memory_space=pltpu.VMEM)
SMALL = pltpu.CompilerParams(vmem_limit_bytes=4 * 1024 * 1024)


def attend(queries, key_part, value_part):
    query_mat = queries[0, :, 0]
    row_count, head_count, head_size = query_mat.shape
    score_scale = 1.0 / math.sqrt(head_size)
    start_state = (
        jnp.full((head_count, row_count), -1e30, jnp.float32),
        jnp.zeros((head_count, row_count), jnp.float32),
        jnp.zeros((row_count, head_count, head_size), jnp.float32),
    )

    def absorb(state, pieces):
        key_piece = pieces[0][0, :, 0]
        value_piece = pieces[1][0, :, 0]
        scores = (
            jnp.einsum("qhd,khd->hqk", query_mat, key_piece, preferred_element_type=jnp.float32)
            * score_scale
        )
        running, totals, accumulated = state
        new_max = jnp.maximum(running, jnp.max(scores, axis=2))
        weights = jnp.exp(scores - new_max[:, :, None])
        factor = jnp.exp(running - new_max)
        totals = totals * factor + jnp.sum(weights, axis=2)
        probabilities = weights.astype(jnp.bfloat16)
        contrib = jnp.einsum(
            "hqk,khd->qhd", probabilities, value_piece, preferred_element_type=jnp.float32
        )
        accumulated = accumulated * factor.T[:, :, None] + contrib
        return (new_max, totals, accumulated)

    whole_keys, whole_values = (
        lax.all_gather(key_part, "blk", axis=1, tiled=True),
        lax.all_gather(value_part, "blk", axis=1, tiled=True),
    )
    key_count = whole_keys.shape[1]
    block_rows = math.gcd(key_count, 1024)

    def one_block(state, counter):
        offset = counter * block_rows
        key_block = lax.dynamic_slice_in_dim(whole_keys, offset, block_rows, 1)
        value_block = lax.dynamic_slice_in_dim(whole_values, offset, block_rows, 1)
        return (absorb(state, (key_block, value_block)), None)

    result, unused = lax.scan(
        one_block, start_state, jnp.arange(key_count // block_rows, dtype=jnp.int32)
    )
    output = (result[2] / result[1].T[:, :, None]).astype(jnp.bfloat16)
    return output.reshape(1, row_count, 1, head_count, head_size)


def local_generic(query_rows, key_rows, value_rows):
    ulysses = lax.axis_size("uly")
    tokens = query_rows.shape[1]
    width = query_rows.shape[2]
    heads_local = width // HD // ulysses

    def split_heads(array):
        array = array.reshape(1, tokens, ulysses, heads_local, HD)
        return lax.all_to_all(array, "uly", split_axis=2, concat_axis=1, tiled=True)

    mixed = attend(split_heads(query_rows), split_heads(key_rows), split_heads(value_rows))
    merged = lax.all_to_all(mixed, "uly", split_axis=1, concat_axis=2, tiled=True)
    return merged.reshape(1, tokens, width)


def run_copies(pairs, sems):
    started = [pltpu.make_async_copy(src, dst, sems.at[at]) for at, (src, dst) in enumerate(pairs)]
    for copy in started:
        copy.start()
    for copy in started:
        copy.wait()


def pack_kernel(messages, part, q_ref, k_ref, v_ref, *refs):
    outs, sems = refs[:-1], refs[-1]
    sources = {"q": q_ref, "k": k_ref, "v": v_ref}
    me = lax.axis_index("blk")
    pairs = []
    for (s, pieces), out in zip(messages, outs):
        start = 0
        for name, first, lanes in pieces:
            columns = pl.ds(pl.multiple_of((me ^ s) * part + first, 128), lanes)
            pairs.append((sources[name].at[0, :, columns], out.at[:, pl.ds(start, lanes)]))
            start += lanes
    run_copies(pairs, sems)


def join_kernel(pieces, *refs):
    lanes = refs[-1].shape[2]
    for at, (source, start) in enumerate(pieces):
        refs[-1][at] = refs[source][:, start : start + lanes]


def join(arrays, starts, lanes, effort=0, after=()):
    shape = (len(arrays), arrays[0].shape[0], lanes)
    return pl.pallas_call(
        functools.partial(join_kernel, list(enumerate(starts))),
        out_shape=jax.ShapeDtypeStruct(shape, arrays[0].dtype),
        in_specs=[VMEM] * (len(arrays) + len(after)),
        out_specs=VMEM,
        compiler_params=SMALL,
        cost_estimate=pl.CostEstimate(
            flops=effort, bytes_accessed=4 * math.prod(shape), transcendentals=0
        ),
        name="join",
    )(*arrays, *after)


def hold_kernel(*refs):
    pass


def hold(arrays, until=(), effort=0):
    return pl.pallas_call(
        hold_kernel,
        out_shape=[jax.ShapeDtypeStruct(array.shape, array.dtype) for array in arrays],
        in_specs=[ANY] * (len(arrays) + len(until)),
        out_specs=[ANY] * len(arrays),
        input_output_aliases={at: at for at in range(len(arrays))},
        compiler_params=SMALL,
        cost_estimate=pl.CostEstimate(flops=effort, bytes_accessed=0, transcendentals=0),
        name="hold",
    )(*arrays, *until)


def attend_kernel(held, keys, queries, *refs):
    key_refs, query_refs, out_refs = refs[:held], refs[held : -len(queries)], refs[-len(queries) :]
    tokens, part = out_refs[0].shape
    scale = 1.0 / math.sqrt(HD)

    def rows(sources, places, first):
        lanes = slice(first, first + HD)
        pieces = [
            sources[at][:, lanes] if row is None else sources[at][row, :, lanes]
            for at, row in places
        ]
        return jnp.concatenate(pieces, axis=0)

    lanes = range(0, part, HD)
    scores = [
        lax.dot_general(
            rows(query_refs, queries, lane),
            rows(key_refs, keys, lane),
            (((1,), (1,)), ((), ())),
            preferred_element_type=jnp.float32,
        )
        * scale
        for lane in lanes
    ]
    weights = [jnp.exp(s - jnp.max(s, axis=1, keepdims=True)) for s in scores]
    mixed = [
        jnp.dot(
            w.astype(jnp.bfloat16),
            rows(key_refs, keys, part + lane),
            preferred_element_type=jnp.float32,
        )
        for w, lane in zip(weights, lanes)
    ]
    for w, m, lane in zip(weights, mixed, lanes):
        result = (m / jnp.sum(w, axis=1, keepdims=True)).astype(jnp.bfloat16)
        for block, ref in enumerate(out_refs):
            ref[:, lane : lane + HD] = result[block * tokens : (block + 1) * tokens]


def unpack_kernel(order, part, *refs):
    ins, out_ref, sems = refs[:-2], refs[-2], refs[-1]
    me = lax.axis_index("blk")
    pairs = []
    for s, ref in zip(order, ins):
        columns = pl.ds(pl.multiple_of((me ^ s) * part, 128), part)
        pairs.append((ref, out_ref.at[0, :, columns]))
    run_copies(pairs, sems)


def local_blocks(query_rows, key_rows, value_rows):
    blocks, columns_of = lax.axis_size("blk"), lax.axis_size("uly")
    tokens, width = query_rows.shape[1:]
    part = width // blocks
    heads = part // HD
    kind = query_rows.dtype
    far = list(range(blocks - 1, 1, -1))

    kv, q = (("k", 0, part), ("v", 0, part)), (("q", 0, part),)
    messages = [(far[0], kv), (1, kv + q), (0, kv), (far[1], kv)] + [(s, q) for s in far + [0]]
    inputs = [pltpu.with_memory_space_constraint(x, pltpu.HBM) for x in (query_rows, key_rows, value_rows)]

    def pack(cut):
        copies = sum(len(names) for s, names in cut)
        size = 2 * tokens * part * copies
        return pl.pallas_call(
            functools.partial(pack_kernel, cut, part),
            out_shape=[
                jax.ShapeDtypeStruct((tokens, sum(piece[2] for piece in names)), kind)
                for s, names in cut
            ],
            in_specs=[HBM] * 3,
            out_specs=[VMEM] * len(cut),
            scratch_shapes=[pltpu.SemaphoreType.DMA((copies,))],
            compiler_params=SMALL,
            cost_estimate=pl.CostEstimate(flops=0, bytes_accessed=2 * size, transcendentals=0),
            name="pack",
        )(*inputs)

    first = 3
    packed = [*pack(messages[:first]), *pack(messages[first:])]

    def to_block(array, s):
        return lax.ppermute(array, "blk", [(i, i ^ s) for i in range(blocks)])

    def to_column(array, t):
        return lax.ppermute(array, "uly", [(i, (i + t) % columns_of) for i in range(columns_of)])

    sent = {message: array for message, array in zip(messages, packed)}
    own_kv, own_q = sent[0, kv], sent[0, q]
    far_kv = [to_block(sent[s, kv], s) for s in far]
    near_kvq = to_block(sent[1, kv + q], 1)
    far_kv = [hold([array], (), effort)[0] for array, effort in zip(far_kv, EFFORT_FAR)]
    near_kv = join([near_kvq], [0], 2 * part, EFFORT_NEAR, far_kv[:1])
    far_q = [to_block(sent[far[0], q], far[0])]
    far_q += [to_block(hold([sent[s, q]], [array])[0], s) for s, array in zip(far[1:], far_kv[1:])]
    own_kv_x, first_x, near_x, second_x = (
        [to_column(group, t) for t in range(1, columns_of)]
        for group in (own_kv, far_kv[0], near_kv[0], far_kv[1])
    )
    own_kv_x = hold(own_kv_x, effort=EFFORT_OWN)
    near_q = join([own_q, near_kvq], [0, 2 * part], part)
    far_q[:1] = hold(far_q[:1], [*own_kv_x, *first_x, *near_x], EFFORT)
    far_q[:1] = hold(far_q[:1], (), EFFORT_QUERIES)

    holders = [near_kvq, own_kv, *far_kv, *own_kv_x, *first_x, *near_x, *second_x]
    keys = [(at, None) for at in range(len(holders))]

    def attend(query_arrays, query_places):
        rows = tokens * len(query_places)
        pairs = heads * rows * tokens * len(keys)
        return pl.pallas_call(
            functools.partial(attend_kernel, len(holders), keys, query_places),
            out_shape=[jax.ShapeDtypeStruct((tokens, part), kind)] * len(query_places),
            in_specs=[VMEM] * (len(holders) + len(query_arrays)),
            out_specs=[VMEM] * len(query_places),
            compiler_params=pltpu.CompilerParams(vmem_limit_bytes=24 * 1024 * 1024),
            cost_estimate=pl.CostEstimate(
                flops=4 * HD * pairs,
                bytes_accessed=4 * part * (rows + tokens * len(keys)),
                transcendentals=pairs,
            ),
            name="attend",
        )(*holders, *query_arrays)

    mixed = dict(zip([0, 1] + far[:-1], attend([near_q] + far_q[:-1], [(0, 0), (0, 1), (1, None)])))
    last_q = hold([far_q[-1]], [mixed[0]])
    mixed[far[-1]] = attend(last_q, [(0, None)])[0]
    mixed[1] = hold([mixed[1]], [mixed[far[-1]]])[0]
    back = {s: to_block(mixed[s], s) for s in far + [1]}
    early = far[:-1]
    back.update(zip(early, hold([back[s] for s in early], effort=EFFORT)))
    back[0] = mixed[0]
    order = [0] + far + [1]
    back = [back[s] for s in order]
    return pl.pallas_call(
        functools.partial(unpack_kernel, order, part),
        out_shape=jax.ShapeDtypeStruct((1, tokens, width), kind),
        in_specs=[VMEM] * blocks,
        out_specs=HBM,
        scratch_shapes=[pltpu.SemaphoreType.DMA((blocks,))],
        compiler_params=SMALL,
        cost_estimate=pl.CostEstimate(
            flops=0, bytes_accessed=2 * tokens * width * 2, transcendentals=0
        ),
        name="unpack",
    )(*back)


def local(query_rows, key_rows, value_rows):
    blocks = lax.axis_size("blk")
    heads = query_rows.shape[2] // HD
    few = blocks == 4 and heads % blocks == 0
    plan = local_blocks if few else local_generic
    return plan(query_rows, key_rows, value_rows)


def solution(mesh):
    in_specs = (
        P("cfg", ("groups", "blk", "uly"), None),
        P("cfg", ("groups", "blk", "uly"), None),
        P("cfg", ("groups", "blk", "uly"), None),
    )
    out_specs = P("cfg", ("groups", "blk", "uly"), None)
    return jax.shard_map(local, mesh=mesh, in_specs=in_specs, out_specs=out_specs, check_vma=False)
```

```python
import functools
import math

import jax
import jax.numpy as jnp
from jax import lax
from jax.experimental import pallas as pl
from jax.experimental.pallas import tpu as pltpu
from jax.sharding import PartitionSpec as P

HD = 128
EFFORT = 0
EFFORT_OWN = 10**9
EFFORT_QUERIES = 2 * 10**8
EFFORT_NEAR = 0
EFFORT_FAR = (53 * 10**7, 5 * 10**8)
ANY = pl.BlockSpec(memory_space=pl.ANY)
HBM = pl.BlockSpec(memory_space=pltpu.HBM)
VMEM = pl.BlockSpec(memory_space=pltpu.VMEM)
SMALL = pltpu.CompilerParams(vmem_limit_bytes=4 * 1024 * 1024)


def attend(queries, key_part, value_part):
    query_mat = queries[0, :, 0]
    row_count, head_count, head_size = query_mat.shape
    score_scale = 1.0 / math.sqrt(head_size)
    start_state = (
        jnp.full((head_count, row_count), -1e30, jnp.float32),
        jnp.zeros((head_count, row_count), jnp.float32),
        jnp.zeros((row_count, head_count, head_size), jnp.float32),
    )

    def absorb(state, pieces):
        key_piece = pieces[0][0, :, 0]
        value_piece = pieces[1][0, :, 0]
        scores = (
            jnp.einsum("qhd,khd->hqk", query_mat, key_piece, preferred_element_type=jnp.float32)
            * score_scale
        )
        running, totals, accumulated = state
        new_max = jnp.maximum(running, jnp.max(scores, axis=2))
        weights = jnp.exp(scores - new_max[:, :, None])
        factor = jnp.exp(running - new_max)
        totals = totals * factor + jnp.sum(weights, axis=2)
        probabilities = weights.astype(jnp.bfloat16)
        contrib = jnp.einsum(
            "hqk,khd->qhd", probabilities, value_piece, preferred_element_type=jnp.float32
        )
        accumulated = accumulated * factor.T[:, :, None] + contrib
        return (new_max, totals, accumulated)

    whole_keys, whole_values = (
        lax.all_gather(key_part, "blk", axis=1, tiled=True),
        lax.all_gather(value_part, "blk", axis=1, tiled=True),
    )
    key_count = whole_keys.shape[1]
    block_rows = math.gcd(key_count, 1024)

    def one_block(state, counter):
        offset = counter * block_rows
        key_block = lax.dynamic_slice_in_dim(whole_keys, offset, block_rows, 1)
        value_block = lax.dynamic_slice_in_dim(whole_values, offset, block_rows, 1)
        return (absorb(state, (key_block, value_block)), None)

    result, unused = lax.scan(
        one_block, start_state, jnp.arange(key_count // block_rows, dtype=jnp.int32)
    )
    output = (result[2] / result[1].T[:, :, None]).astype(jnp.bfloat16)
    return output.reshape(1, row_count, 1, head_count, head_size)


def local_generic(query_rows, key_rows, value_rows):
    ulysses = lax.axis_size("uly")
    tokens = query_rows.shape[1]
    width = query_rows.shape[2]
    heads_local = width // HD // ulysses

    def split_heads(array):
        array = array.reshape(1, tokens, ulysses, heads_local, HD)
        return lax.all_to_all(array, "uly", split_axis=2, concat_axis=1, tiled=True)

    mixed = attend(split_heads(query_rows), split_heads(key_rows), split_heads(value_rows))
    merged = lax.all_to_all(mixed, "uly", split_axis=1, concat_axis=2, tiled=True)
    return merged.reshape(1, tokens, width)


def run_copies(pairs, sems):
    started = [pltpu.make_async_copy(src, dst, sems.at[at]) for at, (src, dst) in enumerate(pairs)]
    for copy in started:
        copy.start()
    for copy in started:
        copy.wait()


def pack_kernel(messages, part, q_ref, k_ref, v_ref, *refs):
    outs, sems = refs[:-1], refs[-1]
    sources = {"q": q_ref, "k": k_ref, "v": v_ref}
    me = lax.axis_index("blk")
    pairs = []
    for (s, pieces), out in zip(messages, outs):
        start = 0
        for name, first, lanes in pieces:
            columns = pl.ds(pl.multiple_of((me ^ s) * part + first, 128), lanes)
            pairs.append((sources[name].at[0, :, columns], out.at[:, pl.ds(start, lanes)]))
            start += lanes
    run_copies(pairs, sems)


def join_kernel(pieces, *refs):
    lanes = refs[-1].shape[2]
    for at, (source, start) in enumerate(pieces):
        refs[-1][at] = refs[source][:, start : start + lanes]


def join(arrays, starts, lanes, effort=0, after=()):
    shape = (len(arrays), arrays[0].shape[0], lanes)
    return pl.pallas_call(
        functools.partial(join_kernel, list(enumerate(starts))),
        out_shape=jax.ShapeDtypeStruct(shape, arrays[0].dtype),
        in_specs=[VMEM] * (len(arrays) + len(after)),
        out_specs=VMEM,
        compiler_params=SMALL,
        cost_estimate=pl.CostEstimate(
            flops=effort, bytes_accessed=4 * math.prod(shape), transcendentals=0
        ),
        name="join",
    )(*arrays, *after)


def hold_kernel(*refs):
    pass


def hold(arrays, until=(), effort=0):
    return pl.pallas_call(
        hold_kernel,
        out_shape=[jax.ShapeDtypeStruct(array.shape, array.dtype) for array in arrays],
        in_specs=[ANY] * (len(arrays) + len(until)),
        out_specs=[ANY] * len(arrays),
        input_output_aliases={at: at for at in range(len(arrays))},
        compiler_params=SMALL,
        cost_estimate=pl.CostEstimate(flops=effort, bytes_accessed=0, transcendentals=0),
        name="hold",
    )(*arrays, *until)


def attend_kernel(held, keys, queries, *refs):
    key_refs, query_refs, out_refs = refs[:held], refs[held : -len(queries)], refs[-len(queries) :]
    tokens, part = out_refs[0].shape
    scale = 1.0 / math.sqrt(HD)

    def rows(sources, places, first):
        lanes = slice(first, first + HD)
        pieces = [
            sources[at][:, lanes] if row is None else sources[at][row, :, lanes]
            for at, row in places
        ]
        return jnp.concatenate(pieces, axis=0)

    lanes = range(0, part, HD)
    scores = [
        lax.dot_general(
            rows(query_refs, queries, lane),
            rows(key_refs, keys, lane),
            (((1,), (1,)), ((), ())),
            preferred_element_type=jnp.float32,
        )
        * scale
        for lane in lanes
    ]
    weights = [jnp.exp(s - jnp.max(s, axis=1, keepdims=True)) for s in scores]
    mixed = [
        jnp.dot(
            w.astype(jnp.bfloat16),
            rows(key_refs, keys, part + lane),
            preferred_element_type=jnp.float32,
        )
        for w, lane in zip(weights, lanes)
    ]
    for w, m, lane in zip(weights, mixed, lanes):
        result = (m / jnp.sum(w, axis=1, keepdims=True)).astype(jnp.bfloat16)
        for block, ref in enumerate(out_refs):
            ref[:, lane : lane + HD] = result[block * tokens : (block + 1) * tokens]


def unpack_kernel(order, part, *refs):
    ins, out_ref, sems = refs[:-2], refs[-2], refs[-1]
    me = lax.axis_index("blk")
    pairs = []
    for s, ref in zip(order, ins):
        columns = pl.ds(pl.multiple_of((me ^ s) * part, 128), part)
        pairs.append((ref, out_ref.at[0, :, columns]))
    run_copies(pairs, sems)


def local_blocks(query_rows, key_rows, value_rows):
    blocks, columns_of = lax.axis_size("blk"), lax.axis_size("uly")
    tokens, width = query_rows.shape[1:]
    part = width // blocks
    heads = part // HD
    kind = query_rows.dtype
    far = list(range(blocks - 1, 1, -1))

    kv, q = (("k", 0, part), ("v", 0, part)), (("q", 0, part),)
    messages = [(far[0], kv), (1, kv + q), (far[1], kv), (0, kv)] + [(s, q) for s in far + [0]]
    inputs = [pltpu.with_memory_space_constraint(x, pltpu.HBM) for x in (query_rows, key_rows, value_rows)]

    def pack(cut):
        copies = sum(len(names) for s, names in cut)
        size = 2 * tokens * part * copies
        return pl.pallas_call(
            functools.partial(pack_kernel, cut, part),
            out_shape=[
                jax.ShapeDtypeStruct((tokens, sum(piece[2] for piece in names)), kind)
                for s, names in cut
            ],
            in_specs=[HBM] * 3,
            out_specs=[VMEM] * len(cut),
            scratch_shapes=[pltpu.SemaphoreType.DMA((copies,))],
            compiler_params=SMALL,
            cost_estimate=pl.CostEstimate(flops=0, bytes_accessed=2 * size, transcendentals=0),
            name="pack",
        )(*inputs)

    first = 2
    packed = [*pack(messages[:first]), *pack(messages[first:])]

    def to_block(array, s):
        return lax.ppermute(array, "blk", [(i, i ^ s) for i in range(blocks)])

    def to_column(array, t):
        return lax.ppermute(array, "uly", [(i, (i + t) % columns_of) for i in range(columns_of)])

    sent = {message: array for message, array in zip(messages, packed)}
    own_kv, own_q = sent[0, kv], sent[0, q]
    far_kv = [to_block(sent[s, kv], s) for s in far]
    near_kvq = to_block(sent[1, kv + q], 1)
    far_kv = [hold([array], (), effort)[0] for array, effort in zip(far_kv, EFFORT_FAR)]
    near_kv = join([near_kvq], [0], 2 * part, EFFORT_NEAR, far_kv[:1])
    far_q = [to_block(sent[far[0], q], far[0])]
    far_q += [to_block(hold([sent[s, q]], [array])[0], s) for s, array in zip(far[1:], far_kv[1:])]
    own_kv_x, first_x, near_x, second_x = (
        [to_column(group, t) for t in range(1, columns_of)]
        for group in (own_kv, far_kv[0], near_kv[0], far_kv[1])
    )
    own_kv_x = hold(own_kv_x, effort=EFFORT_OWN)
    near_q = join([own_q, near_kvq], [0, 2 * part], part)
    far_q[:1] = hold(far_q[:1], [*own_kv_x, *first_x, *near_x], EFFORT)
    far_q[:1] = hold(far_q[:1], (), EFFORT_QUERIES)

    holders = [near_kvq, own_kv, *far_kv, *own_kv_x, *first_x, *near_x, *second_x]
    keys = [(at, None) for at in range(len(holders))]

    def attend(query_arrays, query_places):
        rows = tokens * len(query_places)
        pairs = heads * rows * tokens * len(keys)
        return pl.pallas_call(
            functools.partial(attend_kernel, len(holders), keys, query_places),
            out_shape=[jax.ShapeDtypeStruct((tokens, part), kind)] * len(query_places),
            in_specs=[VMEM] * (len(holders) + len(query_arrays)),
            out_specs=[VMEM] * len(query_places),
            compiler_params=pltpu.CompilerParams(vmem_limit_bytes=24 * 1024 * 1024),
            cost_estimate=pl.CostEstimate(
                flops=4 * HD * pairs,
                bytes_accessed=4 * part * (rows + tokens * len(keys)),
                transcendentals=pairs,
            ),
            name="attend",
        )(*holders, *query_arrays)

    mixed = dict(zip([0, 1] + far[:-1], attend([near_q] + far_q[:-1], [(0, 0), (0, 1), (1, None)])))
    last_q = hold([far_q[-1]], [mixed[0]])
    mixed[far[-1]] = attend(last_q, [(0, None)])[0]
    mixed[1] = hold([mixed[1]], [mixed[far[-1]]])[0]
    back = {s: to_block(mixed[s], s) for s in far + [1]}
    early = far[:-1]
    back.update(zip(early, hold([back[s] for s in early], effort=EFFORT)))
    back[0] = mixed[0]
    order = [0] + far + [1]
    back = [back[s] for s in order]
    return pl.pallas_call(
        functools.partial(unpack_kernel, order, part),
        out_shape=jax.ShapeDtypeStruct((1, tokens, width), kind),
        in_specs=[VMEM] * blocks,
        out_specs=HBM,
        scratch_shapes=[pltpu.SemaphoreType.DMA((blocks,))],
        compiler_params=SMALL,
        cost_estimate=pl.CostEstimate(
            flops=0, bytes_accessed=2 * tokens * width * 2, transcendentals=0
        ),
        name="unpack",
    )(*back)


def local(query_rows, key_rows, value_rows):
    blocks = lax.axis_size("blk")
    heads = query_rows.shape[2] // HD
    few = blocks == 4 and heads % blocks == 0
    plan = local_blocks if few else local_generic
    return plan(query_rows, key_rows, value_rows)


def solution(mesh):
    in_specs = (
        P("cfg", ("groups", "blk", "uly"), None),
        P("cfg", ("groups", "blk", "uly"), None),
        P("cfg", ("groups", "blk", "uly"), None),
    )
    out_specs = P("cfg", ("groups", "blk", "uly"), None)
    return jax.shard_map(local, mesh=mesh, in_specs=in_specs, out_specs=out_specs, check_vma=False)
```

```python
import functools
import math

import jax
import jax.numpy as jnp
from jax import lax
from jax.experimental import pallas as pl
from jax.experimental.pallas import tpu as pltpu
from jax.sharding import PartitionSpec as P

HD = 128
EFFORT = 0
EFFORT_OWN = 10**9
EFFORT_QUERIES = 2 * 10**8
EFFORT_NEAR = 0
EFFORT_FAR = (53 * 10**7, 5 * 10**8)
ANY = pl.BlockSpec(memory_space=pl.ANY)
HBM = pl.BlockSpec(memory_space=pltpu.HBM)
VMEM = pl.BlockSpec(memory_space=pltpu.VMEM)
SMALL = pltpu.CompilerParams(vmem_limit_bytes=4 * 1024 * 1024)


def attend(queries, key_part, value_part):
    query_mat = queries[0, :, 0]
    row_count, head_count, head_size = query_mat.shape
    score_scale = 1.0 / math.sqrt(head_size)
    start_state = (
        jnp.full((head_count, row_count), -1e30, jnp.float32),
        jnp.zeros((head_count, row_count), jnp.float32),
        jnp.zeros((row_count, head_count, head_size), jnp.float32),
    )

    def absorb(state, pieces):
        key_piece = pieces[0][0, :, 0]
        value_piece = pieces[1][0, :, 0]
        scores = (
            jnp.einsum("qhd,khd->hqk", query_mat, key_piece, preferred_element_type=jnp.float32)
            * score_scale
        )
        running, totals, accumulated = state
        new_max = jnp.maximum(running, jnp.max(scores, axis=2))
        weights = jnp.exp(scores - new_max[:, :, None])
        factor = jnp.exp(running - new_max)
        totals = totals * factor + jnp.sum(weights, axis=2)
        probabilities = weights.astype(jnp.bfloat16)
        contrib = jnp.einsum(
            "hqk,khd->qhd", probabilities, value_piece, preferred_element_type=jnp.float32
        )
        accumulated = accumulated * factor.T[:, :, None] + contrib
        return (new_max, totals, accumulated)

    whole_keys, whole_values = (
        lax.all_gather(key_part, "blk", axis=1, tiled=True),
        lax.all_gather(value_part, "blk", axis=1, tiled=True),
    )
    key_count = whole_keys.shape[1]
    block_rows = math.gcd(key_count, 1024)

    def one_block(state, counter):
        offset = counter * block_rows
        key_block = lax.dynamic_slice_in_dim(whole_keys, offset, block_rows, 1)
        value_block = lax.dynamic_slice_in_dim(whole_values, offset, block_rows, 1)
        return (absorb(state, (key_block, value_block)), None)

    result, unused = lax.scan(
        one_block, start_state, jnp.arange(key_count // block_rows, dtype=jnp.int32)
    )
    output = (result[2] / result[1].T[:, :, None]).astype(jnp.bfloat16)
    return output.reshape(1, row_count, 1, head_count, head_size)


def local_generic(query_rows, key_rows, value_rows):
    ulysses = lax.axis_size("uly")
    tokens = query_rows.shape[1]
    width = query_rows.shape[2]
    heads_local = width // HD // ulysses

    def split_heads(array):
        array = array.reshape(1, tokens, ulysses, heads_local, HD)
        return lax.all_to_all(array, "uly", split_axis=2, concat_axis=1, tiled=True)

    mixed = attend(split_heads(query_rows), split_heads(key_rows), split_heads(value_rows))
    merged = lax.all_to_all(mixed, "uly", split_axis=1, concat_axis=2, tiled=True)
    return merged.reshape(1, tokens, width)


def run_copies(pairs, sems):
    started = [pltpu.make_async_copy(src, dst, sems.at[at]) for at, (src, dst) in enumerate(pairs)]
    for copy in started:
        copy.start()
    for copy in started:
        copy.wait()


def pack_kernel(messages, part, q_ref, k_ref, v_ref, *refs):
    outs, sems = refs[:-1], refs[-1]
    sources = {"q": q_ref, "k": k_ref, "v": v_ref}
    me = lax.axis_index("blk")
    pairs = []
    for (s, pieces), out in zip(messages, outs):
        start = 0
        for name, first, lanes in pieces:
            columns = pl.ds(pl.multiple_of((me ^ s) * part + first, 128), lanes)
            pairs.append((sources[name].at[0, :, columns], out.at[:, pl.ds(start, lanes)]))
            start += lanes
    run_copies(pairs, sems)


def join_kernel(pieces, *refs):
    lanes = refs[-1].shape[2]
    for at, (source, start) in enumerate(pieces):
        refs[-1][at] = refs[source][:, start : start + lanes]


def join(arrays, starts, lanes, effort=0, after=()):
    shape = (len(arrays), arrays[0].shape[0], lanes)
    return pl.pallas_call(
        functools.partial(join_kernel, list(enumerate(starts))),
        out_shape=jax.ShapeDtypeStruct(shape, arrays[0].dtype),
        in_specs=[VMEM] * (len(arrays) + len(after)),
        out_specs=VMEM,
        compiler_params=SMALL,
        cost_estimate=pl.CostEstimate(
            flops=effort, bytes_accessed=4 * math.prod(shape), transcendentals=0
        ),
        name="join",
    )(*arrays, *after)


def hold_kernel(*refs):
    pass


def hold(arrays, until=(), effort=0):
    return pl.pallas_call(
        hold_kernel,
        out_shape=[jax.ShapeDtypeStruct(array.shape, array.dtype) for array in arrays],
        in_specs=[ANY] * (len(arrays) + len(until)),
        out_specs=[ANY] * len(arrays),
        input_output_aliases={at: at for at in range(len(arrays))},
        compiler_params=SMALL,
        cost_estimate=pl.CostEstimate(flops=effort, bytes_accessed=0, transcendentals=0),
        name="hold",
    )(*arrays, *until)


def attend_kernel(held, keys, queries, *refs):
    key_refs, query_refs, out_refs = refs[:held], refs[held : -len(queries)], refs[-len(queries) :]
    tokens, part = out_refs[0].shape
    scale = 1.0 / math.sqrt(HD)

    def rows(sources, places, first):
        lanes = slice(first, first + HD)
        pieces = [
            sources[at][:, lanes] if row is None else sources[at][row, :, lanes]
            for at, row in places
        ]
        return jnp.concatenate(pieces, axis=0)

    lanes = range(0, part, HD)
    scores = [
        lax.dot_general(
            rows(query_refs, queries, lane),
            rows(key_refs, keys, lane),
            (((1,), (1,)), ((), ())),
            preferred_element_type=jnp.float32,
        )
        * scale
        for lane in lanes
    ]
    weights = [jnp.exp(s - jnp.max(s, axis=1, keepdims=True)) for s in scores]
    mixed = [
        jnp.dot(
            w.astype(jnp.bfloat16),
            rows(key_refs, keys, part + lane),
            preferred_element_type=jnp.float32,
        )
        for w, lane in zip(weights, lanes)
    ]
    for w, m, lane in zip(weights, mixed, lanes):
        result = (m / jnp.sum(w, axis=1, keepdims=True)).astype(jnp.bfloat16)
        for block, ref in enumerate(out_refs):
            ref[:, lane : lane + HD] = result[block * tokens : (block + 1) * tokens]


def unpack_kernel(order, part, *refs):
    ins, out_ref, sems = refs[:-2], refs[-2], refs[-1]
    me = lax.axis_index("blk")
    pairs = []
    for s, ref in zip(order, ins):
        columns = pl.ds(pl.multiple_of((me ^ s) * part, 128), part)
        pairs.append((ref, out_ref.at[0, :, columns]))
    run_copies(pairs, sems)


def local_blocks(query_rows, key_rows, value_rows):
    blocks, columns_of = lax.axis_size("blk"), lax.axis_size("uly")
    tokens, width = query_rows.shape[1:]
    part = width // blocks
    heads = part // HD
    kind = query_rows.dtype
    far = list(range(blocks - 1, 1, -1))

    kv, q = (("k", 0, part), ("v", 0, part)), (("q", 0, part),)
    messages = [(far[0], kv), (1, kv + q), (far[1], kv), (0, kv)] + [(s, q) for s in far + [0]]
    inputs = [pltpu.with_memory_space_constraint(x, pltpu.HBM) for x in (query_rows, key_rows, value_rows)]

    def pack(cut):
        copies = sum(len(names) for s, names in cut)
        size = 2 * tokens * part * copies
        return pl.pallas_call(
            functools.partial(pack_kernel, cut, part),
            out_shape=[
                jax.ShapeDtypeStruct((tokens, sum(piece[2] for piece in names)), kind)
                for s, names in cut
            ],
            in_specs=[HBM] * 3,
            out_specs=[VMEM] * len(cut),
            scratch_shapes=[pltpu.SemaphoreType.DMA((copies,))],
            compiler_params=SMALL,
            cost_estimate=pl.CostEstimate(flops=0, bytes_accessed=2 * size, transcendentals=0),
            name="pack",
        )(*inputs)

    first = 2
    packed = [*pack(messages[:first]), *pack(messages[first:])]

    def to_block(array, s):
        return lax.ppermute(array, "blk", [(i, i ^ s) for i in range(blocks)])

    def to_column(array, t):
        return lax.ppermute(array, "uly", [(i, (i + t) % columns_of) for i in range(columns_of)])

    sent = {message: array for message, array in zip(messages, packed)}
    own_kv, own_q = sent[0, kv], sent[0, q]
    far_kv = [to_block(sent[s, kv], s) for s in far]
    near_kvq = to_block(sent[1, kv + q], 1)
    far_kv = [hold([array], (), effort)[0] for array, effort in zip(far_kv, EFFORT_FAR)]
    near_kv = join([near_kvq], [0], 2 * part, EFFORT_NEAR, far_kv[:1])
    far_q = [to_block(sent[far[0], q], far[0])]
    far_q += [to_block(hold([sent[s, q]], [array])[0], s) for s, array in zip(far[1:], far_kv[1:])]
    own_kv_x, first_x, near_x, second_x = (
        [to_column(group, t) for t in range(1, columns_of)]
        for group in (own_kv, far_kv[0], near_kv[0], far_kv[1])
    )
    own_kv_x = hold(own_kv_x, effort=EFFORT_OWN)
    near_q = join([own_q, near_kvq], [0, 2 * part], part)
    far_q[:1] = hold(far_q[:1], [*own_kv_x, *first_x, *near_x], EFFORT)
    far_q[:1] = hold(far_q[:1], (), EFFORT_QUERIES)

    holders = [near_kvq, own_kv, *far_kv, *own_kv_x, *first_x, *near_x, *second_x]
    keys = [(at, None) for at in range(len(holders))]

    def attend(query_arrays, query_places):
        rows = tokens * len(query_places)
        pairs = heads * rows * tokens * len(keys)
        return pl.pallas_call(
            functools.partial(attend_kernel, len(holders), keys, query_places),
            out_shape=[jax.ShapeDtypeStruct((tokens, part), kind)] * len(query_places),
            in_specs=[VMEM] * (len(holders) + len(query_arrays)),
            out_specs=[VMEM] * len(query_places),
            compiler_params=pltpu.CompilerParams(vmem_limit_bytes=24 * 1024 * 1024),
            cost_estimate=pl.CostEstimate(
                flops=4 * HD * pairs,
                bytes_accessed=4 * part * (rows + tokens * len(keys)),
                transcendentals=pairs,
            ),
            name="attend",
        )(*holders, *query_arrays)

    mixed = dict(zip([0, 1] + far[:-1], attend([near_q] + far_q[:-1], [(0, 0), (0, 1), (1, None)])))
    last_q = hold([far_q[-1]], [mixed[0]])
    mixed[far[-1]] = attend(last_q, [(0, None)])[0]
    back = {s: to_block(mixed[s], s) for s in far + [1]}
    early = far[:-1]
    back.update(zip(early, hold([back[s] for s in early], effort=EFFORT)))
    back[0] = mixed[0]
    order = [0] + far + [1]
    back = [back[s] for s in order]
    return pl.pallas_call(
        functools.partial(unpack_kernel, order, part),
        out_shape=jax.ShapeDtypeStruct((1, tokens, width), kind),
        in_specs=[VMEM] * blocks,
        out_specs=HBM,
        scratch_shapes=[pltpu.SemaphoreType.DMA((blocks,))],
        compiler_params=SMALL,
        cost_estimate=pl.CostEstimate(
            flops=0, bytes_accessed=2 * tokens * width * 2, transcendentals=0
        ),
        name="unpack",
    )(*back)


def local(query_rows, key_rows, value_rows):
    blocks = lax.axis_size("blk")
    heads = query_rows.shape[2] // HD
    few = blocks == 4 and heads % blocks == 0
    plan = local_blocks if few else local_generic
    return plan(query_rows, key_rows, value_rows)


def solution(mesh):
    in_specs = (
        P("cfg", ("groups", "blk", "uly"), None),
        P("cfg", ("groups", "blk", "uly"), None),
        P("cfg", ("groups", "blk", "uly"), None),
    )
    out_specs = P("cfg", ("groups", "blk", "uly"), None)
    return jax.shard_map(local, mesh=mesh, in_specs=in_specs, out_specs=out_specs, check_vma=False)
```
